32 devices in a mesh: blk: 8 (over z, x), rep: 4 (over y, core).
Axes of the slice: x: 2, y: 2, z: 4, core: 2. Of those that a mesh axis runs over, the one named last changes fastest.
Arguments:
- signals: bfloat16 [8192, 2048], P('rep', 'blk'), may hold values from -6 to 6
- omega: float32 [8, 5, 256, 256], P('blk', None, 'rep'), may hold values from -1.2 to 3, as said below
- pattern: int32 [8, 5], P('blk'), may hold values from 0 to 7, as said below
Outputs:
- omega_next: float32 [8, 5, 256, 256], P('blk', None, 'rep')
The draws below stay inside these ranges and needn't reach their ends.
Inputs may be any that keep to these rules, and one draw needn't show every extreme that they name: pattern[i, 0] = i. For two distinct whole numbers A and B from 1 to 3, the same in every row, pattern[i, 1] to pattern[i, 4] are i + A, i - A, i + B and i - B modulo 8 in some order, the same order in every row. Omega is symmetric: omega[i, k] is the transpose of omega[pattern[i, k], k2] where pattern[pattern[i, k], k2] = i. The diagonal entries of omega[i, 0] lie between 1 and 3.
All inputs are finite; a program needn't handle non-finite values.
Results may differ from the reference program's by a relative error of at most 0.0033.
Values may be sent and summed in bfloat16 or wider, within the bound.
No kernel may reach another device: no remote copies, remote signals or barrier semaphores. Data moves between devices by JAX's collectives and lax.ppermute only.
A program may use at most 128 MiB of HBM per device.

```python
import jax
import jax.numpy as jnp
from jax import lax

TILE = 256
K = 5
NB = 8
VOXELS = 2048
TIME = 8192


def pattern_offsets(key):
    inner = jax.random.fold_in(key, 11)
    first_key, second_key, order_key = jax.random.split(inner, 3)
    half = NB // 2
    first = jax.random.randint(first_key, (), 1, half).astype(jnp.int32)
    step_draw = jax.random.randint(second_key, (), 1, half - 1).astype(jnp.int32)
    second = (1 + jnp.mod(first - 1 + step_draw, half - 1)).astype(jnp.int32)
    canon = jnp.stack([jnp.zeros((), jnp.int32), first, NB - first, second, NB - second]).astype(jnp.int32)
    slot_perm = jax.random.permutation(order_key, 4).astype(jnp.int32)
    full_perm = jnp.concatenate([jnp.zeros((1,), jnp.int32), slot_perm + 1]).astype(jnp.int32)
    return (canon, full_perm)


def draw_pattern(key, part):
    canon, full_perm = pattern_offsets(key)
    offsets = canon[full_perm]
    row_ids = jnp.arange(NB, dtype=jnp.int32)
    return jnp.mod(row_ids[:, None] + offsets[None, :], NB).astype(jnp.int32)


def draw_omega(key, part):
    canon, full_perm = pattern_offsets(key)
    raw_key, diag_key = jax.random.split(jax.random.fold_in(key, 23), 2)
    raw_tiles = jax.random.uniform(raw_key, (NB, 3, TILE, TILE), jnp.float32, -0.45, 0.45)
    row_ids = jnp.arange(NB, dtype=jnp.int32)
    identity = jnp.eye(TILE, dtype=jnp.float32)
    diag_values = jax.random.uniform(diag_key, (NB, TILE), jnp.float32, 1.0, 3.0)
    base = raw_tiles[:, 0]
    diagonal_tile = 0.5 * (base + jnp.swapaxes(base, 1, 2))
    diagonal_tile = diagonal_tile * (1.0 - identity) + identity * diag_values[:, :, None]
    pieces = [diagonal_tile]
    for pair_index in range(2):
        offset = canon[1 + 2 * pair_index]
        lower_ids = jnp.mod(row_ids + NB - offset, NB)
        pair_raw = raw_tiles[:, 1 + pair_index]
        upper_tile = pair_raw
        lower_tile = jnp.swapaxes(pair_raw[lower_ids], 1, 2)
        pieces.append(upper_tile)
        pieces.append(lower_tile)
    stacked = jnp.stack(pieces, axis=1)
    return stacked[:, full_perm]


def block_scale(key, shape, shards, low, high):
    level, own = 1.0, jax.random.fold_in(key, 6)
    for position, shards_of in shards:
        steps = jnp.exp(jax.random.uniform(jax.random.fold_in(own, position), (shards_of,), jnp.float32, low / len(shards), high / len(shards)))
        level = level * jnp.repeat(steps, shape[position] // shards_of).reshape([-1 if axis == position else 1 for axis in range(len(shape))])
    return level


def noise(key, extent, spread, reach, cuts=(), kind=jnp.bfloat16):
    drawn = jax.random.normal(key, extent, jnp.float32) * spread
    if len(cuts) > 0:
        drawn = block_scale(key, extent, cuts, -0.22, 0.18) * drawn
    return jnp.clip(drawn, min=-reach, max=reach).astype(kind)


def setup_inputs(seed: int = 0) -> dict:
    key_of = jax.random.split(jax.random.key(seed), 4)
    return {
        "signals": noise(key_of[0], (TIME, VOXELS), 1.0, 6.0, ((0, 4), (1, 8))),
        "omega": draw_omega(jax.random.fold_in(key_of[3], 71), 0),
        "pattern": draw_pattern(jax.random.fold_in(key_of[3], 71), 0),
    }


def reference(signals, omega, pattern):
    time_length = signals.shape[0]
    blocks = signals.reshape(time_length, NB, TILE).transpose(1, 0, 2)
    weights = omega.astype(jnp.bfloat16)

    def make_mixed(block_row):
        total = jnp.zeros((time_length, TILE), jnp.float32)
        for slot_index in range(K):
            partner = blocks[pattern[block_row, slot_index]]
            total = total + jnp.dot(partner, weights[block_row, slot_index].T, preferred_element_type=jnp.float32)
        return total.astype(jnp.bfloat16)

    rows_all = jnp.arange(NB, dtype=jnp.int32)
    mixed = lax.map(make_mixed, rows_all)

    def make_left(block_row):
        return jnp.stack([jnp.dot(mixed[block_row].T, blocks[pattern[block_row, slot_index]], preferred_element_type=jnp.float32) for slot_index in range(K)])

    left_terms = lax.map(make_left, rows_all)
    identity = jnp.eye(TILE, dtype=jnp.float32)

    def make_update(block_row):
        results = []
        for slot_index in range(K):
            column = pattern[block_row, slot_index]
            mirror = jnp.argmax(pattern[column] == block_row).astype(jnp.int32)
            gradient = (left_terms[block_row, slot_index] + left_terms[column, mirror].T) / (2.0 * time_length)
            current = omega[block_row, slot_index]
            if slot_index == 0:
                diag_values = jnp.sum(current * identity, axis=1)
                gradient = gradient - identity * (1.0 / diag_values)[:, None]
            value = current - 0.5 * gradient
            shrunk = jnp.sign(value) * jnp.maximum(jnp.abs(value) - 0.05, 0.0)
            if slot_index == 0:
                shrunk = jnp.where(identity > 0.5, value, shrunk)
            results.append(shrunk)
        return jnp.stack(results)

    return lax.map(make_update, rows_all)
```

```python
import functools

import jax
import jax.numpy as jnp
from jax import lax
from jax.experimental import pallas as pl
from jax.experimental.pallas import tpu as pltpu
from jax.sharding import PartitionSpec as P

STEP_SIZE = 0.5
PENALTY = 0.1
LOW = 2
VMEM_LIMIT = 56 * 2**20
F32 = jnp.float32
BF16 = jnp.bfloat16

VMEM = pl.BlockSpec(memory_space=pltpu.VMEM)
SMEM = pl.BlockSpec(memory_space=pltpu.SMEM)
PARAMS = pltpu.CompilerParams(vmem_limit_bytes=VMEM_LIMIT)


def stored_offsets(pattern_ref, team, teams):
    drawn = [lax.rem(pattern_ref[0, k] - team + teams, teams) for k in range(1, 5)]
    a = functools.reduce(jnp.minimum, drawn)
    b = functools.reduce(jnp.minimum, [jnp.where(d == a, teams, d) for d in drawn])
    offsets = [jnp.int32(0), a, b, teams - b, teams - a]
    slots = [jnp.int32(0)]
    for offset in offsets[1:]:
        slots.append(sum(jnp.where(d == offset, k + 1, 0) for k, d in enumerate(drawn)))
    return offsets, slots


def weights_kernel(teams, place_ref, pattern_ref, omega_ref, out_ref):
    _, slots = stored_offsets(pattern_ref, place_ref[0], teams)
    for k in range(3):
        out_ref[k] = omega_ref[0, slots[k]].astype(BF16)


def product_kernel(teams, replicas, tile_rows, place_ref, pattern_ref, own_ref, other_ref, omega_ref, *rest):
    chips = replicas // 2
    outs = rest[: LOW * chips]
    mixed_ref, flip_ref, left_ref = rest[LOW * chips :]
    team, replica = place_ref[0], place_ref[1]
    core, chip = lax.rem(replica, 2), lax.div(replica, 2)
    offsets, _ = stored_offsets(pattern_ref, team, teams)
    times, width = own_ref.shape[1], own_ref.shape[2]

    def block(c):
        return jnp.concatenate([own_ref[c], other_ref[c]], axis=0)

    def tile(i, k):
        return omega_ref[i, :, k].reshape(width, width)

    nn = (((1,), (0,)), ((), ()))
    nt = (((1,), (1,)), ((), ()))

    def mix(i, carry):
        total = None
        for k, offset in enumerate(offsets):
            c = lax.rem(i + offset, teams)
            if k < 3:
                term = lax.dot_general(block(c), tile(i, k), nt, preferred_element_type=F32)
            else:
                term = lax.dot_general(block(c), tile(c, 5 - k), nn, preferred_element_type=F32)
            total = term if total is None else total + term
        mixed = total.astype(BF16)
        mixed_ref[i] = mixed
        flip_ref[:, : 2 * times] = mixed.T
        flip_ref[:, 2 * times :] = block(i).T
        for m in range(chips):
            row = (2 * (chip ^ m) + core) * tile_rows
            left_ref[i, m * tile_rows : (m + 1) * tile_rows] = flip_ref[
                pl.ds(pl.multiple_of(row, tile_rows), tile_rows)
            ]
        return carry

    unroll = teams <= 8
    lax.fori_loop(0, teams, mix, 0, unroll=unroll)
    for mx in range(LOW):

        def outer(z, carry):
            i = z * LOW + (lax.rem(team, LOW) ^ mx)
            for k, offset in enumerate(offsets):
                c = lax.rem(i + offset, teams)
                right = jnp.concatenate([own_ref[c], other_ref[c], mixed_ref[c]], axis=0)
                part = lax.dot_general(left_ref[i], right, nn, preferred_element_type=F32).astype(BF16)
                for m in range(chips):
                    outs[mx * chips + m][z, k] = part[m * tile_rows : (m + 1) * tile_rows]
            return carry

        lax.fori_loop(0, teams // LOW, outer, 0, unroll=unroll)


def add_kernel(teams, place_ref, *rest):
    count = teams // LOW
    parts, outs = rest[:-count], rest[-count:]
    z = lax.div(place_ref[0], LOW)
    for m in range(count):
        total = parts[0][z ^ m].astype(F32)
        for part in parts[1:]:
            total = total + part[z ^ m].astype(F32)
        outs[m][...] = total.astype(outs[m].dtype)


def update_kernel(teams, scale, place_ref, pattern_ref, omega_ref, *rest):
    parts, out_ref = rest[:-1], rest[-1]
    _, slots = stored_offsets(pattern_ref, place_ref[0], teams)
    rows, width = out_ref.shape[2:]
    first = place_ref[1] * rows
    row_ids = first + lax.broadcasted_iota(jnp.int32, (rows, width), 0)
    diagonal = row_ids == lax.broadcasted_iota(jnp.int32, (rows, width), 1)
    for k in range(5):
        total = parts[0][k].astype(F32)
        for part in parts[1:]:
            total = total + part[k].astype(F32)
        current = omega_ref[0, slots[k]]
        gradient = total * scale
        if k == 0:
            gradient = gradient - jnp.where(diagonal, 1.0 / current, 0.0)
        value = current - STEP_SIZE * gradient
        bound = STEP_SIZE * PENALTY
        shrunk = jnp.where(value > bound, value - bound, jnp.where(value < -bound, value + bound, 0.0))
        if k == 0:
            shrunk = jnp.where(diagonal, value, shrunk)
        out_ref[0, slots[k]] = shrunk


def per_device(teams, replicas, signals, omega, pattern):
    chips = replicas // 2
    slots, tile_rows, width = omega.shape[1:]
    times = signals.shape[0] // teams
    place = jnp.stack([lax.axis_index("blk"), lax.axis_index("rep")]).astype(jnp.int32)

    def swap(array, blk_mask, rep_mask):
        route = [
            (b * replicas + r, (b ^ blk_mask) * replicas + (r ^ rep_mask))
            for b in range(teams)
            for r in range(replicas)
        ]
        return lax.ppermute(array, ("blk", "rep"), route)

    upper = pl.pallas_call(
        functools.partial(weights_kernel, teams),
        out_shape=jax.ShapeDtypeStruct((3, tile_rows, width), BF16),
        in_specs=[SMEM, SMEM, VMEM],
        out_specs=VMEM,
        compiler_params=PARAMS,
        name="weights",
    )(place, pattern, omega)
    weights = lax.all_gather(upper, ("blk", "rep")).reshape(teams, replicas, 3, tile_rows, width)

    own = lax.all_to_all(signals.reshape(teams, times, width), "blk", 0, 0)
    other = swap(own, 0, 1)

    planes = LOW * chips
    count = teams // LOW
    partial = pl.pallas_call(
        functools.partial(product_kernel, teams, replicas, tile_rows),
        out_shape=[jax.ShapeDtypeStruct((count, slots, tile_rows, width), BF16)] * planes,
        in_specs=[SMEM, SMEM, VMEM, VMEM, VMEM],
        out_specs=[VMEM] * planes,
        scratch_shapes=[
            pltpu.VMEM((teams, 2 * times, width), BF16),
            pltpu.VMEM((width, 4 * times), BF16),
            pltpu.VMEM((teams, chips * tile_rows, 4 * times), BF16),
        ],
        compiler_params=PARAMS,
        name="products",
    )(place, pattern, own, other, weights)
    received = [
        swap(partial[mx * chips + my], mx, 2 * my) if mx + my else partial[0]
        for mx in range(LOW)
        for my in range(chips)
    ]

    summed = pl.pallas_call(
        functools.partial(add_kernel, teams),
        out_shape=[
            jax.ShapeDtypeStruct((slots, tile_rows, width), BF16 if m else F32) for m in range(count)
        ],
        in_specs=[SMEM] + [VMEM] * planes,
        out_specs=[VMEM] * count,
        compiler_params=PARAMS,
        name="plane_sum",
    )(place, *received)
    arrived = [swap(summed[m], m * LOW, 0) if m else summed[0] for m in range(count)]

    scale = 1.0 / (2.0 * signals.shape[0] * replicas)
    return pl.pallas_call(
        functools.partial(update_kernel, teams, scale),
        out_shape=jax.ShapeDtypeStruct(omega.shape, F32),
        in_specs=[SMEM, SMEM, VMEM] + [VMEM] * count,
        out_specs=VMEM,
        compiler_params=PARAMS,
        name="update",
    )(place, pattern, omega, *arrived)


def solution(mesh):
    return jax.shard_map(
        functools.partial(per_device, mesh.shape["blk"], mesh.shape["rep"]),
        mesh=mesh,
        in_specs=(P("rep", "blk"), P("blk", None, "rep", None), P("blk", None)),
        out_specs=P("blk", None, "rep", None),
        check_vma=False,
    )
```

```python
import functools

import jax
import jax.numpy as jnp
from jax import lax
from jax.experimental import pallas as pl
from jax.experimental.pallas import tpu as pltpu
from jax.sharding import PartitionSpec as P

STEP_SIZE = 0.5
PENALTY = 0.1
LOW = 2
VMEM_LIMIT = 56 * 2**20
F32 = jnp.float32
BF16 = jnp.bfloat16

VMEM = pl.BlockSpec(memory_space=pltpu.VMEM)
ANY = pl.BlockSpec(memory_space=pl.ANY)
SMEM = pl.BlockSpec(memory_space=pltpu.SMEM)
PARAMS = pltpu.CompilerParams(vmem_limit_bytes=VMEM_LIMIT)


def stored_offsets(pattern_ref, team, teams):
    drawn = [lax.rem(pattern_ref[0, k] - team + teams, teams) for k in range(1, 5)]
    a = functools.reduce(jnp.minimum, drawn)
    b = functools.reduce(jnp.minimum, [jnp.where(d == a, teams, d) for d in drawn])
    offsets = [jnp.int32(0), a, b, teams - b, teams - a]
    slots = [jnp.int32(0)]
    for offset in offsets[1:]:
        slots.append(sum(jnp.where(d == offset, k + 1, 0) for k, d in enumerate(drawn)))
    return offsets, slots


def prepare_kernel(teams, place_ref, pattern_ref, omega_ref, signals_ref, out_ref, *rest):
    chunks, sems = rest[:-1], rest[-1]
    team = place_ref[0]
    times = chunks[0].shape[0]
    copies = []
    for m, chunk in enumerate(chunks, 1):
        first = pl.multiple_of((team ^ m) * times, times)
        copies.append(pltpu.make_async_copy(signals_ref.at[pl.ds(first, times)], chunk, sems.at[m - 1]))
    for copy in copies:
        copy.start()
    _, slots = stored_offsets(pattern_ref, team, teams)
    for k in range(3):
        out_ref[k] = omega_ref[0, slots[k]].astype(BF16)
    for copy in copies:
        copy.wait()


def product_kernel(teams, replicas, tile_rows, place_ref, pattern_ref, signals_ref, *rest):
    chips = replicas // 2
    planes = LOW * chips
    depth = teams // LOW
    own_refs, rest = rest[: teams - 1], rest[teams - 1 :]
    other_refs, rest = rest[:teams], rest[teams:]
    weight_refs, rest = rest[: 2 * planes], rest[2 * planes :]
    outs, rest = rest[:planes], rest[planes:]
    data_ref, omega_ref, mixed_ref, flip_ref, left_ref, data_sems, omega_sems = rest
    team, replica = place_ref[0], place_ref[1]
    core, chip = lax.rem(replica, 2), lax.div(replica, 2)
    high, low = lax.div(team, LOW), lax.rem(team, LOW)
    offsets, _ = stored_offsets(pattern_ref, team, teams)
    times, width = data_ref.shape[1] // 2, data_ref.shape[2]

    copies = []
    for half in range(2):
        for m in range(teams):
            if half:
                source = other_refs[m]
            elif m:
                source = own_refs[m - 1]
            else:
                source = signals_ref.at[pl.ds(pl.multiple_of(team * times, times), times)]
            target = data_ref.at[team ^ m, pl.ds(half * times, times)]
            copies.append(pltpu.make_async_copy(source, target, data_sems.at[half * teams + m]))
    for half in range(2):
        for mx in range(LOW):
            for my in range(chips):
                plane = mx * chips + my
                row = (2 * (chip ^ my) + (core ^ half)) * tile_rows
                for mz in range(depth):
                    i = (high ^ mz) * LOW + (low ^ mx)
                    target = omega_ref.at[i, :, pl.ds(pl.multiple_of(row, tile_rows), tile_rows)]
                    copies.append(
                        pltpu.make_async_copy(
                            weight_refs[half * planes + plane].at[mz],
                            target,
                            omega_sems.at[(half * planes + plane) * depth + mz],
                        )
                    )
    for copy in copies:
        copy.start()
    for copy in copies:
        copy.wait()

    nn = (((1,), (0,)), ((), ()))
    nt = (((1,), (1,)), ((), ()))

    def mix(i, carry):
        total = None
        for k, offset in enumerate(offsets):
            c = lax.rem(i + offset, teams)
            if k < 3:
                term = lax.dot_general(data_ref[c], omega_ref[i, k], nt, preferred_element_type=F32)
            else:
                term = lax.dot_general(data_ref[c], omega_ref[c, 5 - k], nn, preferred_element_type=F32)
            total = term if total is None else total + term
        mixed = total.astype(BF16)
        mixed_ref[i] = mixed
        flip_ref[:, : 2 * times] = mixed.T
        flip_ref[:, 2 * times :] = data_ref[i].T
        for m in range(chips):
            row = (2 * (chip ^ m) + core) * tile_rows
            left_ref[i, m * tile_rows : (m + 1) * tile_rows] = flip_ref[
                pl.ds(pl.multiple_of(row, tile_rows), tile_rows)
            ]
        return carry

    unroll = teams <= 8
    lax.fori_loop(0, teams, mix, 0, unroll=unroll)
    for mx in range(LOW):

        def outer(z, carry):
            i = z * LOW + (low ^ mx)
            for k, offset in enumerate(offsets):
                c = lax.rem(i + offset, teams)
                right = jnp.concatenate([data_ref[c], mixed_ref[c]], axis=0)
                part = lax.dot_general(left_ref[i], right, nn, preferred_element_type=F32).astype(BF16)
                for m in range(chips):
                    outs[mx * chips + m][z, k] = part[m * tile_rows : (m + 1) * tile_rows]
            return carry

        lax.fori_loop(0, depth, outer, 0, unroll=unroll)


def add_kernel(teams, place_ref, *rest):
    count = teams // LOW
    parts, outs = rest[:-count], rest[-count:]
    z = lax.div(place_ref[0], LOW)
    for m in range(count):
        total = parts[0][z ^ m].astype(F32)
        for part in parts[1:]:
            total = total + part[z ^ m].astype(F32)
        outs[m][...] = total.astype(outs[m].dtype)


def update_kernel(teams, scale, place_ref, pattern_ref, omega_ref, *rest):
    parts, out_ref = rest[:-1], rest[-1]
    _, slots = stored_offsets(pattern_ref, place_ref[0], teams)
    rows, width = out_ref.shape[2:]
    first = place_ref[1] * rows
    row_ids = first + lax.broadcasted_iota(jnp.int32, (rows, width), 0)
    diagonal = row_ids == lax.broadcasted_iota(jnp.int32, (rows, width), 1)
    for k in range(5):
        total = parts[0][k].astype(F32)
        for part in parts[1:]:
            total = total + part[k].astype(F32)
        current = omega_ref[0, slots[k]]
        gradient = total * scale
        if k == 0:
            gradient = gradient - jnp.where(diagonal, 1.0 / current, 0.0)
        value = current - STEP_SIZE * gradient
        bound = STEP_SIZE * PENALTY
        shrunk = jnp.where(value > bound, value - bound, jnp.where(value < -bound, value + bound, 0.0))
        if k == 0:
            shrunk = jnp.where(diagonal, value, shrunk)
        out_ref[0, slots[k]] = shrunk


def per_device(teams, replicas, signals, omega, pattern):
    chips = replicas // 2
    slots, tile_rows, width = omega.shape[1:]
    times = signals.shape[0] // teams
    place = jnp.stack([lax.axis_index("blk"), lax.axis_index("rep")]).astype(jnp.int32)

    def swap(array, blk_mask, rep_mask):
        route = [
            (b * replicas + r, (b ^ blk_mask) * replicas + (r ^ rep_mask))
            for b in range(teams)
            for r in range(replicas)
        ]
        return lax.ppermute(array, ("blk", "rep"), route)

    planes = LOW * chips
    count = teams // LOW
    upper, *chunks = pl.pallas_call(
        functools.partial(prepare_kernel, teams),
        out_shape=[jax.ShapeDtypeStruct((3, tile_rows, width), BF16)]
        + [jax.ShapeDtypeStruct((times, width), BF16)] * (teams - 1),
        in_specs=[SMEM, SMEM, VMEM, ANY],
        out_specs=[VMEM] + [ANY] * (teams - 1),
        scratch_shapes=[pltpu.SemaphoreType.DMA((teams - 1,))],
        compiler_params=PARAMS,
        name="prepare",
    )(place, pattern, omega, signals)

    line = jnp.stack([upper] + [swap(upper, m * LOW, 0) for m in range(1, count)])
    own = [swap(chunk, m, 0) for m, chunk in enumerate(chunks, 1)]
    weights = [
        swap(line, mx, 2 * my) if mx + my else line for mx in range(LOW) for my in range(chips)
    ]
    weights += [swap(array, 0, 1) for array in weights]
    first = lax.dynamic_slice_in_dim(signals, place[0] * times, times, 0)
    other = [swap(array, 0, 1) for array in [first] + own]

    partial = pl.pallas_call(
        functools.partial(product_kernel, teams, replicas, tile_rows),
        out_shape=[jax.ShapeDtypeStruct((count, slots, tile_rows, width), BF16)] * planes,
        in_specs=[SMEM, SMEM] + [ANY] * (1 + 2 * teams - 1 + 2 * planes),
        out_specs=[VMEM] * planes,
        scratch_shapes=[
            pltpu.VMEM((teams, 2 * times, width), BF16),
            pltpu.VMEM((teams, 3, width, width), BF16),
            pltpu.VMEM((teams, 2 * times, width), BF16),
            pltpu.VMEM((width, 4 * times), BF16),
            pltpu.VMEM((teams, chips * tile_rows, 4 * times), BF16),
            pltpu.SemaphoreType.DMA((2 * teams,)),
            pltpu.SemaphoreType.DMA((2 * planes * count,)),
        ],
        compiler_params=PARAMS,
        name="products",
    )(place, pattern, signals, *own, *other, *weights)
    received = [
        swap(partial[mx * chips + my], mx, 2 * my) if mx + my else partial[0]
        for mx in range(LOW)
        for my in range(chips)
    ]

    summed = pl.pallas_call(
        functools.partial(add_kernel, teams),
        out_shape=[
            jax.ShapeDtypeStruct((slots, tile_rows, width), BF16 if m else F32) for m in range(count)
        ],
        in_specs=[SMEM] + [VMEM] * planes,
        out_specs=[VMEM] * count,
        compiler_params=PARAMS,
        name="plane_sum",
    )(place, *received)
    arrived = [swap(summed[m], m * LOW, 0) if m else summed[0] for m in range(count)]

    scale = 1.0 / (2.0 * signals.shape[0] * replicas)
    return pl.pallas_call(
        functools.partial(update_kernel, teams, scale),
        out_shape=jax.ShapeDtypeStruct(omega.shape, F32),
        in_specs=[SMEM, SMEM, VMEM] + [VMEM] * count,
        out_specs=VMEM,
        compiler_params=PARAMS,
        name="update",
    )(place, pattern, omega, *arrived)


def solution(mesh):
    return jax.shard_map(
        functools.partial(per_device, mesh.shape["blk"], mesh.shape["rep"]),
        mesh=mesh,
        in_specs=(P("rep", "blk"), P("blk", None, "rep", None), P("blk", None)),
        out_specs=P("blk", None, "rep", None),
        check_vma=False,
    )
```

```python
import functools

import jax
import jax.numpy as jnp
from jax import lax
from jax.experimental import pallas as pl
from jax.experimental.pallas import tpu as pltpu
from jax.sharding import PartitionSpec as P

STEP_SIZE = 0.5
PENALTY = 0.1
LOW = 2
F32 = jnp.float32
BF16 = jnp.bfloat16

VMEM = pl.BlockSpec(memory_space=pltpu.VMEM)
ANY = pl.BlockSpec(memory_space=pl.ANY)
SMEM = pl.BlockSpec(memory_space=pltpu.SMEM)
SMALL = pltpu.CompilerParams(vmem_limit_bytes=8 * 2**20)


def stored_offsets(pattern_ref, team, teams):
    drawn = [lax.rem(pattern_ref[0, k] - team + teams, teams) for k in range(1, 5)]
    a = functools.reduce(jnp.minimum, drawn)
    b = functools.reduce(jnp.minimum, [jnp.where(d == a, teams, d) for d in drawn])
    offsets = [jnp.int32(0), a, b, teams - b, teams - a]
    slots = [jnp.int32(0)]
    for offset in offsets[1:]:
        slots.append(sum(jnp.where(d == offset, k + 1, 0) for k, d in enumerate(drawn)))
    return offsets, slots


def prepare_kernel(teams, place_ref, pattern_ref, omega_ref, out_ref):
    _, slots = stored_offsets(pattern_ref, place_ref[0], teams)
    for k in range(3):
        out_ref[k] = omega_ref[0, slots[k]].astype(BF16)


def product_kernel(teams, replicas, tile_rows, place_ref, pattern_ref, own_ref, other_ref, *rest):
    chips = replicas // 2
    planes = LOW * chips
    depth = teams // LOW
    weight_refs, rest = rest[: 2 * planes], rest[2 * planes :]
    outs, rest = rest[:planes], rest[planes:]
    data_ref, omega_ref, mixed_ref, flip_ref, left_ref, data_sems, omega_sems = rest
    team, replica = place_ref[0], place_ref[1]
    core, chip = lax.rem(replica, 2), lax.div(replica, 2)
    high, low = lax.div(team, LOW), lax.rem(team, LOW)
    offsets, _ = stored_offsets(pattern_ref, team, teams)
    times, width = data_ref.shape[1] // 2, data_ref.shape[2]

    copies = [
        pltpu.make_async_copy(source, data_ref.at[:, pl.ds(half * times, times)], data_sems.at[half])
        for half, source in enumerate([own_ref, other_ref])
    ]
    for half in range(2):
        for mx in range(LOW):
            for my in range(chips):
                plane = mx * chips + my
                row = (2 * (chip ^ my) + (core ^ half)) * tile_rows
                for mz in range(depth):
                    i = (high ^ mz) * LOW + (low ^ mx)
                    target = omega_ref.at[i, :, pl.ds(pl.multiple_of(row, tile_rows), tile_rows)]
                    copies.append(
                        pltpu.make_async_copy(
                            weight_refs[half * planes + plane].at[mz],
                            target,
                            omega_sems.at[(half * planes + plane) * depth + mz],
                        )
                    )
    for copy in copies:
        copy.start()
    for copy in copies:
        copy.wait()

    nn = (((1,), (0,)), ((), ()))
    nt = (((1,), (1,)), ((), ()))

    def mix(i, carry):
        total = None
        for k, offset in enumerate(offsets):
            c = lax.rem(i + offset, teams)
            if k < 3:
                term = lax.dot_general(data_ref[c], omega_ref[i, k], nt, preferred_element_type=F32)
            else:
                term = lax.dot_general(data_ref[c], omega_ref[c, 5 - k], nn, preferred_element_type=F32)
            total = term if total is None else total + term
        mixed = total.astype(BF16)
        mixed_ref[i] = mixed
        flip_ref[:, : 2 * times] = mixed.T
        flip_ref[:, 2 * times :] = data_ref[i].T
        for m in range(chips):
            row = (2 * (chip ^ m) + core) * tile_rows
            left_ref[i, m * tile_rows : (m + 1) * tile_rows] = flip_ref[
                pl.ds(pl.multiple_of(row, tile_rows), tile_rows)
            ]
        return carry

    unroll = teams <= 8
    lax.fori_loop(0, teams, mix, 0, unroll=unroll)
    for mx in range(LOW):

        def outer(z, carry):
            i = z * LOW + (low ^ mx)
            for k, offset in enumerate(offsets):
                c = lax.rem(i + offset, teams)
                right = jnp.concatenate([data_ref[c], mixed_ref[c]], axis=0)
                part = lax.dot_general(left_ref[i], right, nn, preferred_element_type=F32).astype(BF16)
                for m in range(chips):
                    outs[mx * chips + m][z, k] = part[m * tile_rows : (m + 1) * tile_rows]
            return carry

        lax.fori_loop(0, depth, outer, 0, unroll=unroll)


def add_kernel(teams, place_ref, *rest):
    count = teams // LOW
    parts, outs = rest[:-count], rest[-count:]
    z = lax.div(place_ref[0], LOW)
    for m in range(count):
        total = parts[0][z ^ m].astype(F32)
        for part in parts[1:]:
            total = total + part[z ^ m].astype(F32)
        outs[m][...] = total.astype(outs[m].dtype)


def update_kernel(teams, scale, place_ref, pattern_ref, omega_ref, *rest):
    parts, out_ref = rest[:-1], rest[-1]
    _, slots = stored_offsets(pattern_ref, place_ref[0], teams)
    rows, width = out_ref.shape[2:]
    first = place_ref[1] * rows
    row_ids = first + lax.broadcasted_iota(jnp.int32, (rows, width), 0)
    diagonal = row_ids == lax.broadcasted_iota(jnp.int32, (rows, width), 1)
    for k in range(5):
        total = parts[0][k].astype(F32)
        for part in parts[1:]:
            total = total + part[k].astype(F32)
        current = omega_ref[0, slots[k]]
        gradient = total * scale
        if k == 0:
            gradient = gradient - jnp.where(diagonal, 1.0 / current, 0.0)
        value = current - STEP_SIZE * gradient
        bound = STEP_SIZE * PENALTY
        shrunk = jnp.where(value > bound, value - bound, jnp.where(value < -bound, value + bound, 0.0))
        if k == 0:
            shrunk = jnp.where(diagonal, value, shrunk)
        out_ref[0, slots[k]] = shrunk


def per_device(teams, replicas, signals, omega, pattern):
    chips = replicas // 2
    slots, tile_rows, width = omega.shape[1:]
    times = signals.shape[0] // teams
    place = jnp.stack([lax.axis_index("blk"), lax.axis_index("rep")]).astype(jnp.int32)

    def swap(array, blk_mask, rep_mask):
        route = [
            (b * replicas + r, (b ^ blk_mask) * replicas + (r ^ rep_mask))
            for b in range(teams)
            for r in range(replicas)
        ]
        return lax.ppermute(array, ("blk", "rep"), route)

    planes = LOW * chips
    count = teams // LOW
    upper = pl.pallas_call(
        functools.partial(prepare_kernel, teams),
        out_shape=jax.ShapeDtypeStruct((3, tile_rows, width), BF16),
        in_specs=[SMEM, SMEM, VMEM],
        out_specs=VMEM,
        compiler_params=SMALL,
        name="prepare",
    )(place, pattern, omega)

    line = jnp.stack([upper] + [swap(upper, m * LOW, 0) for m in range(1, count)])
    line, signals = lax.optimization_barrier((line, signals))
    weights = [
        swap(line, mx, 2 * my) if mx + my else line for mx in range(LOW) for my in range(chips)
    ]
    own = lax.all_to_all(signals.reshape(teams, times, width), "blk", 0, 0)
    other = swap(own, 0, 1)
    weights += [swap(array, 0, 1) for array in weights]

    partial = pl.pallas_call(
        functools.partial(product_kernel, teams, replicas, tile_rows),
        out_shape=[jax.ShapeDtypeStruct((count, slots, tile_rows, width), BF16)] * planes,
        in_specs=[SMEM, SMEM] + [ANY] * (2 + 2 * planes),
        out_specs=[VMEM] * planes,
        scratch_shapes=[
            pltpu.VMEM((teams, 2 * times, width), BF16),
            pltpu.VMEM((teams, 3, width, width), BF16),
            pltpu.VMEM((teams, 2 * times, width), BF16),
            pltpu.VMEM((width, 4 * times), BF16),
            pltpu.VMEM((teams, chips * tile_rows, 4 * times), BF16),
            pltpu.SemaphoreType.DMA((2,)),
            pltpu.SemaphoreType.DMA((2 * planes * count,)),
        ],
        compiler_params=pltpu.CompilerParams(vmem_limit_bytes=(16 if teams <= 8 else 48) * 2**20),
        name="products",
    )(place, pattern, own, other, *weights)
    received = [
        swap(partial[mx * chips + my], mx, 2 * my) if mx + my else partial[0]
        for mx in range(LOW)
        for my in range(chips)
    ]

    summed = pl.pallas_call(
        functools.partial(add_kernel, teams),
        out_shape=[
            jax.ShapeDtypeStruct((slots, tile_rows, width), BF16 if m else F32) for m in range(count)
        ],
        in_specs=[SMEM] + [VMEM] * planes,
        out_specs=[VMEM] * count,
        compiler_params=pltpu.CompilerParams(vmem_limit_bytes=(8 if teams <= 8 else 48) * 2**20),
        name="plane_sum",
    )(place, *received)
    arrived = [swap(summed[m], m * LOW, 0) if m else summed[0] for m in range(count)]

    scale = 1.0 / (2.0 * signals.shape[0] * replicas)
    return pl.pallas_call(
        functools.partial(update_kernel, teams, scale),
        out_shape=jax.ShapeDtypeStruct(omega.shape, F32),
        in_specs=[SMEM, SMEM, VMEM] + [VMEM] * count,
        out_specs=VMEM,
        compiler_params=pltpu.CompilerParams(vmem_limit_bytes=(8 if teams <= 8 else 48) * 2**20),
        name="update",
    )(place, pattern, omega, *arrived)


def solution(mesh):
    return jax.shard_map(
        functools.partial(per_device, mesh.shape["blk"], mesh.shape["rep"]),
        mesh=mesh,
        in_specs=(P("rep", "blk"), P("blk", None, "rep", None), P("blk", None)),
        out_specs=P("blk", None, "rep", None),
        check_vma=False,
    )
```

```python
import functools

import jax
import jax.numpy as jnp
from jax import lax
from jax.experimental import pallas as pl
from jax.experimental.pallas import tpu as pltpu
from jax.sharding import PartitionSpec as P

STEP_SIZE = 0.5
PENALTY = 0.1
LOW = 2
F32 = jnp.float32
BF16 = jnp.bfloat16

VMEM = pl.BlockSpec(memory_space=pltpu.VMEM)
ANY = pl.BlockSpec(memory_space=pl.ANY)
SMEM = pl.BlockSpec(memory_space=pltpu.SMEM)
SMALL = pltpu.CompilerParams(vmem_limit_bytes=8 * 2**20)


def stored_offsets(pattern_ref, team, teams):
    drawn = [lax.rem(pattern_ref[0, k] - team + teams, teams) for k in range(1, 5)]
    a = functools.reduce(jnp.minimum, drawn)
    b = functools.reduce(jnp.minimum, [jnp.where(d == a, teams, d) for d in drawn])
    offsets = [jnp.int32(0), a, b, teams - b, teams - a]
    slots = [jnp.int32(0)]
    for offset in offsets[1:]:
        slots.append(sum(jnp.where(d == offset, k + 1, 0) for k, d in enumerate(drawn)))
    return offsets, slots


def prepare_kernel(teams, place_ref, pattern_ref, omega_ref, out_ref):
    _, slots = stored_offsets(pattern_ref, place_ref[0], teams)
    for k in range(3):
        out_ref[k] = omega_ref[0, slots[k]].astype(BF16)


def product_kernel(teams, replicas, tile_rows, place_ref, pattern_ref, own_ref, low_ref, high_ref, *rest):
    chips = replicas // 2
    planes = LOW * chips
    depth = teams // LOW
    weight_refs, rest = rest[: 2 * planes], rest[2 * planes :]
    outs, rest = rest[:planes], rest[planes:]
    data_ref, omega_ref, mixed_ref, flip_ref, left_ref, data_sems, omega_sems = rest
    team, replica = place_ref[0], place_ref[1]
    core, chip = lax.rem(replica, 2), lax.div(replica, 2)
    high, low = lax.div(team, LOW), lax.rem(team, LOW)
    offsets, _ = stored_offsets(pattern_ref, team, teams)
    times, width = data_ref.shape[1] // 2, data_ref.shape[2]

    copies = []
    for n, (source, first, half) in enumerate([(own_ref, 0, 0), (low_ref, 0, 1), (high_ref, teams // 2, 1)]):
        target = data_ref.at[pl.ds(first, source.shape[0]), pl.ds(half * times, times)]
        copies.append(pltpu.make_async_copy(source, target, data_sems.at[n]))
    for half in range(2):
        for mx in range(LOW):
            for my in range(chips):
                plane = mx * chips + my
                row = (2 * (chip ^ my) + (core ^ half)) * tile_rows
                for mz in range(depth):
                    i = (high ^ mz) * LOW + (low ^ mx)
                    target = omega_ref.at[i, :, pl.ds(pl.multiple_of(row, tile_rows), tile_rows)]
                    copies.append(
                        pltpu.make_async_copy(
                            weight_refs[half * planes + plane].at[mz],
                            target,
                            omega_sems.at[(half * planes + plane) * depth + mz],
                        )
                    )
    for copy in copies:
        copy.start()
    for copy in copies:
        copy.wait()

    nn = (((1,), (0,)), ((), ()))
    nt = (((1,), (1,)), ((), ()))

    def mix(i, carry):
        total = None
        for k, offset in enumerate(offsets):
            c = lax.rem(i + offset, teams)
            if k < 3:
                term = lax.dot_general(data_ref[c], omega_ref[i, k], nt, preferred_element_type=F32)
            else:
                term = lax.dot_general(data_ref[c], omega_ref[c, 5 - k], nn, preferred_element_type=F32)
            total = term if total is None else total + term
        mixed = total.astype(BF16)
        mixed_ref[i] = mixed
        flip_ref[:, : 2 * times] = mixed.T
        flip_ref[:, 2 * times :] = data_ref[i].T
        for m in range(chips):
            row = (2 * (chip ^ m) + core) * tile_rows
            left_ref[i, m * tile_rows : (m + 1) * tile_rows] = flip_ref[
                pl.ds(pl.multiple_of(row, tile_rows), tile_rows)
            ]
        return carry

    unroll = teams <= 8
    lax.fori_loop(0, teams, mix, 0, unroll=unroll)
    for mx in range(LOW):

        def outer(z, carry):
            i = z * LOW + (low ^ mx)
            for k, offset in enumerate(offsets):
                c = lax.rem(i + offset, teams)
                right = jnp.concatenate([data_ref[c], mixed_ref[c]], axis=0)
                part = lax.dot_general(left_ref[i], right, nn, preferred_element_type=F32).astype(BF16)
                for m in range(chips):
                    outs[mx * chips + m][z, k] = part[m * tile_rows : (m + 1) * tile_rows]
            return carry

        lax.fori_loop(0, depth, outer, 0, unroll=unroll)


def add_kernel(teams, place_ref, *rest):
    count = teams // LOW
    parts, outs = rest[:-count], rest[-count:]
    z = lax.div(place_ref[0], LOW)
    for m in range(count):
        total = parts[0][z ^ m].astype(F32)
        for part in parts[1:]:
            total = total + part[z ^ m].astype(F32)
        outs[m][...] = total.astype(outs[m].dtype)


def update_kernel(teams, scale, place_ref, pattern_ref, omega_ref, *rest):
    parts, out_ref = rest[:-1], rest[-1]
    _, slots = stored_offsets(pattern_ref, place_ref[0], teams)
    rows, width = out_ref.shape[2:]
    first = place_ref[1] * rows
    row_ids = first + lax.broadcasted_iota(jnp.int32, (rows, width), 0)
    diagonal = row_ids == lax.broadcasted_iota(jnp.int32, (rows, width), 1)
    for k in range(5):
        total = parts[0][k].astype(F32)
        for part in parts[1:]:
            total = total + part[k].astype(F32)
        current = omega_ref[0, slots[k]]
        gradient = total * scale
        if k == 0:
            gradient = gradient - jnp.where(diagonal, 1.0 / current, 0.0)
        value = current - STEP_SIZE * gradient
        bound = STEP_SIZE * PENALTY
        shrunk = jnp.where(value > bound, value - bound, jnp.where(value < -bound, value + bound, 0.0))
        if k == 0:
            shrunk = jnp.where(diagonal, value, shrunk)
        out_ref[0, slots[k]] = shrunk


def per_device(teams, replicas, signals, omega, pattern):
    chips = replicas // 2
    slots, tile_rows, width = omega.shape[1:]
    times = signals.shape[0] // teams
    place = jnp.stack([lax.axis_index("blk"), lax.axis_index("rep")]).astype(jnp.int32)

    def swap(array, blk_mask, rep_mask):
        route = [
            (b * replicas + r, (b ^ blk_mask) * replicas + (r ^ rep_mask))
            for b in range(teams)
            for r in range(replicas)
        ]
        return lax.ppermute(array, ("blk", "rep"), route)

    planes = LOW * chips
    count = teams // LOW
    upper = pl.pallas_call(
        functools.partial(prepare_kernel, teams),
        out_shape=jax.ShapeDtypeStruct((3, tile_rows, width), BF16),
        in_specs=[SMEM, SMEM, VMEM],
        out_specs=VMEM,
        compiler_params=SMALL,
        name="prepare",
    )(place, pattern, omega)

    line = jnp.stack([upper] + [swap(upper, m * LOW, 0) for m in range(1, count)])
    line, signals = lax.optimization_barrier((line, signals))
    weights = [
        swap(line, mx, 2 * my) if mx + my else line for mx in range(LOW) for my in range(chips)
    ]
    own = lax.all_to_all(signals.reshape(teams, times, width), "blk", 0, 0)
    other = [swap(part, 0, 1) for part in jnp.split(own, 2)]
    weights += [swap(array, 0, 1) for array in weights]

    partial = pl.pallas_call(
        functools.partial(product_kernel, teams, replicas, tile_rows),
        out_shape=[jax.ShapeDtypeStruct((count, slots, tile_rows, width), BF16)] * planes,
        in_specs=[SMEM, SMEM] + [ANY] * (3 + 2 * planes),
        out_specs=[VMEM] * planes,
        scratch_shapes=[
            pltpu.VMEM((teams, 2 * times, width), BF16),
            pltpu.VMEM((teams, 3, width, width), BF16),
            pltpu.VMEM((teams, 2 * times, width), BF16),
            pltpu.VMEM((width, 4 * times), BF16),
            pltpu.VMEM((teams, chips * tile_rows, 4 * times), BF16),
            pltpu.SemaphoreType.DMA((3,)),
            pltpu.SemaphoreType.DMA((2 * planes * count,)),
        ],
        compiler_params=pltpu.CompilerParams(vmem_limit_bytes=(16 if teams <= 8 else 48) * 2**20),
        name="products",
    )(place, pattern, own, *other, *weights)
    received = [
        swap(partial[mx * chips + my], mx, 2 * my) if mx + my else partial[0]
        for mx in range(LOW)
        for my in range(chips)
    ]

    summed = pl.pallas_call(
        functools.partial(add_kernel, teams),
        out_shape=[
            jax.ShapeDtypeStruct((slots, tile_rows, width), BF16 if m else F32) for m in range(count)
        ],
        in_specs=[SMEM] + [VMEM] * planes,
        out_specs=[VMEM] * count,
        compiler_params=pltpu.CompilerParams(vmem_limit_bytes=(8 if teams <= 8 else 48) * 2**20),
        name="plane_sum",
    )(place, *received)
    arrived = [swap(summed[m], m * LOW, 0) if m else summed[0] for m in range(count)]

    scale = 1.0 / (2.0 * signals.shape[0] * replicas)
    return pl.pallas_call(
        functools.partial(update_kernel, teams, scale),
        out_shape=jax.ShapeDtypeStruct(omega.shape, F32),
        in_specs=[SMEM, SMEM, VMEM] + [VMEM] * count,
        out_specs=VMEM,
        compiler_params=pltpu.CompilerParams(vmem_limit_bytes=(8 if teams <= 8 else 48) * 2**20),
        name="update",
    )(place, pattern, omega, *arrived)


def solution(mesh):
    return jax.shard_map(
        functools.partial(per_device, mesh.shape["blk"], mesh.shape["rep"]),
        mesh=mesh,
        in_specs=(P("rep", "blk"), P("blk", None, "rep", None), P("blk", None)),
        out_specs=P("blk", None, "rep", None),
        check_vma=False,
    )
```

```python
import functools

import jax
import jax.numpy as jnp
from jax import lax
from jax.experimental import pallas as pl
from jax.experimental.pallas import tpu as pltpu
from jax.sharding import PartitionSpec as P

STEP_SIZE = 0.5
PENALTY = 0.1
LOW = 2
F32 = jnp.float32
BF16 = jnp.bfloat16

VMEM = pl.BlockSpec(memory_space=pltpu.VMEM)
ANY = pl.BlockSpec(memory_space=pl.ANY)
SMEM = pl.BlockSpec(memory_space=pltpu.SMEM)
SMALL = pltpu.CompilerParams(vmem_limit_bytes=8 * 2**20)


def stored_offsets(pattern_ref, team, teams):
    drawn = [lax.rem(pattern_ref[0, k] - team + teams, teams) for k in range(1, 5)]
    a = functools.reduce(jnp.minimum, drawn)
    b = functools.reduce(jnp.minimum, [jnp.where(d == a, teams, d) for d in drawn])
    offsets = [jnp.int32(0), a, b, teams - b, teams - a]
    slots = [jnp.int32(0)]
    for offset in offsets[1:]:
        slots.append(sum(jnp.where(d == offset, k + 1, 0) for k, d in enumerate(drawn)))
    return offsets, slots


def prepare_kernel(teams, place_ref, pattern_ref, omega_ref, out_ref):
    _, slots = stored_offsets(pattern_ref, place_ref[0], teams)
    for k in range(3):
        out_ref[k] = omega_ref[0, slots[k]].astype(BF16)


def product_kernel(teams, replicas, tile_rows, place_ref, pattern_ref, own_ref, low_ref, high_ref, *rest):
    chips = replicas // 2
    planes = LOW * chips
    depth = teams // LOW
    weight_refs, rest = rest[: 2 * planes], rest[2 * planes :]
    pair_outs, diagonal_outs, rest = rest[:planes], rest[planes : 2 * planes], rest[2 * planes :]
    data_ref, omega_ref, mixed_ref, flip_ref, left_ref, data_sems, omega_sems = rest
    team, replica = place_ref[0], place_ref[1]
    core, chip = lax.rem(replica, 2), lax.div(replica, 2)
    high, low = lax.div(team, LOW), lax.rem(team, LOW)
    offsets, _ = stored_offsets(pattern_ref, team, teams)
    times, width = data_ref.shape[1] // 2, data_ref.shape[2]

    copies = []
    for n, (source, first, half) in enumerate([(own_ref, 0, 0), (low_ref, 0, 1), (high_ref, teams // 2, 1)]):
        target = data_ref.at[pl.ds(first, source.shape[0]), pl.ds(half * times, times)]
        copies.append(pltpu.make_async_copy(source, target, data_sems.at[n]))
    for half in range(2):
        for mx in range(LOW):
            for my in range(chips):
                plane = mx * chips + my
                row = (2 * (chip ^ my) + (core ^ half)) * tile_rows
                for mz in range(depth):
                    i = (high ^ mz) * LOW + (low ^ mx)
                    target = omega_ref.at[i, :, pl.ds(pl.multiple_of(row, tile_rows), tile_rows)]
                    copies.append(
                        pltpu.make_async_copy(
                            weight_refs[half * planes + plane].at[mz],
                            target,
                            omega_sems.at[(half * planes + plane) * depth + mz],
                        )
                    )
    for copy in copies:
        copy.start()
    for copy in copies:
        copy.wait()

    nn = (((1,), (0,)), ((), ()))
    nt = (((1,), (1,)), ((), ()))

    def mix(i, carry):
        total = None
        for k, offset in enumerate(offsets):
            c = lax.rem(i + offset, teams)
            if k < 3:
                term = lax.dot_general(data_ref[c], omega_ref[i, k], nt, preferred_element_type=F32)
            else:
                term = lax.dot_general(data_ref[c], omega_ref[c, 5 - k], nn, preferred_element_type=F32)
            total = term if total is None else total + term
        mixed = total.astype(BF16)
        mixed_ref[i] = mixed
        flip_ref[:, : 2 * times] = mixed.T
        flip_ref[:, 2 * times :] = data_ref[i].T
        for m in range(chips):
            row = (2 * (chip ^ m) + core) * tile_rows
            left_ref[i, m * tile_rows : (m + 1) * tile_rows] = flip_ref[
                pl.ds(pl.multiple_of(row, tile_rows), tile_rows)
            ]
        return carry

    unroll = teams <= 8
    lax.fori_loop(0, teams, mix, 0, unroll=unroll)
    for mx in range(LOW):

        def outer(z, carry):
            i = z * LOW + (low ^ mx)
            for k, offset in enumerate(offsets[:3]):
                c = lax.rem(i + offset, teams)
                right = jnp.concatenate([data_ref[c], mixed_ref[c]], axis=0)
                part = lax.dot_general(left_ref[i], right, nn, preferred_element_type=F32).astype(BF16)
                for m in range(chips):
                    rows = part[m * tile_rows : (m + 1) * tile_rows]
                    if k:
                        pair_outs[mx * chips + m][z, k - 1] = rows
                    else:
                        diagonal_outs[mx * chips + m][z, 0] = rows
            return carry

        lax.fori_loop(0, depth, outer, 0, unroll=unroll)


def add_kernel(teams, place_ref, *rest):
    count = teams // LOW
    parts, outs = rest[:-count], rest[-count:]
    z = lax.div(place_ref[0], LOW)
    for m in range(count):
        total = parts[0][z ^ m].astype(F32)
        for part in parts[1:]:
            total = total + part[z ^ m].astype(F32)
        outs[m][...] = total.astype(outs[m].dtype)


def mirror_kernel(replicas, *rest):
    parts, own_ref, turned_ref = rest[:-2], rest[-2], rest[-1]
    tile_rows, width = own_ref.shape[1:]
    turned = []
    for k in range(2):
        total = parts[0][k].astype(F32)
        for part in parts[1:]:
            total = total + part[k].astype(F32)
        own_ref[k] = total
        turned.append(total.T)
    turned = jnp.concatenate(turned, axis=1).astype(BF16)
    turned_ref[...] = turned.reshape(replicas, width // replicas, 2 * tile_rows)


def update_kernel(teams, replicas, scale, place_ref, pattern_ref, omega_ref, pair_ref, *rest):
    parts, shifted = rest[: teams // LOW], rest[teams // LOW : -2]
    out_ref, chosen_ref = rest[-2:]
    offsets, slots = stored_offsets(pattern_ref, place_ref[0], teams)
    rows, width = out_ref.shape[2:]
    for distance, array in enumerate(shifted, 1):
        for k in range(2):

            @pl.when(offsets[k + 1] == distance)
            def _():
                chosen_ref[k] = array[...]

    first = place_ref[1] * rows
    row_ids = first + lax.broadcasted_iota(jnp.int32, (rows, width), 0)
    diagonal = row_ids == lax.broadcasted_iota(jnp.int32, (rows, width), 1)
    bound = STEP_SIZE * PENALTY
    for k in range(5):
        if k == 0:
            total = parts[0][0].astype(F32)
            for part in parts[1:]:
                total = total + part[0].astype(F32)
        elif k < 3:
            total = pair_ref[k - 1]
        else:
            side = 4 - k
            total = jnp.concatenate(
                [chosen_ref[side, r][:, side * rows : (side + 1) * rows] for r in range(replicas)], axis=1
            ).astype(F32)
        current = omega_ref[0, slots[k]]
        gradient = total * scale
        if k == 0:
            gradient = gradient - jnp.where(diagonal, 1.0 / current, 0.0)
        value = current - STEP_SIZE * gradient
        shrunk = jnp.where(value > bound, value - bound, jnp.where(value < -bound, value + bound, 0.0))
        if k == 0:
            shrunk = jnp.where(diagonal, value, shrunk)
        out_ref[0, slots[k]] = shrunk


def per_device(teams, replicas, signals, omega, pattern):
    chips = replicas // 2
    slots, tile_rows, width = omega.shape[1:]
    times = signals.shape[0] // teams
    place = jnp.stack([lax.axis_index("blk"), lax.axis_index("rep")]).astype(jnp.int32)

    def swap(array, blk_mask, rep_mask):
        route = [
            (b * replicas + r, (b ^ blk_mask) * replicas + (r ^ rep_mask))
            for b in range(teams)
            for r in range(replicas)
        ]
        return lax.ppermute(array, ("blk", "rep"), route)

    planes = LOW * chips
    count = teams // LOW
    upper = pl.pallas_call(
        functools.partial(prepare_kernel, teams),
        out_shape=jax.ShapeDtypeStruct((3, tile_rows, width), BF16),
        in_specs=[SMEM, SMEM, VMEM],
        out_specs=VMEM,
        compiler_params=SMALL,
        name="prepare",
    )(place, pattern, omega)

    line = jnp.stack([upper] + [swap(upper, m * LOW, 0) for m in range(1, count)])
    weights = [
        swap(line, mx, 2 * my) if mx + my else line for mx in range(LOW) for my in range(chips)
    ]
    own = lax.all_to_all(signals.reshape(teams, times, width), "blk", 0, 0)
    other = [swap(part, 0, 1) for part in jnp.split(own, 2)]
    weights += [swap(array, 0, 1) for array in weights]

    small = pltpu.CompilerParams(vmem_limit_bytes=(8 if teams <= 8 else 48) * 2**20)
    large = pltpu.CompilerParams(vmem_limit_bytes=(16 if teams <= 8 else 48) * 2**20)
    partial = pl.pallas_call(
        functools.partial(product_kernel, teams, replicas, tile_rows),
        out_shape=[jax.ShapeDtypeStruct((count, 2, tile_rows, width), BF16)] * planes
        + [jax.ShapeDtypeStruct((count, 1, tile_rows, width), BF16)] * planes,
        in_specs=[SMEM, SMEM] + [ANY] * (3 + 2 * planes),
        out_specs=[VMEM] * (2 * planes),
        scratch_shapes=[
            pltpu.VMEM((teams, 2 * times, width), BF16),
            pltpu.VMEM((teams, 3, width, width), BF16),
            pltpu.VMEM((teams, 2 * times, width), BF16),
            pltpu.VMEM((width, 4 * times), BF16),
            pltpu.VMEM((teams, chips * tile_rows, 4 * times), BF16),
            pltpu.SemaphoreType.DMA((3,)),
            pltpu.SemaphoreType.DMA((2 * planes * count,)),
        ],
        compiler_params=large,
        name="products",
    )(place, pattern, own, *other, *weights)

    def add_time(parts, tiles):
        received = [
            swap(parts[mx * chips + my], mx, 2 * my) if mx + my else parts[0]
            for mx in range(LOW)
            for my in range(chips)
        ]
        summed = pl.pallas_call(
            functools.partial(add_kernel, teams),
            out_shape=[
                jax.ShapeDtypeStruct((tiles, tile_rows, width), BF16 if m else F32) for m in range(count)
            ],
            in_specs=[SMEM] + [VMEM] * planes,
            out_specs=[VMEM] * count,
            compiler_params=small,
            name="plane_sum",
        )(place, *received)
        return [swap(summed[m], m * LOW, 0) if m else summed[0] for m in range(count)]

    pairs = add_time(partial[:planes], 2)
    diagonals = add_time(partial[planes:], 1)
    pair_sum, turned = pl.pallas_call(
        functools.partial(mirror_kernel, replicas),
        out_shape=[
            jax.ShapeDtypeStruct((2, tile_rows, width), F32),
            jax.ShapeDtypeStruct((replicas, width // replicas, 2 * tile_rows), BF16),
        ],
        in_specs=[VMEM] * count,
        out_specs=[VMEM] * 2,
        compiler_params=small,
        name="mirror",
    )(*pairs)
    turned = lax.all_to_all(turned, "rep", 0, 0)
    shifted = [
        lax.ppermute(turned, "blk", [(i, (i + d) % teams) for i in range(teams)])
        for d in range(1, (teams + 1) // 2)
    ]

    scale = 1.0 / (2.0 * signals.shape[0] * replicas)
    return pl.pallas_call(
        functools.partial(update_kernel, teams, replicas, scale),
        out_shape=jax.ShapeDtypeStruct(omega.shape, F32),
        in_specs=[SMEM, SMEM] + [VMEM] * (2 + count + len(shifted)),
        out_specs=VMEM,
        scratch_shapes=[pltpu.VMEM((2,) + turned.shape, BF16)],
        compiler_params=small,
        name="update",
    )(place, pattern, omega, pair_sum, *diagonals, *shifted)


def solution(mesh):
    return jax.shard_map(
        functools.partial(per_device, mesh.shape["blk"], mesh.shape["rep"]),
        mesh=mesh,
        in_specs=(P("rep", "blk"), P("blk", None, "rep", None), P("blk", None)),
        out_specs=P("blk", None, "rep", None),
        check_vma=False,
    )
```

```python
import functools

import jax
import jax.numpy as jnp
from jax import lax
from jax.experimental import pallas as pl
from jax.experimental.pallas import tpu as pltpu
from jax.sharding import Mesh, PartitionSpec as P

STEP_SIZE = 0.5
PENALTY = 0.1
LOW = 2
LINE_FIRST = (3, 4)
PLANE_FIRST = (0, 1, 2)
AXES = ("line", "low", "chip", "core")
BLK, REP = AXES[:2], AXES[2:]
F32 = jnp.float32
BF16 = jnp.bfloat16

VMEM = pl.BlockSpec(memory_space=pltpu.VMEM)
ANY = pl.BlockSpec(memory_space=pl.ANY)
SMEM = pl.BlockSpec(memory_space=pltpu.SMEM)


def stored_offsets(pattern_ref, team, teams):
    drawn = [lax.rem(pattern_ref[0, k] - team + teams, teams) for k in range(1, 5)]
    a = functools.reduce(jnp.minimum, drawn)
    b = functools.reduce(jnp.minimum, [jnp.where(d == a, teams, d) for d in drawn])
    offsets = [jnp.int32(0), a, b, teams - b, teams - a]
    slots = [jnp.int32(0)]
    for offset in offsets[1:]:
        slots.append(sum(jnp.where(d == offset, k + 1, 0) for k, d in enumerate(drawn)))
    return offsets, slots


def prepare_kernel(teams, place_ref, pattern_ref, omega_ref, signals_ref, upper_ref, across_ref, sem):
    team = place_ref[0]
    rows = across_ref.shape[0]
    first = pl.multiple_of((lax.rem(team, LOW) ^ 1) * rows, rows)
    copy = pltpu.make_async_copy(signals_ref.at[pl.ds(first, rows)], across_ref, sem)
    copy.start()
    _, slots = stored_offsets(pattern_ref, team, teams)
    for k in range(3):
        upper_ref[k] = omega_ref[0, slots[k]].astype(BF16)
    copy.wait()


def deal_kernel(place_ref, signals_ref, across_ref, out_ref, sems):
    rows = across_ref.shape[0]
    first = pl.multiple_of(lax.rem(place_ref[0], LOW) * rows, rows)
    sources = [signals_ref.at[pl.ds(first, rows)], across_ref]
    copies = [
        pltpu.make_async_copy(source.reshape(out_ref.shape[0], *out_ref.shape[2:]), out_ref.at[:, n], sems.at[n])
        for n, source in enumerate(sources)
    ]
    for copy in copies:
        copy.start()
    for copy in copies:
        copy.wait()


def product_kernel(teams, replicas, tile_rows, place_ref, pattern_ref, *rest):
    chips = replicas // 2
    planes = LOW * chips
    depth = teams // LOW
    block_refs, rest = rest[:3], rest[3:]
    weight_refs, rest = rest[: 2 * planes], rest[2 * planes :]
    plane_outs, line_out, rest = rest[:planes], rest[planes], rest[planes + 1 :]
    data_ref, omega_ref, mixed_ref, flip_ref, left_ref, data_sems, omega_sems = rest
    team, replica = place_ref[0], place_ref[1]
    core, chip = lax.rem(replica, 2), lax.div(replica, 2)
    high, low = lax.div(team, LOW), lax.rem(team, LOW)
    offsets, _ = stored_offsets(pattern_ref, team, teams)
    times, width = data_ref.shape[1] // 2, data_ref.shape[2]

    copies = []
    for half in range(2):
        for z in range(depth):
            source = block_refs[half + (z >= depth // 2) * half].at[z % (depth // 2) if half else z]
            for n in range(LOW):
                copies.append(
                    pltpu.make_async_copy(
                        source.at[n],
                        data_ref.at[z * LOW + (low ^ n), pl.ds(half * times, times)],
                        data_sems.at[(half * depth + z) * LOW + n],
                    )
                )
    for half in range(2):
        for mx in range(LOW):
            for my in range(chips):
                plane = mx * chips + my
                row = (2 * (chip ^ my) + (core ^ half)) * tile_rows
                for mz in range(depth):
                    i = (high ^ mz) * LOW + (low ^ mx)
                    target = omega_ref.at[i, :, pl.ds(pl.multiple_of(row, tile_rows), tile_rows)]
                    copies.append(
                        pltpu.make_async_copy(
                            weight_refs[half * planes + plane].at[mz],
                            target,
                            omega_sems.at[(half * planes + plane) * depth + mz],
                        )
                    )
    for copy in copies:
        copy.start()
    for copy in copies:
        copy.wait()

    nn = (((1,), (0,)), ((), ()))
    nt = (((1,), (1,)), ((), ()))

    def mix(i, carry):
        total = None
        for k, offset in enumerate(offsets):
            c = lax.rem(i + offset, teams)
            if k < 3:
                term = lax.dot_general(data_ref[c], omega_ref[i, k], nt, preferred_element_type=F32)
            else:
                term = lax.dot_general(data_ref[c], omega_ref[c, 5 - k], nn, preferred_element_type=F32)
            total = term if total is None else total + term
        mixed = total.astype(BF16)
        mixed_ref[i] = mixed
        flip_ref[:, : 2 * times] = mixed.T
        flip_ref[:, 2 * times :] = data_ref[i].T
        for m in range(chips):
            row = (2 * (chip ^ m) + core) * tile_rows
            left_ref[i, m * tile_rows : (m + 1) * tile_rows] = flip_ref[
                pl.ds(pl.multiple_of(row, tile_rows), tile_rows)
            ]
        return carry

    unroll = teams <= 8
    lax.fori_loop(0, teams, mix, 0, unroll=unroll)

    def part(i, k):
        c = lax.rem(i + offsets[k], teams)
        right = jnp.concatenate([data_ref[c], mixed_ref[c]], axis=0)
        product = lax.dot_general(left_ref[i], right, nn, preferred_element_type=F32).astype(BF16)
        return [product[m * tile_rows : (m + 1) * tile_rows] for m in range(chips)]

    for mx in range(LOW):

        def outer(z, carry):
            i = z * LOW + (low ^ mx)
            for n, k in enumerate(LINE_FIRST):
                for m, rows in enumerate(part(i, k)):
                    line_out[z, mx * chips + m, n] = rows
            for n, k in enumerate(PLANE_FIRST):
                for m, rows in enumerate(part(i, k)):
                    plane_outs[mx * chips + m][z, n] = rows
            return carry

        lax.fori_loop(0, depth, outer, 0, unroll=unroll)


def line_sum_kernel(parts_ref, *outs):
    for m, out in enumerate(outs):
        total = parts_ref[0, m].astype(F32)
        for z in range(1, parts_ref.shape[0]):
            total = total + parts_ref[z, m].astype(F32)
        out[...] = total.astype(out.dtype)


def plane_sum_kernel(teams, place_ref, *rest):
    count = teams // LOW
    parts, outs = rest[:-count], rest[-count:]
    z = lax.div(place_ref[0], LOW)
    for m in range(count):
        total = parts[0][z ^ m].astype(F32)
        for part in parts[1:]:
            total = total + part[z ^ m].astype(F32)
        outs[m][...] = total.astype(outs[m].dtype)


def update_kernel(teams, scale, place_ref, pattern_ref, omega_ref, *rest):
    depth = teams // LOW
    plane_first, line_first, out_ref = rest[:depth], rest[depth:-1], rest[-1]
    _, slots = stored_offsets(pattern_ref, place_ref[0], teams)
    rows, width = out_ref.shape[2:]
    first = place_ref[1] * rows
    row_ids = first + lax.broadcasted_iota(jnp.int32, (rows, width), 0)
    diagonal = row_ids == lax.broadcasted_iota(jnp.int32, (rows, width), 1)
    for k in range(5):
        parts, n = (line_first, LINE_FIRST.index(k)) if k in LINE_FIRST else (plane_first, PLANE_FIRST.index(k))
        total = parts[0][n].astype(F32)
        for part in parts[1:]:
            total = total + part[n].astype(F32)
        current = omega_ref[0, slots[k]]
        gradient = total * scale
        if k == 0:
            gradient = gradient - jnp.where(diagonal, 1.0 / current, 0.0)
        value = current - STEP_SIZE * gradient
        bound = STEP_SIZE * PENALTY
        shrunk = jnp.where(value > bound, value - bound, jnp.where(value < -bound, value + bound, 0.0))
        if k == 0:
            shrunk = jnp.where(diagonal, value, shrunk)
        out_ref[0, slots[k]] = shrunk


def per_device(teams, replicas, signals, omega, pattern):
    chips = replicas // 2
    slots, tile_rows, width = omega.shape[1:]
    times = signals.shape[0] // teams
    place = jnp.stack([lax.axis_index(BLK), lax.axis_index(REP)]).astype(jnp.int32)

    def swap(array, blk_mask, rep_mask):
        route = [
            (b * replicas + r, (b ^ blk_mask) * replicas + (r ^ rep_mask))
            for b in range(teams)
            for r in range(replicas)
        ]
        return lax.ppermute(array, AXES, route)

    planes = LOW * chips
    count = teams // LOW
    planes = LOW * chips
    count = teams // LOW
    small = pltpu.CompilerParams(vmem_limit_bytes=(8 if teams <= 8 else 48) * 2**20)
    large = pltpu.CompilerParams(vmem_limit_bytes=(18 if teams <= 8 else 56) * 2**20)

    def across_plane(arrays):
        return [
            swap(arrays[mx * chips + my], mx, 2 * my) if mx + my else arrays[0]
            for mx in range(LOW)
            for my in range(chips)
        ]

    def along_line(arrays):
        return [swap(array, m * LOW, 0) if m else array for m, array in enumerate(arrays)]

    upper, across = pl.pallas_call(
        functools.partial(prepare_kernel, teams),
        out_shape=[
            jax.ShapeDtypeStruct((3, tile_rows, width), BF16),
            jax.ShapeDtypeStruct((count * times, width), BF16),
        ],
        in_specs=[SMEM, SMEM, VMEM, ANY],
        out_specs=[VMEM, VMEM],
        scratch_shapes=[pltpu.SemaphoreType.DMA],
        compiler_params=small,
        name="prepare",
    )(place, pattern, omega, signals)

    across = swap(across, 1, 0)
    line = jnp.stack(along_line([upper] * count))
    weights = across_plane([line] * planes)
    weights += [swap(array, 0, 1) for array in weights]
    dealt = pl.pallas_call(
        deal_kernel,
        out_shape=jax.ShapeDtypeStruct((count, LOW, times, width), BF16),
        in_specs=[SMEM, ANY, VMEM],
        out_specs=VMEM,
        scratch_shapes=[pltpu.SemaphoreType.DMA((2,))],
        compiler_params=small,
        name="deal",
    )(place, signals, across)
    own = lax.all_to_all(dealt, "line", 0, 0)
    blocks = [own] + [swap(array, 0, 1) for array in jnp.split(own, 2)]

    partial = pl.pallas_call(
        functools.partial(product_kernel, teams, replicas, tile_rows),
        out_shape=[jax.ShapeDtypeStruct((count, len(PLANE_FIRST), tile_rows, width), BF16)] * planes
        + [jax.ShapeDtypeStruct((count, planes, len(LINE_FIRST), tile_rows, width), BF16)],
        in_specs=[SMEM, SMEM] + [ANY] * (3 + 2 * planes),
        out_specs=[VMEM] * (planes + 1),
        scratch_shapes=[
            pltpu.VMEM((teams, 2 * times, width), BF16),
            pltpu.VMEM((teams, 3, width, width), BF16),
            pltpu.VMEM((teams, 2 * times, width), BF16),
            pltpu.VMEM((width, 4 * times), BF16),
            pltpu.VMEM((teams, chips * tile_rows, 4 * times), BF16),
            pltpu.SemaphoreType.DMA((2 * teams,)),
            pltpu.SemaphoreType.DMA((2 * planes * count,)),
        ],
        compiler_params=large,
        name="products",
    )(place, pattern, *blocks, *weights)

    line_parts = lax.all_to_all(partial[planes], "line", 0, 0)
    plane_parts = across_plane(partial[:planes])
    plane_sums = pl.pallas_call(
        functools.partial(plane_sum_kernel, teams),
        out_shape=[
            jax.ShapeDtypeStruct((len(PLANE_FIRST), tile_rows, width), BF16 if m else F32) for m in range(count)
        ],
        in_specs=[SMEM] + [VMEM] * planes,
        out_specs=[VMEM] * count,
        compiler_params=small,
        name="plane_sum",
    )(place, *plane_parts)
    plane_sums = along_line(plane_sums)
    line_parts, plane_sums[1] = lax.optimization_barrier((line_parts, plane_sums[1]))
    line_sums = pl.pallas_call(
        line_sum_kernel,
        out_shape=[
            jax.ShapeDtypeStruct((len(LINE_FIRST), tile_rows, width), BF16 if m else F32) for m in range(planes)
        ],
        in_specs=[VMEM],
        out_specs=[VMEM] * planes,
        compiler_params=small,
        name="line_sum",
    )(line_parts)

    scale = 1.0 / (2.0 * signals.shape[0] * replicas)
    return pl.pallas_call(
        functools.partial(update_kernel, teams, scale),
        out_shape=jax.ShapeDtypeStruct(omega.shape, F32),
        in_specs=[SMEM, SMEM, VMEM] + [VMEM] * (count + planes),
        out_specs=VMEM,
        compiler_params=small,
        name="update",
    )(place, pattern, omega, *plane_sums, *across_plane(line_sums))


def solution(mesh):
    teams, replicas = mesh.shape["blk"], mesh.shape["rep"]
    fine = Mesh(mesh.devices.reshape(teams // LOW, LOW, replicas // 2, 2), AXES)
    return jax.shard_map(
        functools.partial(per_device, teams, replicas),
        mesh=fine,
        in_specs=(P(REP, BLK), P(BLK, None, REP, None), P(BLK, None)),
        out_specs=P(BLK, None, REP, None),
        check_vma=False,
    )
```

```python
import functools

import jax
import jax.numpy as jnp
from jax import lax
from jax.experimental import pallas as pl
from jax.experimental.pallas import tpu as pltpu
from jax.sharding import PartitionSpec as P

STEP_SIZE = 0.5
PENALTY = 0.1
LOW = 2
LINE_FIRST = (3, 4)
PLANE_FIRST = (0, 1, 2)
F32 = jnp.float32
BF16 = jnp.bfloat16

VMEM = pl.BlockSpec(memory_space=pltpu.VMEM)
ANY = pl.BlockSpec(memory_space=pl.ANY)
SMEM = pl.BlockSpec(memory_space=pltpu.SMEM)


def stored_offsets(pattern_ref, team, teams):
    drawn = [lax.rem(pattern_ref[0, k] - team + teams, teams) for k in range(1, 5)]
    a = functools.reduce(jnp.minimum, drawn)
    b = functools.reduce(jnp.minimum, [jnp.where(d == a, teams, d) for d in drawn])
    offsets = [jnp.int32(0), a, b, teams - b, teams - a]
    slots = [jnp.int32(0)]
    for offset in offsets[1:]:
        slots.append(sum(jnp.where(d == offset, k + 1, 0) for k, d in enumerate(drawn)))
    return offsets, slots


def prepare_kernel(teams, place_ref, pattern_ref, omega_ref, out_ref):
    _, slots = stored_offsets(pattern_ref, place_ref[0], teams)
    for k in range(3):
        out_ref[k] = omega_ref[0, slots[k]].astype(BF16)


def product_kernel(teams, replicas, tile_rows, place_ref, pattern_ref, *rest):
    chips = replicas // 2
    planes = LOW * chips
    depth = teams // LOW
    own_ref, low_ref, high_ref, *rest = rest
    weight_refs, rest = rest[: 2 * planes], rest[2 * planes :]
    plane_outs, line_outs, rest = rest[:planes], rest[planes : planes + depth], rest[planes + depth :]
    data_ref, omega_ref, mixed_ref, flip_ref, left_ref, data_sems, omega_sems = rest
    team, replica = place_ref[0], place_ref[1]
    core, chip = lax.rem(replica, 2), lax.div(replica, 2)
    high, low = lax.div(team, LOW), lax.rem(team, LOW)
    offsets, _ = stored_offsets(pattern_ref, team, teams)
    times, width = data_ref.shape[1] // 2, data_ref.shape[2]

    copies = []
    for n, (source, first, half) in enumerate([(own_ref, 0, 0), (low_ref, 0, 1), (high_ref, teams // 2, 1)]):
        target = data_ref.at[pl.ds(first, source.shape[0]), pl.ds(half * times, times)]
        copies.append(pltpu.make_async_copy(source, target, data_sems.at[n]))
    for half in range(2):
        for mx in range(LOW):
            for my in range(chips):
                plane = mx * chips + my
                row = (2 * (chip ^ my) + (core ^ half)) * tile_rows
                for mz in range(depth):
                    i = (high ^ mz) * LOW + (low ^ mx)
                    target = omega_ref.at[i, :, pl.ds(pl.multiple_of(row, tile_rows), tile_rows)]
                    copies.append(
                        pltpu.make_async_copy(
                            weight_refs[half * planes + plane].at[mz],
                            target,
                            omega_sems.at[(half * planes + plane) * depth + mz],
                        )
                    )
    for copy in copies:
        copy.start()
    for copy in copies:
        copy.wait()

    nn = (((1,), (0,)), ((), ()))
    nt = (((1,), (1,)), ((), ()))

    def mix(i, carry):
        total = None
        for k, offset in enumerate(offsets):
            c = lax.rem(i + offset, teams)
            if k < 3:
                term = lax.dot_general(data_ref[c], omega_ref[i, k], nt, preferred_element_type=F32)
            else:
                term = lax.dot_general(data_ref[c], omega_ref[c, 5 - k], nn, preferred_element_type=F32)
            total = term if total is None else total + term
        mixed = total.astype(BF16)
        mixed_ref[i] = mixed
        flip_ref[:, : 2 * times] = mixed.T
        flip_ref[:, 2 * times :] = data_ref[i].T
        for m in range(chips):
            row = (2 * (chip ^ m) + core) * tile_rows
            left_ref[i, m * tile_rows : (m + 1) * tile_rows] = flip_ref[
                pl.ds(pl.multiple_of(row, tile_rows), tile_rows)
            ]
        return carry

    unroll = teams <= 8
    lax.fori_loop(0, teams, mix, 0, unroll=unroll)

    def part(i, k):
        c = lax.rem(i + offsets[k], teams)
        right = jnp.concatenate([data_ref[c], mixed_ref[c]], axis=0)
        product = lax.dot_general(left_ref[i], right, nn, preferred_element_type=F32).astype(BF16)
        return [product[m * tile_rows : (m + 1) * tile_rows] for m in range(chips)]

    for mx in range(LOW):
        for mz in range(depth):
            i = (high ^ mz) * LOW + (low ^ mx)
            for n, k in enumerate(LINE_FIRST):
                for m, rows in enumerate(part(i, k)):
                    line_outs[mz][mx * chips + m, n] = rows
    for mx in range(LOW):

        def outer(z, carry):
            i = z * LOW + (low ^ mx)
            for n, k in enumerate(PLANE_FIRST):
                for m, rows in enumerate(part(i, k)):
                    plane_outs[mx * chips + m][z, n] = rows
            return carry

        lax.fori_loop(0, depth, outer, 0, unroll=unroll)


def line_sum_kernel(planes, *rest):
    parts, outs = rest[:-planes], rest[-planes:]
    for m in range(planes):
        total = parts[0][m].astype(F32)
        for part in parts[1:]:
            total = total + part[m].astype(F32)
        outs[m][...] = total.astype(outs[m].dtype)


def plane_sum_kernel(teams, place_ref, *rest):
    count = teams // LOW
    parts, outs = rest[:-count], rest[-count:]
    z = lax.div(place_ref[0], LOW)
    for m in range(count):
        total = parts[0][z ^ m].astype(F32)
        for part in parts[1:]:
            total = total + part[z ^ m].astype(F32)
        outs[m][...] = total.astype(outs[m].dtype)


def update_kernel(teams, scale, place_ref, pattern_ref, omega_ref, *rest):
    depth = teams // LOW
    plane_first, line_first, out_ref = rest[:depth], rest[depth:-1], rest[-1]
    _, slots = stored_offsets(pattern_ref, place_ref[0], teams)
    rows, width = out_ref.shape[2:]
    first = place_ref[1] * rows
    row_ids = first + lax.broadcasted_iota(jnp.int32, (rows, width), 0)
    diagonal = row_ids == lax.broadcasted_iota(jnp.int32, (rows, width), 1)
    for k in range(5):
        parts, n = (line_first, LINE_FIRST.index(k)) if k in LINE_FIRST else (plane_first, PLANE_FIRST.index(k))
        total = parts[0][n].astype(F32)
        for part in parts[1:]:
            total = total + part[n].astype(F32)
        current = omega_ref[0, slots[k]]
        gradient = total * scale
        if k == 0:
            gradient = gradient - jnp.where(diagonal, 1.0 / current, 0.0)
        value = current - STEP_SIZE * gradient
        bound = STEP_SIZE * PENALTY
        shrunk = jnp.where(value > bound, value - bound, jnp.where(value < -bound, value + bound, 0.0))
        if k == 0:
            shrunk = jnp.where(diagonal, value, shrunk)
        out_ref[0, slots[k]] = shrunk


def per_device(teams, replicas, signals, omega, pattern):
    chips = replicas // 2
    slots, tile_rows, width = omega.shape[1:]
    times = signals.shape[0] // teams
    place = jnp.stack([lax.axis_index("blk"), lax.axis_index("rep")]).astype(jnp.int32)

    def swap(array, blk_mask, rep_mask):
        route = [
            (b * replicas + r, (b ^ blk_mask) * replicas + (r ^ rep_mask))
            for b in range(teams)
            for r in range(replicas)
        ]
        return lax.ppermute(array, ("blk", "rep"), route)

    planes = LOW * chips
    count = teams // LOW
    planes = LOW * chips
    count = teams // LOW
    small = pltpu.CompilerParams(vmem_limit_bytes=(8 if teams <= 8 else 48) * 2**20)
    large = pltpu.CompilerParams(vmem_limit_bytes=(14 if teams <= 8 else 56) * 2**20)

    def across_plane(arrays):
        return [
            swap(arrays[mx * chips + my], mx, 2 * my) if mx + my else arrays[0]
            for mx in range(LOW)
            for my in range(chips)
        ]

    def along_line(arrays):
        return [swap(array, m * LOW, 0) if m else array for m, array in enumerate(arrays)]

    upper = pl.pallas_call(
        functools.partial(prepare_kernel, teams),
        out_shape=jax.ShapeDtypeStruct((3, tile_rows, width), BF16),
        in_specs=[SMEM, SMEM, VMEM],
        out_specs=VMEM,
        compiler_params=small,
        name="prepare",
    )(place, pattern, omega)

    line = jnp.stack(along_line([upper] * count))
    line, signals = lax.optimization_barrier((line, signals))
    rows = [line, swap(line, 1, 0)]
    weights = [swap(row, 0, 2 * my) if my else row for row in rows for my in range(chips)]
    own = lax.all_to_all(signals.reshape(teams, times, width), "blk", 0, 0)
    weights[-1], own = lax.optimization_barrier((weights[-1], own))
    other = [swap(part, 0, 1) for part in jnp.split(own, 2)]
    weights += [swap(array, 0, 1) for array in weights]

    partial = pl.pallas_call(
        functools.partial(product_kernel, teams, replicas, tile_rows),
        out_shape=[jax.ShapeDtypeStruct((count, len(PLANE_FIRST), tile_rows, width), BF16)] * planes
        + [jax.ShapeDtypeStruct((planes, len(LINE_FIRST), tile_rows, width), BF16)] * count,
        in_specs=[SMEM, SMEM] + [ANY] * (3 + 2 * planes),
        out_specs=[VMEM] * (planes + count),
        scratch_shapes=[
            pltpu.VMEM((teams, 2 * times, width), BF16),
            pltpu.VMEM((teams, 3, width, width), BF16),
            pltpu.VMEM((teams, 2 * times, width), BF16),
            pltpu.VMEM((width, 4 * times), BF16),
            pltpu.VMEM((teams, chips * tile_rows, 4 * times), BF16),
            pltpu.SemaphoreType.DMA((3,)),
            pltpu.SemaphoreType.DMA((2 * planes * count,)),
        ],
        compiler_params=large,
        name="products",
    )(place, pattern, own, *other, *weights)

    partial = list(partial)
    line_parts = along_line(partial[planes:])
    partial[planes - 1], line_parts[2] = lax.optimization_barrier((partial[planes - 1], line_parts[2]))
    plane_parts = across_plane(partial[:planes])
    plane_sums = pl.pallas_call(
        functools.partial(plane_sum_kernel, teams),
        out_shape=[
            jax.ShapeDtypeStruct((len(PLANE_FIRST), tile_rows, width), BF16 if m else F32) for m in range(count)
        ],
        in_specs=[SMEM] + [VMEM] * planes,
        out_specs=[VMEM] * count,
        compiler_params=small,
        name="plane_sum",
    )(place, *plane_parts)
    plane_sums = along_line(plane_sums)
    line_parts[1], plane_sums[1] = lax.optimization_barrier((line_parts[1], plane_sums[1]))
    line_sums = pl.pallas_call(
        functools.partial(line_sum_kernel, planes),
        out_shape=[
            jax.ShapeDtypeStruct((len(LINE_FIRST), tile_rows, width), BF16 if m else F32) for m in range(planes)
        ],
        in_specs=[VMEM] * count,
        out_specs=[VMEM] * planes,
        compiler_params=small,
        name="line_sum",
    )(*line_parts)

    scale = 1.0 / (2.0 * signals.shape[0] * replicas)
    return pl.pallas_call(
        functools.partial(update_kernel, teams, scale),
        out_shape=jax.ShapeDtypeStruct(omega.shape, F32),
        in_specs=[SMEM, SMEM, VMEM] + [VMEM] * (count + planes),
        out_specs=VMEM,
        compiler_params=small,
        name="update",
    )(place, pattern, omega, *plane_sums, *across_plane(line_sums))


def solution(mesh):
    return jax.shard_map(
        functools.partial(per_device, mesh.shape["blk"], mesh.shape["rep"]),
        mesh=mesh,
        in_specs=(P("rep", "blk"), P("blk", None, "rep", None), P("blk", None)),
        out_specs=P("blk", None, "rep", None),
        check_vma=False,
    )
```

```python
import functools

import jax
import jax.numpy as jnp
from jax import lax
from jax.experimental import pallas as pl
from jax.experimental.pallas import tpu as pltpu
from jax.sharding import PartitionSpec as P

STEP_SIZE = 0.5
PENALTY = 0.1
LOW = 2
LINE_FIRST = (4,)
PLANE_FIRST = (0, 1, 2, 3)
F32 = jnp.float32
BF16 = jnp.bfloat16

VMEM = pl.BlockSpec(memory_space=pltpu.VMEM)
ANY = pl.BlockSpec(memory_space=pl.ANY)
SMEM = pl.BlockSpec(memory_space=pltpu.SMEM)


def stored_offsets(pattern_ref, team, teams):
    drawn = [lax.rem(pattern_ref[0, k] - team + teams, teams) for k in range(1, 5)]
    a = functools.reduce(jnp.minimum, drawn)
    b = functools.reduce(jnp.minimum, [jnp.where(d == a, teams, d) for d in drawn])
    offsets = [jnp.int32(0), a, b, teams - b, teams - a]
    slots = [jnp.int32(0)]
    for offset in offsets[1:]:
        slots.append(sum(jnp.where(d == offset, k + 1, 0) for k, d in enumerate(drawn)))
    return offsets, slots


def prepare_kernel(teams, place_ref, pattern_ref, omega_ref, out_ref):
    _, slots = stored_offsets(pattern_ref, place_ref[0], teams)
    for k in range(3):
        out_ref[k] = omega_ref[0, slots[k]].astype(BF16)


NN = (((1,), (0,)), ((), ()))
NT = (((1,), (1,)), ((), ()))


def block(data_refs, c):
    return jnp.concatenate([ref[c] for ref in data_refs], axis=0)


def mix_kernel(teams, replicas, tile_rows, place_ref, pattern_ref, *rest):
    chips = replicas // 2
    planes = LOW * chips
    depth = teams // LOW
    data_refs, rest = rest[:3], rest[3:]
    weight_refs, rest = rest[: 2 * planes], rest[2 * planes :]
    mixed_ref, left_ref, omega_ref, flip_ref, sems = rest
    team, replica = place_ref[0], place_ref[1]
    core, chip = lax.rem(replica, 2), lax.div(replica, 2)
    high, low = lax.div(team, LOW), lax.rem(team, LOW)
    offsets, _ = stored_offsets(pattern_ref, team, teams)
    times = mixed_ref.shape[1]

    copies = []
    for half in range(2):
        for mx in range(LOW):
            for my in range(chips):
                plane = mx * chips + my
                row = (2 * (chip ^ my) + (core ^ half)) * tile_rows
                for mz in range(depth):
                    i = (high ^ mz) * LOW + (low ^ mx)
                    target = omega_ref.at[i, :, pl.ds(pl.multiple_of(row, tile_rows), tile_rows)]
                    copies.append(
                        pltpu.make_async_copy(
                            weight_refs[half * planes + plane].at[mz],
                            target,
                            sems.at[(half * planes + plane) * depth + mz],
                        )
                    )
    for copy in copies:
        copy.start()

    def keep(i, first, array):
        flip_ref[...] = array.T
        for m in range(chips):
            row = (2 * (chip ^ m) + core) * tile_rows
            left_ref[i, m * tile_rows : (m + 1) * tile_rows, first : first + times] = flip_ref[
                pl.ds(pl.multiple_of(row, tile_rows), tile_rows)
            ]

    def turn(i, carry):
        keep(i, times, block(data_refs, i))
        return carry

    def mix(i, carry):
        total = None
        for k, offset in enumerate(offsets):
            c = lax.rem(i + offset, teams)
            if k < 3:
                term = lax.dot_general(block(data_refs, c), omega_ref[i, k], NT, preferred_element_type=F32)
            else:
                term = lax.dot_general(block(data_refs, c), omega_ref[c, 5 - k], NN, preferred_element_type=F32)
            total = term if total is None else total + term
        mixed = total.astype(BF16)
        mixed_ref[i] = mixed
        keep(i, 0, mixed)
        return carry

    unroll = teams <= 8
    lax.fori_loop(0, teams, turn, 0, unroll=unroll)
    for copy in copies:
        copy.wait()
    lax.fori_loop(0, teams, mix, 0, unroll=unroll)


def product_kernel(teams, chips, far, place_ref, pattern_ref, *rest):
    depth = teams // LOW
    data_refs, mixed_ref, left_ref, outs = rest[:3], rest[3], rest[4], rest[5:]
    plane_outs, line_outs = outs[: chips * len(far)], outs[chips * len(far) :]
    team = place_ref[0]
    high, low = lax.div(team, LOW), lax.rem(team, LOW)
    offsets, _ = stored_offsets(pattern_ref, team, teams)
    tile_rows = left_ref.shape[1] // chips

    def part(i, k):
        c = lax.rem(i + offsets[k], teams)
        right = jnp.concatenate([block(data_refs, c), mixed_ref[c]], axis=0)
        product = lax.dot_general(left_ref[i], right, NN, preferred_element_type=F32).astype(BF16)
        return [product[m * tile_rows : (m + 1) * tile_rows] for m in range(chips)]

    if line_outs:
        for mx in range(LOW):
            for mz in range(depth):
                i = (high ^ mz) * LOW + (low ^ mx)
                for n, k in enumerate(LINE_FIRST):
                    for m, rows in enumerate(part(i, k)):
                        line_outs[mz][mx * chips + m, n] = rows
    for index, mx in enumerate(far):

        def outer(z, carry):
            i = z * LOW + (low ^ mx)
            for n, k in enumerate(PLANE_FIRST):
                for m, rows in enumerate(part(i, k)):
                    plane_outs[index * chips + m][z, n] = rows
            return carry

        lax.fori_loop(0, depth, outer, 0, unroll=teams <= 8)


def line_sum_kernel(planes, *rest):
    parts, outs = rest[:-planes], rest[-planes:]
    for m in range(planes):
        total = parts[0][m].astype(F32)
        for part in parts[1:]:
            total = total + part[m].astype(F32)
        outs[m][...] = total.astype(outs[m].dtype)


def plane_sum_kernel(teams, place_ref, *rest):
    count = teams // LOW
    parts, outs = rest[:-count], rest[-count:]
    z = lax.div(place_ref[0], LOW)
    for m in range(count):
        total = parts[0][z ^ m].astype(F32)
        for part in parts[1:]:
            total = total + part[z ^ m].astype(F32)
        outs[m][...] = total.astype(outs[m].dtype)


def update_kernel(teams, scale, place_ref, pattern_ref, omega_ref, *rest):
    depth = teams // LOW
    plane_first, line_first, out_ref = rest[:depth], rest[depth:-1], rest[-1]
    _, slots = stored_offsets(pattern_ref, place_ref[0], teams)
    rows, width = out_ref.shape[2:]
    first = place_ref[1] * rows
    row_ids = first + lax.broadcasted_iota(jnp.int32, (rows, width), 0)
    diagonal = row_ids == lax.broadcasted_iota(jnp.int32, (rows, width), 1)
    for k in range(5):
        parts, n = (line_first, LINE_FIRST.index(k)) if k in LINE_FIRST else (plane_first, PLANE_FIRST.index(k))
        total = parts[0][n].astype(F32)
        for part in parts[1:]:
            total = total + part[n].astype(F32)
        current = omega_ref[0, slots[k]]
        gradient = total * scale
        if k == 0:
            gradient = gradient - jnp.where(diagonal, 1.0 / current, 0.0)
        value = current - STEP_SIZE * gradient
        bound = STEP_SIZE * PENALTY
        shrunk = jnp.where(value > bound, value - bound, jnp.where(value < -bound, value + bound, 0.0))
        if k == 0:
            shrunk = jnp.where(diagonal, value, shrunk)
        out_ref[0, slots[k]] = shrunk


def per_device(teams, replicas, signals, omega, pattern):
    chips = replicas // 2
    slots, tile_rows, width = omega.shape[1:]
    times = signals.shape[0] // teams
    place = jnp.stack([lax.axis_index("blk"), lax.axis_index("rep")]).astype(jnp.int32)

    def swap(array, blk_mask, rep_mask):
        route = [
            (b * replicas + r, (b ^ blk_mask) * replicas + (r ^ rep_mask))
            for b in range(teams)
            for r in range(replicas)
        ]
        return lax.ppermute(array, ("blk", "rep"), route)

    planes = LOW * chips
    count = teams // LOW
    planes = LOW * chips
    count = teams // LOW
    small = pltpu.CompilerParams(vmem_limit_bytes=(6 if teams <= 8 else 24) * 2**20)
    large = pltpu.CompilerParams(vmem_limit_bytes=(8 if teams <= 8 else 32) * 2**20)

    def across_plane(arrays):
        return [
            swap(arrays[mx * chips + my], mx, 2 * my) if mx + my else arrays[0]
            for mx in range(LOW)
            for my in range(chips)
        ]

    def along_line(arrays):
        return [swap(array, m * LOW, 0) if m else array for m, array in enumerate(arrays)]

    upper = pl.pallas_call(
        functools.partial(prepare_kernel, teams),
        out_shape=jax.ShapeDtypeStruct((3, tile_rows, width), BF16),
        in_specs=[SMEM, SMEM, VMEM],
        out_specs=VMEM,
        compiler_params=small,
        name="prepare",
    )(place, pattern, omega)

    line = jnp.stack(along_line([upper] * count))
    line, signals = lax.optimization_barrier((line, signals))
    weights = across_plane([line] * planes)
    own = lax.all_to_all(signals.reshape(teams, times, width), "blk", 0, 0)
    data = [own] + [swap(part, 0, 1) for part in jnp.split(own, 2, axis=1)]
    weights += [swap(array, 0, 1) for array in weights]

    mixed, left = pl.pallas_call(
        functools.partial(mix_kernel, teams, replicas, tile_rows),
        out_shape=[
            jax.ShapeDtypeStruct((teams, 2 * times, width), BF16),
            jax.ShapeDtypeStruct((teams, chips * tile_rows, 4 * times), BF16),
        ],
        in_specs=[SMEM, SMEM] + [VMEM] * 3 + [ANY] * (2 * planes),
        out_specs=[VMEM, VMEM],
        scratch_shapes=[
            pltpu.VMEM((teams, 3, width, width), BF16),
            pltpu.VMEM((width, 2 * times), BF16),
            pltpu.SemaphoreType.DMA((2 * planes * count,)),
        ],
        compiler_params=large,
        name="mix",
    )(place, pattern, *data, *weights)

    def products(far, lines):
        return pl.pallas_call(
            functools.partial(product_kernel, teams, chips, far),
            out_shape=[jax.ShapeDtypeStruct((count, len(PLANE_FIRST), tile_rows, width), BF16)] * (chips * len(far))
            + [jax.ShapeDtypeStruct((planes, len(LINE_FIRST), tile_rows, width), BF16)] * lines,
            in_specs=[SMEM, SMEM] + [VMEM] * 5,
            out_specs=[VMEM] * (chips * len(far) + lines),
            compiler_params=small,
            name="products",
        )(place, pattern, *data, mixed, left)

    far_parts = products((1,), 0)
    near_parts = products((0,), count)
    plane_parts = across_plane(list(near_parts[:chips]) + list(far_parts))
    line_parts = along_line(near_parts[chips:])
    line_sums = pl.pallas_call(
        functools.partial(line_sum_kernel, planes),
        out_shape=[
            jax.ShapeDtypeStruct((len(LINE_FIRST), tile_rows, width), BF16 if m else F32) for m in range(planes)
        ],
        in_specs=[VMEM] * count,
        out_specs=[VMEM] * planes,
        compiler_params=small,
        name="line_sum",
    )(*line_parts)
    line_sums = across_plane(line_sums)
    plane_parts, line_sums = lax.optimization_barrier((plane_parts, line_sums))
    plane_sums = pl.pallas_call(
        functools.partial(plane_sum_kernel, teams),
        out_shape=[
            jax.ShapeDtypeStruct((len(PLANE_FIRST), tile_rows, width), BF16 if m else F32) for m in range(count)
        ],
        in_specs=[SMEM] + [VMEM] * planes,
        out_specs=[VMEM] * count,
        compiler_params=small,
        name="plane_sum",
    )(place, *plane_parts)
    plane_sums = along_line(plane_sums)

    scale = 1.0 / (2.0 * signals.shape[0] * replicas)
    return pl.pallas_call(
        functools.partial(update_kernel, teams, scale),
        out_shape=jax.ShapeDtypeStruct(omega.shape, F32),
        in_specs=[SMEM, SMEM, VMEM] + [VMEM] * (count + planes),
        out_specs=VMEM,
        compiler_params=small,
        name="update",
    )(place, pattern, omega, *plane_sums, *line_sums)


def solution(mesh):
    return jax.shard_map(
        functools.partial(per_device, mesh.shape["blk"], mesh.shape["rep"]),
        mesh=mesh,
        in_specs=(P("rep", "blk"), P("blk", None, "rep", None), P("blk", None)),
        out_specs=P("blk", None, "rep", None),
        check_vma=False,
    )
```

```python
import functools

import jax
import jax.numpy as jnp
from jax import lax
from jax.experimental import pallas as pl
from jax.experimental.pallas import tpu as pltpu
from jax.sharding import PartitionSpec as P

STEP_SIZE = 0.5
PENALTY = 0.1
LOW = 2
F32 = jnp.float32
BF16 = jnp.bfloat16

VMEM = pl.BlockSpec(memory_space=pltpu.VMEM)
ANY = pl.BlockSpec(memory_space=pl.ANY)
SMEM = pl.BlockSpec(memory_space=pltpu.SMEM)


def stored_offsets(pattern_ref, team, teams):
    drawn = [lax.rem(pattern_ref[0, k] - team + teams, teams) for k in range(1, 5)]
    a = functools.reduce(jnp.minimum, drawn)
    b = functools.reduce(jnp.minimum, [jnp.where(d == a, teams, d) for d in drawn])
    offsets = [jnp.int32(0), a, b, teams - b, teams - a]
    slots = [jnp.int32(0)]
    for offset in offsets[1:]:
        slots.append(sum(jnp.where(d == offset, k + 1, 0) for k, d in enumerate(drawn)))
    return offsets, slots


def prepare_kernel(teams, place_ref, pattern_ref, omega_ref, out_ref):
    _, slots = stored_offsets(pattern_ref, place_ref[0], teams)
    for k in range(3):
        out_ref[k] = omega_ref[0, slots[k]].astype(BF16)


NN = (((1,), (0,)), ((), ()))
NT = (((1,), (1,)), ((), ()))


def block(data_refs, c):
    return jnp.concatenate([ref[c] for ref in data_refs], axis=0)


def mix_kernel(teams, replicas, tile_rows, place_ref, pattern_ref, *rest):
    chips = replicas // 2
    planes = LOW * chips
    depth = teams // LOW
    data_refs, rest = rest[:3], rest[3:]
    weight_refs, rest = rest[: 2 * planes], rest[2 * planes :]
    mixed_ref, left_ref, omega_ref, flip_ref, sems = rest
    team, replica = place_ref[0], place_ref[1]
    core, chip = lax.rem(replica, 2), lax.div(replica, 2)
    high, low = lax.div(team, LOW), lax.rem(team, LOW)
    offsets, _ = stored_offsets(pattern_ref, team, teams)
    times = mixed_ref.shape[1]

    copies = []
    for half in range(2):
        for mx in range(LOW):
            for my in range(chips):
                plane = mx * chips + my
                row = (2 * (chip ^ my) + (core ^ half)) * tile_rows
                for mz in range(depth):
                    i = (high ^ mz) * LOW + (low ^ mx)
                    target = omega_ref.at[i, :, pl.ds(pl.multiple_of(row, tile_rows), tile_rows)]
                    copies.append(
                        pltpu.make_async_copy(
                            weight_refs[half * planes + plane].at[mz],
                            target,
                            sems.at[(half * planes + plane) * depth + mz],
                        )
                    )
    for copy in copies:
        copy.start()

    def keep(i, first, array):
        flip_ref[...] = array.T
        for m in range(chips):
            row = (2 * (chip ^ m) + core) * tile_rows
            left_ref[i, m * tile_rows : (m + 1) * tile_rows, first : first + times] = flip_ref[
                pl.ds(pl.multiple_of(row, tile_rows), tile_rows)
            ]

    def turn(i, carry):
        keep(i, times, block(data_refs, i))
        return carry

    def mix(i, carry):
        total = None
        for k, offset in enumerate(offsets):
            c = lax.rem(i + offset, teams)
            if k < 3:
                term = lax.dot_general(block(data_refs, c), omega_ref[i, k], NT, preferred_element_type=F32)
            else:
                term = lax.dot_general(block(data_refs, c), omega_ref[c, 5 - k], NN, preferred_element_type=F32)
            total = term if total is None else total + term
        mixed = total.astype(BF16)
        mixed_ref[i] = mixed
        keep(i, 0, mixed)
        return carry

    unroll = teams <= 8
    lax.fori_loop(0, teams, turn, 0, unroll=unroll)
    for copy in copies:
        copy.wait()
    lax.fori_loop(0, teams, mix, 0, unroll=unroll)


def product_kernel(teams, chips, wanted, place_ref, pattern_ref, *rest):
    data_refs, mixed_ref, left_ref, outs = rest[:3], rest[3], rest[4], rest[5:]
    team = place_ref[0]
    high, low = lax.div(team, LOW), lax.rem(team, LOW)
    offsets, _ = stored_offsets(pattern_ref, team, teams)
    tile_rows = left_ref.shape[1] // chips
    for mz, mx in sorted({key[:2] for key in wanted}):
        i = (high ^ mz) * LOW + (low ^ mx)
        for k, offset in enumerate(offsets):
            c = lax.rem(i + offset, teams)
            right = jnp.concatenate([block(data_refs, c), mixed_ref[c]], axis=0)
            product = lax.dot_general(left_ref[i], right, NN, preferred_element_type=F32)
            for m in range(chips):
                if (mz, mx, m) in wanted:
                    out, place = wanted[mz, mx, m]
                    outs[out][place + (k,)] = product[m * tile_rows : (m + 1) * tile_rows].astype(outs[out].dtype)


def add_kernel(groups, *refs):
    outs = refs[len(refs) - len(groups) :]
    for out, terms in zip(outs, groups):
        total = None
        for source, index in terms:
            term = (refs[source][...] if index is None else refs[source][index]).astype(F32)
            total = term if total is None else total + term
        out[...] = total.astype(out.dtype)


def update_kernel(teams, scale, place_ref, pattern_ref, omega_ref, *rest):
    parts, out_ref = rest[:-1], rest[-1]
    _, slots = stored_offsets(pattern_ref, place_ref[0], teams)
    rows, width = out_ref.shape[2:]
    first = place_ref[1] * rows
    row_ids = first + lax.broadcasted_iota(jnp.int32, (rows, width), 0)
    diagonal = row_ids == lax.broadcasted_iota(jnp.int32, (rows, width), 1)
    for k in range(5):
        total = parts[0][k].astype(F32)
        for part in parts[1:]:
            total = total + part[k].astype(F32)
        current = omega_ref[0, slots[k]]
        gradient = total * scale
        if k == 0:
            gradient = gradient - jnp.where(diagonal, 1.0 / current, 0.0)
        value = current - STEP_SIZE * gradient
        bound = STEP_SIZE * PENALTY
        shrunk = jnp.where(value > bound, value - bound, jnp.where(value < -bound, value + bound, 0.0))
        if k == 0:
            shrunk = jnp.where(diagonal, value, shrunk)
        out_ref[0, slots[k]] = shrunk


def per_device(teams, replicas, signals, omega, pattern):
    chips = replicas // 2
    slots, tile_rows, width = omega.shape[1:]
    times = signals.shape[0] // teams
    place = jnp.stack([lax.axis_index("blk"), lax.axis_index("rep")]).astype(jnp.int32)

    def swap(array, blk_mask, rep_mask):
        route = [
            (b * replicas + r, (b ^ blk_mask) * replicas + (r ^ rep_mask))
            for b in range(teams)
            for r in range(replicas)
        ]
        return lax.ppermute(array, ("blk", "rep"), route)

    planes = LOW * chips
    count = teams // LOW
    planes = LOW * chips
    count = teams // LOW
    small = pltpu.CompilerParams(vmem_limit_bytes=(6 if teams <= 8 else 24) * 2**20)
    large = pltpu.CompilerParams(vmem_limit_bytes=(8 if teams <= 8 else 32) * 2**20)

    def across_plane(arrays):
        return [
            swap(arrays[mx * chips + my], mx, 2 * my) if mx + my else arrays[0]
            for mx in range(LOW)
            for my in range(chips)
        ]

    def along_line(arrays):
        return [swap(array, m * LOW, 0) if m else array for m, array in enumerate(arrays)]

    upper = pl.pallas_call(
        functools.partial(prepare_kernel, teams),
        out_shape=jax.ShapeDtypeStruct((3, tile_rows, width), BF16),
        in_specs=[SMEM, SMEM, VMEM],
        out_specs=VMEM,
        compiler_params=small,
        name="prepare",
    )(place, pattern, omega)

    line = jnp.stack(along_line([upper] * count))
    line, signals = lax.optimization_barrier((line, signals))
    weights = across_plane([line] * planes)
    own = lax.all_to_all(signals.reshape(teams, times, width), "blk", 0, 0)
    data = [own] + [swap(part, 0, 1) for part in jnp.split(own, 2, axis=1)]
    weights += [swap(array, 0, 1) for array in weights]

    mixed, left = pl.pallas_call(
        functools.partial(mix_kernel, teams, replicas, tile_rows),
        out_shape=[
            jax.ShapeDtypeStruct((teams, 2 * times, width), BF16),
            jax.ShapeDtypeStruct((teams, chips * tile_rows, 4 * times), BF16),
        ],
        in_specs=[SMEM, SMEM] + [VMEM] * 3 + [ANY] * (2 * planes),
        out_specs=[VMEM, VMEM],
        scratch_shapes=[
            pltpu.VMEM((teams, 3, width, width), BF16),
            pltpu.VMEM((width, 2 * times), BF16),
            pltpu.SemaphoreType.DMA((2 * planes * count,)),
        ],
        compiler_params=large,
        name="mix",
    )(place, pattern, *data, *weights)

    tile = (slots, tile_rows, width)

    def shape(lead, dtype):
        return jax.ShapeDtypeStruct(tuple(lead) + tile, dtype)

    def products(wanted, shapes):
        return pl.pallas_call(
            functools.partial(product_kernel, teams, chips, wanted),
            out_shape=shapes,
            in_specs=[SMEM, SMEM] + [VMEM] * 5,
            out_specs=[VMEM] * len(shapes),
            compiler_params=small,
            name="products",
        )(place, pattern, *data, mixed, left)

    def add(groups, shapes, *arrays):
        return pl.pallas_call(
            functools.partial(add_kernel, groups),
            out_shape=shapes,
            in_specs=[VMEM] * len(arrays),
            out_specs=[VMEM] * len(shapes),
            compiler_params=small,
            name="add",
        )(*arrays)

    half = count // 2
    outer, inner = range(half, count), range(half)
    chip_range = range(chips)
    (outer_sent,) = products(
        {(mz, 1, my): (0, (my, mz - half)) for mz in outer for my in chip_range}, [shape((chips, half), BF16)]
    )
    outer_sent = swap(outer_sent, 1, 0)
    inner_parts = products(
        {(mz, mx, my): (my, (mx, mz)) for mz in inner for mx in range(LOW) for my in chip_range},
        [shape((LOW, half), BF16 if my else F32) for my in chip_range],
    )
    inner_parts = [swap(array, 0, 2 * my) if my else array for my, array in enumerate(inner_parts)]
    (outer_kept,) = products(
        {(mz, 0, my): (0, (my, mz - half)) for mz in outer for my in chip_range}, [shape((chips, half), F32)]
    )
    outer_parts = add(
        [[(0, my), (1, my)] for my in chip_range],
        [shape((half,), BF16 if my else F32) for my in chip_range],
        outer_kept,
        outer_sent,
    )
    outer_parts = [swap(array, 0, 2 * my) if my else array for my, array in enumerate(outer_parts)]
    inner_parts = add(
        [[(n, mx) for n in chip_range] for mx in range(LOW)],
        [shape((half,), BF16 if mx else F32) for mx in range(LOW)],
        *inner_parts,
    )
    inner_parts = [inner_parts[0], swap(inner_parts[1], 1, 0)]
    outer_sums = add(
        [[(n, mz - half) for n in chip_range] for mz in outer], [shape((), BF16) for _ in outer], *outer_parts
    )
    inner_sums = add(
        [[(n, mz) for n in range(LOW)] for mz in inner], [shape((), BF16 if mz else F32) for mz in inner], *inner_parts
    )
    sums = along_line(list(inner_sums) + list(outer_sums))

    scale = 1.0 / (2.0 * signals.shape[0] * replicas)
    return pl.pallas_call(
        functools.partial(update_kernel, teams, scale),
        out_shape=jax.ShapeDtypeStruct(omega.shape, F32),
        in_specs=[SMEM, SMEM, VMEM] + [VMEM] * count,
        out_specs=VMEM,
        compiler_params=small,
        name="update",
    )(place, pattern, omega, *sums)


def solution(mesh):
    return jax.shard_map(
        functools.partial(per_device, mesh.shape["blk"], mesh.shape["rep"]),
        mesh=mesh,
        in_specs=(P("rep", "blk"), P("blk", None, "rep", None), P("blk", None)),
        out_specs=P("blk", None, "rep", None),
        check_vma=False,
    )
```

```python
import functools

import jax
import jax.numpy as jnp
from jax import lax
from jax.experimental import pallas as pl
from jax.experimental.pallas import tpu as pltpu
from jax.sharding import Mesh, PartitionSpec as P

STEP_SIZE = 0.5
PENALTY = 0.1
LOW = 2
AXES = ("line", "low", "chip", "core")
BLK, REP = AXES[:2], AXES[2:]
F32 = jnp.float32
BF16 = jnp.bfloat16

VMEM = pl.BlockSpec(memory_space=pltpu.VMEM)
ANY = pl.BlockSpec(memory_space=pl.ANY)
SMEM = pl.BlockSpec(memory_space=pltpu.SMEM)


def stored_offsets(pattern_ref, team, teams):
    drawn = [lax.rem(pattern_ref[0, k] - team + teams, teams) for k in range(1, 5)]
    a = functools.reduce(jnp.minimum, drawn)
    b = functools.reduce(jnp.minimum, [jnp.where(d == a, teams, d) for d in drawn])
    offsets = [jnp.int32(0), a, b, teams - b, teams - a]
    slots = [jnp.int32(0)]
    for offset in offsets[1:]:
        slots.append(sum(jnp.where(d == offset, k + 1, 0) for k, d in enumerate(drawn)))
    return offsets, slots


def prepare_kernel(teams, place_ref, pattern_ref, omega_ref, signals_ref, upper_ref, across_ref, sem):
    team = place_ref[0]
    rows = across_ref.shape[0]
    first = pl.multiple_of((lax.rem(team, LOW) ^ 1) * rows, rows)
    copy = pltpu.make_async_copy(signals_ref.at[pl.ds(first, rows)], across_ref, sem)
    copy.start()
    _, slots = stored_offsets(pattern_ref, team, teams)
    for k in range(3):
        upper_ref[k] = omega_ref[0, slots[k]].astype(BF16)
    copy.wait()


def deal_kernel(place_ref, signals_ref, across_ref, out_ref, sems):
    rows = across_ref.shape[0]
    first = pl.multiple_of(lax.rem(place_ref[0], LOW) * rows, rows)
    sources = [signals_ref.at[pl.ds(first, rows)], across_ref]
    copies = [
        pltpu.make_async_copy(source.reshape(out_ref.shape[0], *out_ref.shape[2:]), out_ref.at[:, n], sems.at[n])
        for n, source in enumerate(sources)
    ]
    for copy in copies:
        copy.start()
    for copy in copies:
        copy.wait()


NN = (((1,), (0,)), ((), ()))
NT = (((1,), (1,)), ((), ()))


def gather_kernel(teams, chips, tile_rows, place_ref, *rest):
    weight_refs, omega_ref, sems = rest[:-2], rest[-2], rest[-1]
    planes = LOW * chips
    depth = teams // LOW
    team, replica = place_ref[0], place_ref[1]
    core, chip = lax.rem(replica, 2), lax.div(replica, 2)
    high, low = lax.div(team, LOW), lax.rem(team, LOW)
    copies = []
    for half in range(2):
        for mx in range(LOW):
            for my in range(chips):
                plane = mx * chips + my
                row = (2 * (chip ^ my) + (core ^ half)) * tile_rows
                for mz in range(depth):
                    i = (high ^ mz) * LOW + (low ^ mx)
                    target = omega_ref.at[i, :, pl.ds(pl.multiple_of(row, tile_rows), tile_rows)]
                    copies.append(
                        pltpu.make_async_copy(
                            weight_refs[half * planes + plane].at[mz],
                            target,
                            sems.at[(half * planes + plane) * depth + mz],
                        )
                    )
    for copy in copies:
        copy.start()
    for copy in copies:
        copy.wait()


def block(data_ref, low, c):
    return data_ref[lax.div(c, LOW), lax.rem(c, LOW) ^ low]


def mix_kernel(teams, replicas, tile_rows, place_ref, pattern_ref, data_ref, omega_ref, mixed_ref, left_ref, flip_ref):
    chips = replicas // 2
    team, replica = place_ref[0], place_ref[1]
    core, chip = lax.rem(replica, 2), lax.div(replica, 2)
    low = lax.rem(team, LOW)
    offsets, _ = stored_offsets(pattern_ref, team, teams)
    times = mixed_ref.shape[1]

    def mix(i, carry):
        total = None
        for k, offset in enumerate(offsets):
            c = lax.rem(i + offset, teams)
            right, dims = (omega_ref[i, k], NT) if k < 3 else (omega_ref[c, 5 - k], NN)
            term = lax.dot_general(block(data_ref, low, c), right, dims, preferred_element_type=F32)
            total = term if total is None else total + term
        mixed = total.astype(BF16)
        mixed_ref[i] = mixed
        for n, array in enumerate([mixed, block(data_ref, low, i)]):
            flip_ref[n] = array.T
            for m in range(chips):
                row = (2 * (chip ^ m) + core) * tile_rows
                left_ref[i, m * tile_rows : (m + 1) * tile_rows, n * times : (n + 1) * times] = flip_ref[
                    n, pl.ds(pl.multiple_of(row, tile_rows), tile_rows)
                ]
        return carry

    lax.fori_loop(0, teams, mix, 0, unroll=teams <= 8)


def product_kernel(teams, chips, wanted, place_ref, pattern_ref, *rest):
    cores, outs = [rest[:3], rest[3:6]], rest[6:]
    team = place_ref[0]
    high, low = lax.div(team, LOW), lax.rem(team, LOW)
    offsets, _ = stored_offsets(pattern_ref, team, teams)
    tile_rows = cores[0][2].shape[1] // chips
    for mz, mx in sorted({key[:2] for key in wanted}):
        i = (high ^ mz) * LOW + (low ^ mx)
        for k, offset in enumerate(offsets):
            c = lax.rem(i + offset, teams)
            left = jnp.concatenate([left_ref[i] for _, _, left_ref in cores], axis=1)
            right = jnp.concatenate(
                [part for data_ref, mixed_ref, _ in cores for part in (block(data_ref, low, c), mixed_ref[c])], axis=0
            )
            product = lax.dot_general(left, right, NN, preferred_element_type=F32)
            for m in range(chips):
                if (mz, mx, m) in wanted:
                    out, place = wanted[mz, mx, m]
                    outs[out][place + (k,)] = product[m * tile_rows : (m + 1) * tile_rows].astype(outs[out].dtype)


def add_kernel(groups, *refs):
    outs = refs[len(refs) - len(groups) :]
    for out, terms in zip(outs, groups):
        total = None
        for source, index in terms:
            term = (refs[source][...] if index is None else refs[source][index]).astype(F32)
            total = term if total is None else total + term
        out[...] = total.astype(out.dtype)


def update_kernel(teams, scale, place_ref, pattern_ref, omega_ref, *rest):
    parts, out_ref = rest[:-1], rest[-1]
    _, slots = stored_offsets(pattern_ref, place_ref[0], teams)
    rows, width = out_ref.shape[2:]
    first = place_ref[1] * rows
    row_ids = first + lax.broadcasted_iota(jnp.int32, (rows, width), 0)
    diagonal = row_ids == lax.broadcasted_iota(jnp.int32, (rows, width), 1)
    for k in range(5):
        total = parts[0][k].astype(F32)
        for part in parts[1:]:
            total = total + part[k].astype(F32)
        current = omega_ref[0, slots[k]]
        gradient = total * scale
        if k == 0:
            gradient = gradient - jnp.where(diagonal, 1.0 / current, 0.0)
        value = current - STEP_SIZE * gradient
        bound = STEP_SIZE * PENALTY
        shrunk = jnp.where(value > bound, value - bound, jnp.where(value < -bound, value + bound, 0.0))
        if k == 0:
            shrunk = jnp.where(diagonal, value, shrunk)
        out_ref[0, slots[k]] = shrunk


def per_device(teams, replicas, signals, omega, pattern):
    chips = replicas // 2
    slots, tile_rows, width = omega.shape[1:]
    times = signals.shape[0] // teams
    place = jnp.stack([lax.axis_index(BLK), lax.axis_index(REP)]).astype(jnp.int32)

    def swap(array, blk_mask, rep_mask):
        route = [
            (b * replicas + r, (b ^ blk_mask) * replicas + (r ^ rep_mask))
            for b in range(teams)
            for r in range(replicas)
        ]
        return lax.ppermute(array, AXES, route)

    planes = LOW * chips
    count = teams // LOW
    planes = LOW * chips
    count = teams // LOW
    small = pltpu.CompilerParams(vmem_limit_bytes=(6 if teams <= 8 else 24) * 2**20)

    def across_plane(arrays):
        return [
            swap(arrays[mx * chips + my], mx, 2 * my) if mx + my else arrays[0]
            for mx in range(LOW)
            for my in range(chips)
        ]

    def along_line(arrays):
        return [swap(array, m * LOW, 0) if m else array for m, array in enumerate(arrays)]

    upper, across = pl.pallas_call(
        functools.partial(prepare_kernel, teams),
        out_shape=[
            jax.ShapeDtypeStruct((3, tile_rows, width), BF16),
            jax.ShapeDtypeStruct((count * times, width), BF16),
        ],
        in_specs=[SMEM, SMEM, VMEM, ANY],
        out_specs=[VMEM, VMEM],
        scratch_shapes=[pltpu.SemaphoreType.DMA],
        compiler_params=small,
        name="prepare",
    )(place, pattern, omega, signals)

    line = jnp.stack(along_line([upper] * count))
    across = swap(across, 1, 0)
    line, across = lax.optimization_barrier((line, across))
    weights = across_plane([line] * planes)
    dealt = pl.pallas_call(
        deal_kernel,
        out_shape=jax.ShapeDtypeStruct((count, LOW, times, width), BF16),
        in_specs=[SMEM, ANY, VMEM],
        out_specs=VMEM,
        scratch_shapes=[pltpu.SemaphoreType.DMA((2,))],
        compiler_params=small,
        name="deal",
    )(place, signals, across)
    own = lax.all_to_all(dealt, "line", 0, 0)
    weights += [swap(array, 0, 1) for array in weights]
    tiles = pl.pallas_call(
        functools.partial(gather_kernel, teams, chips, tile_rows),
        out_shape=jax.ShapeDtypeStruct((teams, 3, width, width), BF16),
        in_specs=[SMEM] + [ANY] * (2 * planes),
        out_specs=VMEM,
        scratch_shapes=[pltpu.SemaphoreType.DMA((2 * planes * count,))],
        compiler_params=small,
        name="gather",
    )(place, *weights)
    own, tiles = lax.optimization_barrier((own, tiles))

    def mix(data):
        return pl.pallas_call(
            functools.partial(mix_kernel, teams, replicas, tile_rows),
            out_shape=[
                jax.ShapeDtypeStruct((teams, times, width), BF16),
                jax.ShapeDtypeStruct((teams, chips * tile_rows, 2 * times), BF16),
            ],
            in_specs=[SMEM, SMEM, VMEM, VMEM],
            out_specs=[VMEM, VMEM],
            scratch_shapes=[pltpu.VMEM((2, width, times), BF16)],
            compiler_params=small,
            name="mix",
        )(place, pattern, data, tiles)

    other = swap(own, 0, 1)
    cores = [own, *mix(own), other, *mix(other)]

    tile = (slots, tile_rows, width)

    def shape(lead, dtype):
        return jax.ShapeDtypeStruct(tuple(lead) + tile, dtype)

    def products(wanted, shapes):
        return pl.pallas_call(
            functools.partial(product_kernel, teams, chips, wanted),
            out_shape=shapes,
            in_specs=[SMEM, SMEM] + [VMEM] * 6,
            out_specs=[VMEM] * len(shapes),
            compiler_params=small,
            name="products",
        )(place, pattern, *cores)

    def add(groups, shapes, *arrays):
        return pl.pallas_call(
            functools.partial(add_kernel, groups),
            out_shape=shapes,
            in_specs=[VMEM] * len(arrays),
            out_specs=[VMEM] * len(shapes),
            compiler_params=small,
            name="add",
        )(*arrays)

    half = count // 2
    outer, inner = range(half, count), range(half)
    chip_range = range(chips)
    (outer_sent,) = products(
        {(mz, 1, my): (0, (my, mz - half)) for mz in outer for my in chip_range}, [shape((chips, half), BF16)]
    )
    outer_sent = swap(outer_sent, 1, 0)
    inner_parts = products(
        {(mz, mx, my): (my, (mx, mz)) for mz in inner for mx in range(LOW) for my in chip_range},
        [shape((LOW, half), BF16 if my else F32) for my in chip_range],
    )
    inner_parts = [swap(array, 0, 2 * my) if my else array for my, array in enumerate(inner_parts)]
    (outer_kept,) = products(
        {(mz, 0, my): (0, (my, mz - half)) for mz in outer for my in chip_range}, [shape((chips, half), F32)]
    )
    outer_parts = add(
        [[(0, my), (1, my)] for my in chip_range],
        [shape((half,), BF16 if my else F32) for my in chip_range],
        outer_kept,
        outer_sent,
    )
    outer_parts = [swap(array, 0, 2 * my) if my else array for my, array in enumerate(outer_parts)]
    inner_parts = add(
        [[(n, mx) for n in chip_range] for mx in range(LOW)],
        [shape((half,), BF16 if mx else F32) for mx in range(LOW)],
        *inner_parts,
    )
    inner_parts = [inner_parts[0], swap(inner_parts[1], 1, 0)]
    outer_sums = add(
        [[(n, mz - half) for n in chip_range] for mz in outer], [shape((), BF16) for _ in outer], *outer_parts
    )
    inner_sums = add(
        [[(n, mz) for n in range(LOW)] for mz in inner], [shape((), BF16 if mz else F32) for mz in inner], *inner_parts
    )
    sums = along_line(list(inner_sums) + list(outer_sums))

    scale = 1.0 / (2.0 * signals.shape[0] * replicas)
    return pl.pallas_call(
        functools.partial(update_kernel, teams, scale),
        out_shape=jax.ShapeDtypeStruct(omega.shape, F32),
        in_specs=[SMEM, SMEM, VMEM] + [VMEM] * count,
        out_specs=VMEM,
        compiler_params=small,
        name="update",
    )(place, pattern, omega, *sums)


def solution(mesh):
    teams, replicas = mesh.shape["blk"], mesh.shape["rep"]
    fine = Mesh(mesh.devices.reshape(teams // LOW, LOW, replicas // 2, 2), AXES)
    return jax.shard_map(
        functools.partial(per_device, teams, replicas),
        mesh=fine,
        in_specs=(P(REP, BLK), P(BLK, None, REP, None), P(BLK, None)),
        out_specs=P(BLK, None, REP, None),
        check_vma=False,
    )
```

```python
import functools

import jax
import jax.numpy as jnp
from jax import lax
from jax.experimental import pallas as pl
from jax.experimental.pallas import tpu as pltpu
from jax.sharding import Mesh, PartitionSpec as P

STEP_SIZE = 0.5
PENALTY = 0.1
LOW = 2
AXES = ("line", "low", "chip", "core")
BLK, REP = AXES[:2], AXES[2:]
F32 = jnp.float32
BF16 = jnp.bfloat16

VMEM = pl.BlockSpec(memory_space=pltpu.VMEM)
ANY = pl.BlockSpec(memory_space=pl.ANY)
HBM = pl.BlockSpec(memory_space=pltpu.HBM)
SMEM = pl.BlockSpec(memory_space=pltpu.SMEM)


def stored_offsets(place_ref, teams):
    drawn = [lax.rem(place_ref[2 + k] - place_ref[0] + teams, teams) for k in range(1, 5)]
    a = functools.reduce(jnp.minimum, drawn)
    b = functools.reduce(jnp.minimum, [jnp.where(d == a, teams, d) for d in drawn])
    offsets = [jnp.int32(0), a, b, teams - b, teams - a]
    slots = [jnp.int32(0)]
    for offset in offsets[1:]:
        slots.append(sum(jnp.where(d == offset, k + 1, 0) for k, d in enumerate(drawn)))
    return offsets, slots


def prepare_kernel(teams, place_ref, omega_ref, out_ref):
    _, slots = stored_offsets(place_ref, teams)
    for k in range(3):
        out_ref[k] = omega_ref[0, slots[k]].astype(BF16)


def deal_kernel(kept_ref, across_ref, out_ref, sems):
    shape = (out_ref.shape[0],) + out_ref.shape[2:]
    copies = [
        pltpu.make_async_copy(source.reshape(shape), out_ref.at[:, n], sems.at[n])
        for n, source in enumerate([kept_ref, across_ref])
    ]
    for copy in copies:
        copy.start()
    for copy in copies:
        copy.wait()


NN = (((1,), (0,)), ((), ()))
NT = (((1,), (1,)), ((), ()))


def gather_kernel(teams, chips, tile_rows, place_ref, *rest):
    weight_refs, omega_ref, sems = rest[:-2], rest[-2], rest[-1]
    planes = LOW * chips
    depth = teams // LOW
    team, replica = place_ref[0], place_ref[1]
    core, chip = lax.rem(replica, 2), lax.div(replica, 2)
    high, low = lax.div(team, LOW), lax.rem(team, LOW)
    copies = []
    for half in range(2):
        for mx in range(LOW):
            for my in range(chips):
                plane = mx * chips + my
                row = (2 * (chip ^ my) + (core ^ half)) * tile_rows
                for mz in range(depth):
                    i = (high ^ mz) * LOW + (low ^ mx)
                    target = omega_ref.at[i, :, pl.ds(pl.multiple_of(row, tile_rows), tile_rows)]
                    copies.append(
                        pltpu.make_async_copy(
                            weight_refs[half * planes + plane].at[mz],
                            target,
                            sems.at[(half * planes + plane) * depth + mz],
                        )
                    )
    for copy in copies:
        copy.start()
    for copy in copies:
        copy.wait()


def block(data_ref, low, c):
    return data_ref[lax.div(c, LOW), lax.rem(c, LOW) ^ low]


def mix_kernel(teams, replicas, tile_rows, place_ref, data_ref, omega_ref, right_ref, left_ref, flip_ref):
    chips = replicas // 2
    team, replica = place_ref[0], place_ref[1]
    core, chip = lax.rem(replica, 2), lax.div(replica, 2)
    low = lax.rem(team, LOW)
    offsets, _ = stored_offsets(place_ref, teams)
    times = right_ref.shape[1] // 2

    def mix(i, carry):
        total = None
        for k, offset in enumerate(offsets):
            c = lax.rem(i + offset, teams)
            right, dims = (omega_ref[i, k], NT) if k < 3 else (omega_ref[c, 5 - k], NN)
            term = lax.dot_general(block(data_ref, low, c), right, dims, preferred_element_type=F32)
            total = term if total is None else total + term
        mixed = total.astype(BF16)
        data = block(data_ref, low, i)
        right_ref[i, :times] = data
        right_ref[i, times:] = mixed
        for n, array in enumerate([mixed, data]):
            flip_ref[n] = array.T
            for m in range(chips):
                row = (2 * (chip ^ m) + core) * tile_rows
                left_ref[i, m * tile_rows : (m + 1) * tile_rows, n * times : (n + 1) * times] = flip_ref[
                    n, pl.ds(pl.multiple_of(row, tile_rows), tile_rows)
                ]
        return carry

    lax.fori_loop(0, teams, mix, 0, unroll=teams <= 8)


def product_kernel(teams, chips, wanted, place_ref, *rest):
    rights, lefts, outs = rest[0:4:2], rest[1:4:2], rest[4:]
    team = place_ref[0]
    high, low = lax.div(team, LOW), lax.rem(team, LOW)
    offsets, _ = stored_offsets(place_ref, teams)
    tile_rows = lefts[0].shape[1] // chips
    for mz, mx in sorted({key[:2] for key in wanted}):
        i = (high ^ mz) * LOW + (low ^ mx)
        for k, offset in enumerate(offsets):
            c = lax.rem(i + offset, teams)
            left = jnp.concatenate([ref[i] for ref in lefts], axis=1)
            right = jnp.concatenate([ref[c] for ref in rights], axis=0)
            product = lax.dot_general(left, right, NN, preferred_element_type=F32)
            for m in range(chips):
                if (mz, mx, m) in wanted:
                    out, place = wanted[mz, mx, m]
                    outs[out][place + (k,)] = product[m * tile_rows : (m + 1) * tile_rows].astype(outs[out].dtype)


def add_kernel(groups, *refs):
    outs = refs[len(refs) - len(groups) :]
    for out, terms in zip(outs, groups):
        total = None
        for source, index in terms:
            term = (refs[source][...] if index is None else refs[source][index]).astype(F32)
            total = term if total is None else total + term
        out[...] = total.astype(out.dtype)


def update_kernel(teams, scale, place_ref, omega_ref, *rest):
    parts, out_ref = rest[:-1], rest[-1]
    _, slots = stored_offsets(place_ref, teams)
    rows, width = out_ref.shape[2:]
    first = place_ref[1] * rows
    row_ids = first + lax.broadcasted_iota(jnp.int32, (rows, width), 0)
    diagonal = row_ids == lax.broadcasted_iota(jnp.int32, (rows, width), 1)
    for k in range(5):
        total = parts[0][k].astype(F32)
        for part in parts[1:]:
            total = total + part[k].astype(F32)
        current = omega_ref[0, slots[k]]
        gradient = total * scale
        if k == 0:
            gradient = gradient - jnp.where(diagonal, 1.0 / current, 0.0)
        value = current - STEP_SIZE * gradient
        bound = STEP_SIZE * PENALTY
        shrunk = jnp.where(value > bound, value - bound, jnp.where(value < -bound, value + bound, 0.0))
        if k == 0:
            shrunk = jnp.where(diagonal, value, shrunk)
        out_ref[0, slots[k]] = shrunk


def per_device(teams, replicas, signals, omega, pattern):
    chips = replicas // 2
    slots, tile_rows, width = omega.shape[1:]
    times = signals.shape[0] // teams
    place = jnp.concatenate([jnp.stack([lax.axis_index(BLK), lax.axis_index(REP)]).astype(jnp.int32), pattern[0]])

    def swap(array, blk_mask, rep_mask):
        route = [
            (b * replicas + r, (b ^ blk_mask) * replicas + (r ^ rep_mask))
            for b in range(teams)
            for r in range(replicas)
        ]
        return lax.ppermute(array, AXES, route)

    planes = LOW * chips
    count = teams // LOW
    planes = LOW * chips
    count = teams // LOW
    small = pltpu.CompilerParams(vmem_limit_bytes=(6 if teams <= 8 else 24) * 2**20)

    def across_plane(arrays):
        return [
            swap(arrays[mx * chips + my], mx, 2 * my) if mx + my else arrays[0]
            for mx in range(LOW)
            for my in range(chips)
        ]

    def along_line(arrays):
        return [swap(array, m * LOW, 0) if m else array for m, array in enumerate(arrays)]

    low = lax.axis_index("low")
    across = swap(lax.dynamic_slice_in_dim(signals, (low ^ 1) * count * times, count * times, 0), 1, 0)
    upper = pl.pallas_call(
        functools.partial(prepare_kernel, teams),
        out_shape=jax.ShapeDtypeStruct((3, tile_rows, width), BF16),
        in_specs=[SMEM, VMEM],
        out_specs=VMEM,
        compiler_params=small,
        name="prepare",
    )(place, omega)
    line = jnp.stack(along_line([upper] * count))
    line, across, signals = lax.optimization_barrier((line, across, signals))
    kept = lax.dynamic_slice_in_dim(signals, low * count * times, count * times, 0)
    weights = across_plane([line] * planes)
    dealt = pl.pallas_call(
        deal_kernel,
        out_shape=jax.ShapeDtypeStruct((count, LOW, times, width), BF16),
        in_specs=[VMEM, VMEM],
        out_specs=HBM,
        scratch_shapes=[pltpu.SemaphoreType.DMA((2,))],
        compiler_params=small,
        name="deal",
    )(kept, across)
    own = lax.all_to_all(dealt, "line", 0, 0)
    weights += [swap(array, 0, 1) for array in weights]
    tiles = pl.pallas_call(
        functools.partial(gather_kernel, teams, chips, tile_rows),
        out_shape=jax.ShapeDtypeStruct((teams, 3, width, width), BF16),
        in_specs=[SMEM] + [ANY] * (2 * planes),
        out_specs=VMEM,
        scratch_shapes=[pltpu.SemaphoreType.DMA((2 * planes * count,))],
        compiler_params=small,
        name="gather",
    )(place, *weights)
    own, tiles = lax.optimization_barrier((own, tiles))

    def mix(data):
        return pl.pallas_call(
            functools.partial(mix_kernel, teams, replicas, tile_rows),
            out_shape=[
                jax.ShapeDtypeStruct((teams, 2 * times, width), BF16),
                jax.ShapeDtypeStruct((teams, chips * tile_rows, 2 * times), BF16),
            ],
            in_specs=[SMEM, VMEM, VMEM],
            out_specs=[VMEM, VMEM],
            scratch_shapes=[pltpu.VMEM((2, width, times), BF16)],
            compiler_params=small,
            name="mix",
        )(place, data, tiles)

    other = swap(own, 0, 1)
    cores = [*mix(own), *mix(other)]

    tile = (slots, tile_rows, width)

    def shape(lead, dtype):
        return jax.ShapeDtypeStruct(tuple(lead) + tile, dtype)

    def products(wanted, shapes):
        return pl.pallas_call(
            functools.partial(product_kernel, teams, chips, wanted),
            out_shape=shapes,
            in_specs=[SMEM] + [VMEM] * 4,
            out_specs=[VMEM] * len(shapes),
            compiler_params=small,
            name="products",
        )(place, *cores)

    def add(groups, shapes, *arrays):
        return pl.pallas_call(
            functools.partial(add_kernel, groups),
            out_shape=shapes,
            in_specs=[VMEM] * len(arrays),
            out_specs=[VMEM] * len(shapes),
            compiler_params=small,
            name="add",
        )(*arrays)

    half = count // 2
    outer, inner = range(half, count), range(half)
    chip_range = range(chips)
    (outer_sent,) = products(
        {(mz, 1, my): (0, (my, mz - half)) for mz in outer for my in chip_range}, [shape((chips, half), BF16)]
    )
    outer_sent = swap(outer_sent, 1, 0)
    inner_parts = products(
        {(mz, mx, my): (my, (mx, mz)) for mz in inner for mx in range(LOW) for my in chip_range},
        [shape((LOW, half), BF16 if my else F32) for my in chip_range],
    )
    inner_parts = [swap(array, 0, 2 * my) if my else array for my, array in enumerate(inner_parts)]
    (outer_kept,) = products(
        {(mz, 0, my): (0, (my, mz - half)) for mz in outer for my in chip_range}, [shape((chips, half), F32)]
    )
    outer_parts = add(
        [[(0, my), (1, my)] for my in chip_range],
        [shape((half,), BF16 if my else F32) for my in chip_range],
        outer_kept,
        outer_sent,
    )
    outer_parts = [swap(array, 0, 2 * my) if my else array for my, array in enumerate(outer_parts)]
    inner_parts = add(
        [[(n, mx) for n in chip_range] for mx in range(LOW)],
        [shape((half,), BF16 if mx else F32) for mx in range(LOW)],
        *inner_parts,
    )
    inner_parts = [inner_parts[0], swap(inner_parts[1], 1, 0)]
    outer_sums = add(
        [[(n, mz - half) for n in chip_range] for mz in outer], [shape((), BF16) for _ in outer], *outer_parts
    )
    inner_sums = add(
        [[(n, mz) for n in range(LOW)] for mz in inner], [shape((), BF16 if mz else F32) for mz in inner], *inner_parts
    )
    sums = along_line(list(inner_sums) + list(outer_sums))

    scale = 1.0 / (2.0 * teams * times * replicas)
    return pl.pallas_call(
        functools.partial(update_kernel, teams, scale),
        out_shape=jax.ShapeDtypeStruct(omega.shape, F32),
        in_specs=[SMEM, VMEM] + [VMEM] * count,
        out_specs=VMEM,
        compiler_params=small,
        name="update",
    )(place, omega, *sums)


def solution(mesh):
    teams, replicas = mesh.shape["blk"], mesh.shape["rep"]
    fine = Mesh(mesh.devices.reshape(teams // LOW, LOW, replicas // 2, 2), AXES)
    return jax.shard_map(
        functools.partial(per_device, teams, replicas),
        mesh=fine,
        in_specs=(P(REP, BLK), P(BLK, None, REP, None), P(BLK, None)),
        out_specs=P(BLK, None, REP, None),
        check_vma=False,
    )
```

```python
import functools

import jax
import jax.numpy as jnp
from jax import lax
from jax.experimental import pallas as pl
from jax.experimental.pallas import tpu as pltpu
from jax.sharding import Mesh, PartitionSpec as P

STEP_SIZE = 0.5
PENALTY = 0.1
LOW = 2
AXES = ("line", "low", "chip", "core")
BLK, REP = AXES[:2], AXES[2:]
F32 = jnp.float32
BF16 = jnp.bfloat16

VMEM = pl.BlockSpec(memory_space=pltpu.VMEM)
ANY = pl.BlockSpec(memory_space=pl.ANY)
HBM = pl.BlockSpec(memory_space=pltpu.HBM)
SMEM = pl.BlockSpec(memory_space=pltpu.SMEM)


def stored_offsets(place_ref, teams):
    drawn = [lax.rem(place_ref[2 + k] - place_ref[0] + teams, teams) for k in range(1, 5)]
    a = functools.reduce(jnp.minimum, drawn)
    b = functools.reduce(jnp.minimum, [jnp.where(d == a, teams, d) for d in drawn])
    offsets = [jnp.int32(0), a, b, teams - b, teams - a]
    slots = [jnp.int32(0)]
    for offset in offsets[1:]:
        slots.append(sum(jnp.where(d == offset, k + 1, 0) for k, d in enumerate(drawn)))
    return offsets, slots


def prepare_kernel(teams, place_ref, omega_ref, out_ref):
    _, slots = stored_offsets(place_ref, teams)
    for k in range(3):
        out_ref[k] = omega_ref[0, slots[k]].astype(BF16)


def deal_kernel(kept_ref, across_ref, out_ref, sems):
    shape = (out_ref.shape[0],) + out_ref.shape[2:]
    copies = [
        pltpu.make_async_copy(source.reshape(shape), out_ref.at[:, n], sems.at[n])
        for n, source in enumerate([kept_ref, across_ref])
    ]
    for copy in copies:
        copy.start()
    for copy in copies:
        copy.wait()


NN = (((1,), (0,)), ((), ()))
NT = (((1,), (1,)), ((), ()))


def gather_kernel(teams, chips, tile_rows, place_ref, *rest):
    weight_refs, omega_ref, sems = rest[:-2], rest[-2], rest[-1]
    planes = LOW * chips
    depth = teams // LOW
    team, replica = place_ref[0], place_ref[1]
    core, chip = lax.rem(replica, 2), lax.div(replica, 2)
    high, low = lax.div(team, LOW), lax.rem(team, LOW)
    copies = []
    for half in range(2):
        for mx in range(LOW):
            for my in range(chips):
                plane = mx * chips + my
                row = (2 * (chip ^ my) + (core ^ half)) * tile_rows
                for mz in range(depth):
                    i = (high ^ mz) * LOW + (low ^ mx)
                    target = omega_ref.at[i, :, pl.ds(pl.multiple_of(row, tile_rows), tile_rows)]
                    copies.append(
                        pltpu.make_async_copy(
                            weight_refs[half * planes + plane].at[mz],
                            target,
                            sems.at[(half * planes + plane) * depth + mz],
                        )
                    )
    for copy in copies:
        copy.start()
    for copy in copies:
        copy.wait()


def block(data_ref, low, c):
    return data_ref[lax.div(c, LOW), lax.rem(c, LOW) ^ low]


def mix_kernel(teams, replicas, tile_rows, place_ref, data_ref, omega_ref, right_ref, left_ref, flip_ref):
    chips = replicas // 2
    team, replica = place_ref[0], place_ref[1]
    core, chip = lax.rem(replica, 2), lax.div(replica, 2)
    low = lax.rem(team, LOW)
    offsets, _ = stored_offsets(place_ref, teams)
    times = right_ref.shape[1] // 2

    def mix(i, carry):
        total = None
        for k, offset in enumerate(offsets):
            c = lax.rem(i + offset, teams)
            right, dims = (omega_ref[i, k], NT) if k < 3 else (omega_ref[c, 5 - k], NN)
            term = lax.dot_general(block(data_ref, low, c), right, dims, preferred_element_type=F32)
            total = term if total is None else total + term
        mixed = total.astype(BF16)
        data = block(data_ref, low, i)
        right_ref[i, :times] = data
        right_ref[i, times:] = mixed
        for n, array in enumerate([mixed, data]):
            flip_ref[n] = array.T
            for m in range(chips):
                row = (2 * (chip ^ m) + core) * tile_rows
                left_ref[i, m * tile_rows : (m + 1) * tile_rows, n * times : (n + 1) * times] = flip_ref[
                    n, pl.ds(pl.multiple_of(row, tile_rows), tile_rows)
                ]
        return carry

    lax.fori_loop(0, teams, mix, 0, unroll=teams <= 8)


def product_kernel(teams, chips, wanted, place_ref, *rest):
    rights, lefts, outs = rest[0:4:2], rest[1:4:2], rest[4:]
    team = place_ref[0]
    high, low = lax.div(team, LOW), lax.rem(team, LOW)
    offsets, _ = stored_offsets(place_ref, teams)
    tile_rows = lefts[0].shape[1] // chips
    for mz, mx in sorted({key[:2] for key in wanted}):
        i = (high ^ mz) * LOW + (low ^ mx)
        for k, offset in enumerate(offsets):
            c = lax.rem(i + offset, teams)
            left = jnp.concatenate([ref[i] for ref in lefts], axis=1)
            right = jnp.concatenate([ref[c] for ref in rights], axis=0)
            product = lax.dot_general(left, right, NN, preferred_element_type=F32)
            for m in range(chips):
                if (mz, mx, m) in wanted:
                    out, place = wanted[mz, mx, m]
                    outs[out][place + (k,)] = product[m * tile_rows : (m + 1) * tile_rows].astype(outs[out].dtype)


def add_kernel(groups, *refs):
    outs = refs[len(refs) - len(groups) :]
    for out, terms in zip(outs, groups):
        total = None
        for source, index in terms:
            term = (refs[source][...] if index is None else refs[source][index]).astype(F32)
            total = term if total is None else total + term
        out[...] = total.astype(out.dtype)


def update_kernel(teams, scale, place_ref, omega_ref, *rest):
    parts, out_ref = rest[:-1], rest[-1]
    _, slots = stored_offsets(place_ref, teams)
    rows, width = out_ref.shape[2:]
    first = place_ref[1] * rows
    row_ids = first + lax.broadcasted_iota(jnp.int32, (rows, width), 0)
    diagonal = row_ids == lax.broadcasted_iota(jnp.int32, (rows, width), 1)
    for k in range(5):
        total = parts[0][k].astype(F32)
        for part in parts[1:]:
            total = total + part[k].astype(F32)
        current = omega_ref[0, slots[k]]
        gradient = total * scale
        if k == 0:
            gradient = gradient - jnp.where(diagonal, 1.0 / current, 0.0)
        value = current - STEP_SIZE * gradient
        bound = STEP_SIZE * PENALTY
        shrunk = jnp.where(value > bound, value - bound, jnp.where(value < -bound, value + bound, 0.0))
        if k == 0:
            shrunk = jnp.where(diagonal, value, shrunk)
        out_ref[0, slots[k]] = shrunk


def per_device(teams, replicas, signals, omega, pattern):
    chips = replicas // 2
    slots, tile_rows, width = omega.shape[1:]
    times = signals.shape[0] // teams
    place = jnp.concatenate([jnp.stack([lax.axis_index(BLK), lax.axis_index(REP)]).astype(jnp.int32), pattern[0]])

    def swap(array, blk_mask, rep_mask):
        route = [
            (b * replicas + r, (b ^ blk_mask) * replicas + (r ^ rep_mask))
            for b in range(teams)
            for r in range(replicas)
        ]
        return lax.ppermute(array, AXES, route)

    planes = LOW * chips
    count = teams // LOW
    planes = LOW * chips
    count = teams // LOW
    small = pltpu.CompilerParams(vmem_limit_bytes=(4 if teams <= 8 else 16) * 2**20)
    tiny = pltpu.CompilerParams(vmem_limit_bytes=2 * 2**20)

    def across_plane(arrays):
        return [
            swap(arrays[mx * chips + my], mx, 2 * my) if mx + my else arrays[0]
            for mx in range(LOW)
            for my in range(chips)
        ]

    def along_line(arrays):
        return [swap(array, m * LOW, 0) if m else array for m, array in enumerate(arrays)]

    low = lax.axis_index("low")
    across = swap(lax.dynamic_slice_in_dim(signals, (low ^ 1) * count * times, count * times, 0), 1, 0)
    upper = pl.pallas_call(
        functools.partial(prepare_kernel, teams),
        out_shape=jax.ShapeDtypeStruct((3, tile_rows, width), BF16),
        in_specs=[SMEM, VMEM],
        out_specs=VMEM,
        compiler_params=tiny,
        name="prepare",
    )(place, omega)
    line = jnp.stack(along_line([upper] * count))
    line, across, signals = lax.optimization_barrier((line, across, signals))
    kept = lax.dynamic_slice_in_dim(signals, low * count * times, count * times, 0)
    weights = across_plane([line] * planes)
    dealt = pl.pallas_call(
        deal_kernel,
        out_shape=jax.ShapeDtypeStruct((count, LOW, times, width), BF16),
        in_specs=[VMEM, VMEM],
        out_specs=HBM,
        scratch_shapes=[pltpu.SemaphoreType.DMA((2,))],
        compiler_params=tiny,
        name="deal",
    )(kept, across)
    own = lax.all_to_all(dealt, "line", 0, 0)
    weights += [swap(array, 0, 1) for array in weights]
    tiles = pl.pallas_call(
        functools.partial(gather_kernel, teams, chips, tile_rows),
        out_shape=jax.ShapeDtypeStruct((teams, 3, width, width), BF16),
        in_specs=[SMEM] + [ANY] * (2 * planes),
        out_specs=VMEM,
        scratch_shapes=[pltpu.SemaphoreType.DMA((2 * planes * count,))],
        compiler_params=tiny,
        name="gather",
    )(place, *weights)
    own, tiles = lax.optimization_barrier((own, tiles))

    def mix(data):
        return pl.pallas_call(
            functools.partial(mix_kernel, teams, replicas, tile_rows),
            out_shape=[
                jax.ShapeDtypeStruct((teams, 2 * times, width), BF16),
                jax.ShapeDtypeStruct((teams, chips * tile_rows, 2 * times), BF16),
            ],
            in_specs=[SMEM, VMEM, VMEM],
            out_specs=[VMEM, VMEM],
            scratch_shapes=[pltpu.VMEM((2, width, times), BF16)],
            compiler_params=small,
            name="mix",
        )(place, data, tiles)

    other = swap(own, 0, 1)
    cores = [*mix(own), *mix(other)]

    tile = (slots, tile_rows, width)

    def shape(lead, dtype):
        return jax.ShapeDtypeStruct(tuple(lead) + tile, dtype)

    def products(wanted, shapes):
        return pl.pallas_call(
            functools.partial(product_kernel, teams, chips, wanted),
            out_shape=shapes,
            in_specs=[SMEM] + [VMEM] * 4,
            out_specs=[VMEM] * len(shapes),
            compiler_params=small,
            name="products",
        )(place, *cores)

    def add(groups, shapes, *arrays):
        return pl.pallas_call(
            functools.partial(add_kernel, groups),
            out_shape=shapes,
            in_specs=[VMEM] * len(arrays),
            out_specs=[VMEM] * len(shapes),
            compiler_params=small,
            name="add",
        )(*arrays)

    chip_range = range(chips)

    def plane_sums(group, x_first):
        size = len(group)
        if x_first:
            (far,) = products(
                {(mz, 1, my): (0, (my, n)) for n, mz in enumerate(group) for my in chip_range},
                [shape((chips, size), BF16)],
            )
            far = swap(far, 1, 0)
            (near,) = products(
                {(mz, 0, my): (0, (my, n)) for n, mz in enumerate(group) for my in chip_range},
                [shape((chips, size), F32)],
            )
            groups = [[(0, my), (1, my)] for my in chip_range]
            parts = add(groups, [shape((size,), BF16 if my else F32) for my in chip_range], near, far)
            parts = [swap(array, 0, 2 * my) if my else array for my, array in enumerate(parts)]
        else:
            parts = products(
                {
                    (mz, mx, my): (my, (mx, n))
                    for n, mz in enumerate(group)
                    for mx in range(LOW)
                    for my in chip_range
                },
                [shape((LOW, size), BF16 if my else F32) for my in chip_range],
            )
            parts = [swap(array, 0, 2 * my) if my else array for my, array in enumerate(parts)]
            groups = [[(m, mx) for m in chip_range] for mx in range(LOW)]
            parts = add(groups, [shape((size,), BF16 if mx else F32) for mx in range(LOW)], *parts)
            parts = [swap(array, mx, 0) if mx else array for mx, array in enumerate(parts)]
        groups = [[(m, n) for m in range(len(parts))] for n in range(size)]
        return add(groups, [shape((), BF16 if mz else F32) for mz in group], *parts)

    quarter = count // 4
    bounds = [range(n * quarter, (n + 1) * quarter) for n in range(4)]
    far_sums = [*plane_sums(bounds[2], True), *plane_sums(bounds[3], False)]
    near_sums = [*plane_sums(bounds[0], True), *plane_sums(bounds[1], False)]
    sums = along_line(near_sums + far_sums)

    scale = 1.0 / (2.0 * teams * times * replicas)
    return pl.pallas_call(
        functools.partial(update_kernel, teams, scale),
        out_shape=jax.ShapeDtypeStruct(omega.shape, F32),
        in_specs=[SMEM, VMEM] + [VMEM] * count,
        out_specs=VMEM,
        compiler_params=small,
        name="update",
    )(place, omega, *sums)


def solution(mesh):
    teams, replicas = mesh.shape["blk"], mesh.shape["rep"]
    fine = Mesh(mesh.devices.reshape(teams // LOW, LOW, replicas // 2, 2), AXES)
    return jax.shard_map(
        functools.partial(per_device, teams, replicas),
        mesh=fine,
        in_specs=(P(REP, BLK), P(BLK, None, REP, None), P(BLK, None)),
        out_specs=P(BLK, None, REP, None),
        check_vma=False,
    )
```

```python
import functools

import jax
import jax.numpy as jnp
from jax import lax
from jax.experimental import pallas as pl
from jax.experimental.pallas import tpu as pltpu
from jax.sharding import Mesh, PartitionSpec as P

STEP_SIZE = 0.5
PENALTY = 0.1
LOW = 2
AXES = ("line", "low", "chip", "core")
BLK, REP = AXES[:2], AXES[2:]
F32 = jnp.float32
BF16 = jnp.bfloat16

VMEM = pl.BlockSpec(memory_space=pltpu.VMEM)
ANY = pl.BlockSpec(memory_space=pl.ANY)
HBM = pl.BlockSpec(memory_space=pltpu.HBM)
SMEM = pl.BlockSpec(memory_space=pltpu.SMEM)


def stored_offsets(place_ref, teams):
    drawn = [lax.rem(place_ref[2 + k] - place_ref[0] + teams, teams) for k in range(1, 5)]
    a = functools.reduce(jnp.minimum, drawn)
    b = functools.reduce(jnp.minimum, [jnp.where(d == a, teams, d) for d in drawn])
    offsets = [jnp.int32(0), a, b, teams - b, teams - a]
    slots = [jnp.int32(0)]
    for offset in offsets[1:]:
        slots.append(sum(jnp.where(d == offset, k + 1, 0) for k, d in enumerate(drawn)))
    return offsets, slots


def prepare_kernel(teams, place_ref, omega_ref, out_ref):
    _, slots = stored_offsets(place_ref, teams)
    for k in range(3):
        out_ref[k] = omega_ref[0, slots[k]].astype(BF16)


def deal_kernel(kept_ref, across_ref, out_ref, sems):
    shape = (out_ref.shape[0],) + out_ref.shape[2:]
    copies = [
        pltpu.make_async_copy(source.reshape(shape), out_ref.at[:, n], sems.at[n])
        for n, source in enumerate([kept_ref, across_ref])
    ]
    for copy in copies:
        copy.start()
    for copy in copies:
        copy.wait()


NN = (((1,), (0,)), ((), ()))
NT = (((1,), (1,)), ((), ()))


def gather_kernel(teams, chips, tile_rows, place_ref, *rest):
    weight_refs, omega_ref, sems = rest[:-2], rest[-2], rest[-1]
    planes = LOW * chips
    depth = teams // LOW
    team, replica = place_ref[0], place_ref[1]
    core, chip = lax.rem(replica, 2), lax.div(replica, 2)
    high, low = lax.div(team, LOW), lax.rem(team, LOW)
    copies = []
    for half in range(2):
        for mx in range(LOW):
            for my in range(chips):
                plane = mx * chips + my
                row = (2 * (chip ^ my) + (core ^ half)) * tile_rows
                for mz in range(depth):
                    i = (high ^ mz) * LOW + (low ^ mx)
                    target = omega_ref.at[i, :, pl.ds(pl.multiple_of(row, tile_rows), tile_rows)]
                    copies.append(
                        pltpu.make_async_copy(
                            weight_refs[half * planes + plane].at[mz],
                            target,
                            sems.at[(half * planes + plane) * depth + mz],
                        )
                    )
    for copy in copies:
        copy.start()
    for copy in copies:
        copy.wait()


def block(data_ref, low, c):
    return data_ref[lax.div(c, LOW), lax.rem(c, LOW) ^ low]


def mix_kernel(teams, replicas, tile_rows, place_ref, data_ref, omega_ref, right_ref, left_ref, flip_ref):
    chips = replicas // 2
    team, replica = place_ref[0], place_ref[1]
    core, chip = lax.rem(replica, 2), lax.div(replica, 2)
    low = lax.rem(team, LOW)
    offsets, _ = stored_offsets(place_ref, teams)
    times = right_ref.shape[1] // 2

    def mix(i, carry):
        total = None
        for k, offset in enumerate(offsets):
            c = lax.rem(i + offset, teams)
            right, dims = (omega_ref[i, k], NT) if k < 3 else (omega_ref[c, 5 - k], NN)
            term = lax.dot_general(block(data_ref, low, c), right, dims, preferred_element_type=F32)
            total = term if total is None else total + term
        mixed = total.astype(BF16)
        data = block(data_ref, low, i)
        right_ref[i, :times] = data
        right_ref[i, times:] = mixed
        for n, array in enumerate([mixed, data]):
            flip_ref[n] = array.T
            for m in range(chips):
                row = (2 * (chip ^ m) + core) * tile_rows
                left_ref[i, m * tile_rows : (m + 1) * tile_rows, n * times : (n + 1) * times] = flip_ref[
                    n, pl.ds(pl.multiple_of(row, tile_rows), tile_rows)
                ]
        return carry

    lax.fori_loop(0, teams, mix, 0, unroll=teams <= 8)


def product_kernel(teams, chips, wanted, place_ref, *rest):
    rights, lefts, outs = rest[0:4:2], rest[1:4:2], rest[4:]
    team = place_ref[0]
    high, low = lax.div(team, LOW), lax.rem(team, LOW)
    offsets, _ = stored_offsets(place_ref, teams)
    tile_rows = lefts[0].shape[1] // chips
    for mz, mx in sorted({key[:2] for key in wanted}):
        i = (high ^ mz) * LOW + (low ^ mx)
        for k, offset in enumerate(offsets):
            c = lax.rem(i + offset, teams)
            left = jnp.concatenate([ref[i] for ref in lefts], axis=1)
            right = jnp.concatenate([ref[c] for ref in rights], axis=0)
            product = lax.dot_general(left, right, NN, preferred_element_type=F32)
            for m in range(chips):
                if (mz, mx, m) in wanted:
                    out, place = wanted[mz, mx, m]
                    outs[out][place + (k,)] = product[m * tile_rows : (m + 1) * tile_rows].astype(outs[out].dtype)


def add_kernel(groups, *refs):
    outs = refs[len(refs) - len(groups) :]
    for out, terms in zip(outs, groups):
        total = None
        for source, index in terms:
            term = (refs[source][...] if index is None else refs[source][index]).astype(F32)
            total = term if total is None else total + term
        out[...] = total.astype(out.dtype)


def update_kernel(teams, scale, place_ref, omega_ref, *rest):
    parts, out_ref = rest[:-1], rest[-1]
    _, slots = stored_offsets(place_ref, teams)
    rows, width = out_ref.shape[2:]
    first = place_ref[1] * rows
    row_ids = first + lax.broadcasted_iota(jnp.int32, (rows, width), 0)
    diagonal = row_ids == lax.broadcasted_iota(jnp.int32, (rows, width), 1)
    for k in range(5):
        total = parts[0][k].astype(F32)
        for part in parts[1:]:
            total = total + part[k].astype(F32)
        current = omega_ref[0, slots[k]]
        gradient = total * scale
        if k == 0:
            gradient = gradient - jnp.where(diagonal, 1.0 / current, 0.0)
        value = current - STEP_SIZE * gradient
        bound = STEP_SIZE * PENALTY
        shrunk = jnp.where(value > bound, value - bound, jnp.where(value < -bound, value + bound, 0.0))
        if k == 0:
            shrunk = jnp.where(diagonal, value, shrunk)
        out_ref[0, slots[k]] = shrunk


def per_device(teams, replicas, signals, omega, pattern):
    chips = replicas // 2
    slots, tile_rows, width = omega.shape[1:]
    times = signals.shape[0] // teams
    place = jnp.concatenate([jnp.stack([lax.axis_index(BLK), lax.axis_index(REP)]).astype(jnp.int32), pattern[0]])

    def swap(array, blk_mask, rep_mask):
        route = [
            (b * replicas + r, (b ^ blk_mask) * replicas + (r ^ rep_mask))
            for b in range(teams)
            for r in range(replicas)
        ]
        return lax.ppermute(array, AXES, route)

    planes = LOW * chips
    count = teams // LOW
    planes = LOW * chips
    count = teams // LOW
    small = pltpu.CompilerParams(vmem_limit_bytes=(4 if teams <= 8 else 16) * 2**20)
    tiny = pltpu.CompilerParams(vmem_limit_bytes=2 * 2**20)

    def across_plane(arrays):
        return [
            swap(arrays[mx * chips + my], mx, 2 * my) if mx + my else arrays[0]
            for mx in range(LOW)
            for my in range(chips)
        ]

    def along_line(arrays):
        return [swap(array, m * LOW, 0) if m else array for m, array in enumerate(arrays)]

    low = lax.axis_index("low")
    across = swap(lax.dynamic_slice_in_dim(signals, (low ^ 1) * count * times, count * times, 0), 1, 0)
    upper = pl.pallas_call(
        functools.partial(prepare_kernel, teams),
        out_shape=jax.ShapeDtypeStruct((3, tile_rows, width), BF16),
        in_specs=[SMEM, VMEM],
        out_specs=VMEM,
        compiler_params=tiny,
        name="prepare",
    )(place, omega)
    line = jnp.stack(along_line([upper] * count))
    line, across, signals = lax.optimization_barrier((line, across, signals))
    kept = lax.dynamic_slice_in_dim(signals, low * count * times, count * times, 0)
    weights = across_plane([line] * planes)
    dealt = pl.pallas_call(
        deal_kernel,
        out_shape=jax.ShapeDtypeStruct((count, LOW, times, width), BF16),
        in_specs=[VMEM, VMEM],
        out_specs=HBM,
        scratch_shapes=[pltpu.SemaphoreType.DMA((2,))],
        compiler_params=tiny,
        name="deal",
    )(kept, across)
    own = lax.all_to_all(dealt, "line", 0, 0)
    weights += [swap(array, 0, 1) for array in weights]
    own, weights = lax.optimization_barrier((own, weights))
    tiles = pl.pallas_call(
        functools.partial(gather_kernel, teams, chips, tile_rows),
        out_shape=jax.ShapeDtypeStruct((teams, 3, width, width), BF16),
        in_specs=[SMEM] + [ANY] * (2 * planes),
        out_specs=VMEM,
        scratch_shapes=[pltpu.SemaphoreType.DMA((2 * planes * count,))],
        compiler_params=tiny,
        name="gather",
    )(place, *weights)

    def mix(data):
        return pl.pallas_call(
            functools.partial(mix_kernel, teams, replicas, tile_rows),
            out_shape=[
                jax.ShapeDtypeStruct((teams, 2 * times, width), BF16),
                jax.ShapeDtypeStruct((teams, chips * tile_rows, 2 * times), BF16),
            ],
            in_specs=[SMEM, VMEM, VMEM],
            out_specs=[VMEM, VMEM],
            scratch_shapes=[pltpu.VMEM((2, width, times), BF16)],
            compiler_params=small,
            name="mix",
        )(place, data, tiles)

    other = swap(own, 0, 1)
    cores = [*mix(own), *mix(other)]

    tile = (slots, tile_rows, width)

    def shape(lead, dtype):
        return jax.ShapeDtypeStruct(tuple(lead) + tile, dtype)

    def products(wanted, shapes):
        return pl.pallas_call(
            functools.partial(product_kernel, teams, chips, wanted),
            out_shape=shapes,
            in_specs=[SMEM] + [VMEM] * 4,
            out_specs=[VMEM] * len(shapes),
            compiler_params=small,
            name="products",
        )(place, *cores)

    def add(groups, shapes, *arrays):
        return pl.pallas_call(
            functools.partial(add_kernel, groups),
            out_shape=shapes,
            in_specs=[VMEM] * len(arrays),
            out_specs=[VMEM] * len(shapes),
            compiler_params=small,
            name="add",
        )(*arrays)

    chip_range = range(chips)

    def first_parts(group, x_first):
        size = len(group)
        if x_first:
            far, near = [
                products(
                    {(mz, mx, my): (0, (my, n)) for n, mz in enumerate(group) for my in chip_range},
                    [shape((chips, size), BF16 if mx else F32)],
                )[0]
                for mx in (1, 0)
            ]
            return [far], near
        kept, *sent = products(
            {(mz, mx, my): (my, (mx, n)) for n, mz in enumerate(group) for mx in range(LOW) for my in chip_range},
            [shape((LOW, size), BF16 if my else F32) for my in chip_range],
        )
        return sent, kept

    def first_hop(x_first, sent):
        return [swap(sent[0], 1, 0)] if x_first else [swap(array, 0, 2 * my) for my, array in enumerate(sent, 1)]

    def second_hop(group, x_first, received, kept):
        size = len(group)
        if x_first:
            groups = [[(0, my), (1, my)] for my in chip_range]
            parts = add(groups, [shape((size,), BF16 if my else F32) for my in chip_range], kept, *received)
            return [swap(array, 0, 2 * my) if my else array for my, array in enumerate(parts)]
        groups = [[(m, mx) for m in chip_range] for mx in range(LOW)]
        parts = add(groups, [shape((size,), BF16 if mx else F32) for mx in range(LOW)], kept, *received)
        return [swap(array, mx, 0) if mx else array for mx, array in enumerate(parts)]

    def sums_of(group, parts):
        groups = [[(m, n) for m in range(len(parts))] for n in range(len(group))]
        return add(groups, [shape((), BF16 if mz else F32) for mz in group], *parts)

    quarter = count // 4
    bounds = [range(n * quarter, (n + 1) * quarter) for n in range(4)]
    x_first = [True, False, True, False]
    firsts = [first_parts(*each) for each in zip(bounds, x_first)]
    received = [first_hop(first, sent) for first, (sent, _) in zip(x_first, firsts)]
    sums = [None] * 4
    for n in (2, 3, 0, 1):
        sums[n] = sums_of(bounds[n], second_hop(bounds[n], x_first[n], received[n], firsts[n][1]))
        if n == 3:
            received[:2], firsts[:2], sums[2:] = lax.optimization_barrier((received[:2], firsts[:2], sums[2:]))
    sums = along_line([total for group in sums for total in group])

    scale = 1.0 / (2.0 * teams * times * replicas)
    return pl.pallas_call(
        functools.partial(update_kernel, teams, scale),
        out_shape=jax.ShapeDtypeStruct(omega.shape, F32),
        in_specs=[SMEM, VMEM] + [VMEM] * count,
        out_specs=VMEM,
        compiler_params=small,
        name="update",
    )(place, omega, *sums)


def solution(mesh):
    teams, replicas = mesh.shape["blk"], mesh.shape["rep"]
    fine = Mesh(mesh.devices.reshape(teams // LOW, LOW, replicas // 2, 2), AXES)
    return jax.shard_map(
        functools.partial(per_device, teams, replicas),
        mesh=fine,
        in_specs=(P(REP, BLK), P(BLK, None, REP, None), P(BLK, None)),
        out_specs=P(BLK, None, REP, None),
        check_vma=False,
    )
```

```python
import functools

import jax
import jax.numpy as jnp
from jax import lax
from jax.experimental import pallas as pl
from jax.experimental.pallas import tpu as pltpu
from jax.sharding import Mesh, PartitionSpec as P

STEP_SIZE = 0.5
PENALTY = 0.1
LOW = 2
AXES = ("line", "low", "chip", "core")
BLK, REP = AXES[:2], AXES[2:]
F32 = jnp.float32
BF16 = jnp.bfloat16

VMEM = pl.BlockSpec(memory_space=pltpu.VMEM)
ANY = pl.BlockSpec(memory_space=pl.ANY)
HBM = pl.BlockSpec(memory_space=pltpu.HBM)
SMEM = pl.BlockSpec(memory_space=pltpu.SMEM)


def stored_offsets(place_ref, teams):
    drawn = [lax.rem(place_ref[2 + k] - place_ref[0] + teams, teams) for k in range(1, 5)]
    a = functools.reduce(jnp.minimum, drawn)
    b = functools.reduce(jnp.minimum, [jnp.where(d == a, teams, d) for d in drawn])
    offsets = [jnp.int32(0), a, b, teams - b, teams - a]
    slots = [jnp.int32(0)]
    for offset in offsets[1:]:
        slots.append(sum(jnp.where(d == offset, k + 1, 0) for k, d in enumerate(drawn)))
    return offsets, slots


def prepare_kernel(teams, place_ref, omega_ref, out_ref):
    _, slots = stored_offsets(place_ref, teams)
    for k in range(3):
        out_ref[k] = omega_ref[0, slots[k]].astype(BF16)


def deal_kernel(kept_ref, across_ref, out_ref, sems):
    shape = (out_ref.shape[0],) + out_ref.shape[2:]
    copies = [
        pltpu.make_async_copy(source.reshape(shape), out_ref.at[:, n], sems.at[n])
        for n, source in enumerate([kept_ref, across_ref])
    ]
    for copy in copies:
        copy.start()
    for copy in copies:
        copy.wait()


NN = (((1,), (0,)), ((), ()))
NT = (((1,), (1,)), ((), ()))


def gather_kernel(teams, chips, tile_rows, place_ref, *rest):
    weight_refs, omega_ref, sems = rest[:-2], rest[-2], rest[-1]
    planes = LOW * chips
    depth = teams // LOW
    team, replica = place_ref[0], place_ref[1]
    core, chip = lax.rem(replica, 2), lax.div(replica, 2)
    high, low = lax.div(team, LOW), lax.rem(team, LOW)
    copies = []
    for half in range(2):
        for mx in range(LOW):
            for my in range(chips):
                plane = mx * chips + my
                row = (2 * (chip ^ my) + (core ^ half)) * tile_rows
                for mz in range(depth):
                    i = (high ^ mz) * LOW + (low ^ mx)
                    target = omega_ref.at[i, :, pl.ds(pl.multiple_of(row, tile_rows), tile_rows)]
                    copies.append(
                        pltpu.make_async_copy(
                            weight_refs[half * planes + plane].at[mz],
                            target,
                            sems.at[(half * planes + plane) * depth + mz],
                        )
                    )
    for copy in copies:
        copy.start()
    for copy in copies:
        copy.wait()


def block(data_ref, low, c):
    return data_ref[lax.div(c, LOW), lax.rem(c, LOW) ^ low]


def mix_kernel(teams, replicas, tile_rows, place_ref, data_ref, omega_ref, right_ref, left_ref, flip_ref):
    chips = replicas // 2
    team, replica = place_ref[0], place_ref[1]
    core, chip = lax.rem(replica, 2), lax.div(replica, 2)
    low = lax.rem(team, LOW)
    offsets, _ = stored_offsets(place_ref, teams)
    times = right_ref.shape[1] // 2

    def mix(i, carry):
        total = None
        for k, offset in enumerate(offsets):
            c = lax.rem(i + offset, teams)
            right, dims = (omega_ref[i, k], NT) if k < 3 else (omega_ref[c, 5 - k], NN)
            term = lax.dot_general(block(data_ref, low, c), right, dims, preferred_element_type=F32)
            total = term if total is None else total + term
        mixed = total.astype(BF16)
        data = block(data_ref, low, i)
        right_ref[i, :times] = data
        right_ref[i, times:] = mixed
        for n, array in enumerate([mixed, data]):
            flip_ref[n] = array.T
            for m in range(chips):
                row = (2 * (chip ^ m) + core) * tile_rows
                left_ref[i, m * tile_rows : (m + 1) * tile_rows, n * times : (n + 1) * times] = flip_ref[
                    n, pl.ds(pl.multiple_of(row, tile_rows), tile_rows)
                ]
        return carry

    lax.fori_loop(0, teams, mix, 0, unroll=teams <= 8)


def product_kernel(teams, chips, wanted, place_ref, _, *rest):
    rights, lefts, outs = rest[0:4:2], rest[1:4:2], rest[4:]
    team = place_ref[0]
    high, low = lax.div(team, LOW), lax.rem(team, LOW)
    offsets, _ = stored_offsets(place_ref, teams)
    tile_rows = lefts[0].shape[1] // chips
    for mz, mx in sorted({key[:2] for key in wanted}):
        i = (high ^ mz) * LOW + (low ^ mx)
        for k, offset in enumerate(offsets):
            c = lax.rem(i + offset, teams)
            left = jnp.concatenate([ref[i] for ref in lefts], axis=1)
            right = jnp.concatenate([ref[c] for ref in rights], axis=0)
            product = lax.dot_general(left, right, NN, preferred_element_type=F32)
            for m in range(chips):
                if (mz, mx, m) in wanted:
                    out, place = wanted[mz, mx, m]
                    outs[out][place + (k,)] = product[m * tile_rows : (m + 1) * tile_rows].astype(outs[out].dtype)


def add_kernel(groups, *refs):
    outs = refs[len(refs) - len(groups) :]
    for out, terms in zip(outs, groups):
        total = None
        for source, index in terms:
            term = (refs[source][...] if index is None else refs[source][index]).astype(F32)
            total = term if total is None else total + term
        out[...] = total.astype(out.dtype)


def update_kernel(teams, scale, place_ref, omega_ref, *rest):
    parts, out_ref = rest[:-1], rest[-1]
    _, slots = stored_offsets(place_ref, teams)
    rows, width = out_ref.shape[2:]
    first = place_ref[1] * rows
    row_ids = first + lax.broadcasted_iota(jnp.int32, (rows, width), 0)
    diagonal = row_ids == lax.broadcasted_iota(jnp.int32, (rows, width), 1)
    for k in range(5):
        total = parts[0][k].astype(F32)
        for part in parts[1:]:
            total = total + part[k].astype(F32)
        current = omega_ref[0, slots[k]]
        gradient = total * scale
        if k == 0:
            gradient = gradient - jnp.where(diagonal, 1.0 / current, 0.0)
        value = current - STEP_SIZE * gradient
        bound = STEP_SIZE * PENALTY
        shrunk = jnp.where(value > bound, value - bound, jnp.where(value < -bound, value + bound, 0.0))
        if k == 0:
            shrunk = jnp.where(diagonal, value, shrunk)
        out_ref[0, slots[k]] = shrunk


def per_device(teams, replicas, signals, omega, pattern):
    chips = replicas // 2
    slots, tile_rows, width = omega.shape[1:]
    times = signals.shape[0] // teams
    place = jnp.concatenate([jnp.stack([lax.axis_index(BLK), lax.axis_index(REP)]).astype(jnp.int32), pattern[0]])

    def swap(array, blk_mask, rep_mask):
        route = [
            (b * replicas + r, (b ^ blk_mask) * replicas + (r ^ rep_mask))
            for b in range(teams)
            for r in range(replicas)
        ]
        return lax.ppermute(array, AXES, route)

    planes = LOW * chips
    count = teams // LOW
    planes = LOW * chips
    count = teams // LOW
    small = pltpu.CompilerParams(vmem_limit_bytes=(4 if teams <= 8 else 16) * 2**20)
    tiny = pltpu.CompilerParams(vmem_limit_bytes=2 * 2**20)

    def across_plane(arrays):
        return [
            swap(arrays[mx * chips + my], mx, 2 * my) if mx + my else arrays[0]
            for mx in range(LOW)
            for my in range(chips)
        ]

    def along_line(arrays):
        return [swap(array, m * LOW, 0) if m else array for m, array in enumerate(arrays)]

    low = lax.axis_index("low")
    across = swap(lax.dynamic_slice_in_dim(signals, (low ^ 1) * count * times, count * times, 0), 1, 0)
    upper = pl.pallas_call(
        functools.partial(prepare_kernel, teams),
        out_shape=jax.ShapeDtypeStruct((3, tile_rows, width), BF16),
        in_specs=[SMEM, VMEM],
        out_specs=VMEM,
        compiler_params=tiny,
        name="prepare",
    )(place, omega)
    line = jnp.stack(along_line([upper] * count))
    line, across, signals = lax.optimization_barrier((line, across, signals))
    kept = lax.dynamic_slice_in_dim(signals, low * count * times, count * times, 0)
    weights = across_plane([line] * planes)
    dealt = pl.pallas_call(
        deal_kernel,
        out_shape=jax.ShapeDtypeStruct((count, LOW, times, width), BF16),
        in_specs=[VMEM, VMEM],
        out_specs=HBM,
        scratch_shapes=[pltpu.SemaphoreType.DMA((2,))],
        compiler_params=tiny,
        name="deal",
    )(kept, across)
    own = lax.all_to_all(dealt, "line", 0, 0)
    weights += [swap(array, 0, 1) for array in weights]
    tiles = pl.pallas_call(
        functools.partial(gather_kernel, teams, chips, tile_rows),
        out_shape=jax.ShapeDtypeStruct((teams, 3, width, width), BF16),
        in_specs=[SMEM] + [ANY] * (2 * planes),
        out_specs=VMEM,
        scratch_shapes=[pltpu.SemaphoreType.DMA((2 * planes * count,))],
        compiler_params=tiny,
        name="gather",
    )(place, *weights)

    own, tiles = lax.optimization_barrier((own, tiles))

    def mix(data):
        return pl.pallas_call(
            functools.partial(mix_kernel, teams, replicas, tile_rows),
            out_shape=[
                jax.ShapeDtypeStruct((teams, 2 * times, width), BF16),
                jax.ShapeDtypeStruct((teams, chips * tile_rows, 2 * times), BF16),
            ],
            in_specs=[SMEM, VMEM, VMEM],
            out_specs=[VMEM, VMEM],
            scratch_shapes=[pltpu.VMEM((2, width, times), BF16)],
            compiler_params=small,
            name="mix",
        )(place, data, tiles)

    other = swap(own, 0, 1)
    cores = [*mix(own), *mix(other)]

    tile = (slots, tile_rows, width)

    def shape(lead, dtype):
        return jax.ShapeDtypeStruct(tuple(lead) + tile, dtype)

    def products(wanted, shapes):
        return pl.pallas_call(
            functools.partial(product_kernel, teams, chips, wanted),
            out_shape=shapes,
            in_specs=[SMEM, ANY] + [VMEM] * 4,
            out_specs=[VMEM] * len(shapes),
            compiler_params=small,
            name="products",
        )(place, own, *cores)

    def add(groups, shapes, *arrays):
        return pl.pallas_call(
            functools.partial(add_kernel, groups),
            out_shape=shapes,
            in_specs=[VMEM] * len(arrays),
            out_specs=[VMEM] * len(shapes),
            compiler_params=small,
            name="add",
        )(*arrays)

    chip_range = range(chips)

    def first_parts(group, x_first):
        size = len(group)
        if x_first:
            far, near = [
                products(
                    {(mz, mx, my): (0, (my, n)) for n, mz in enumerate(group) for my in chip_range},
                    [shape((chips, size), BF16 if mx else F32)],
                )[0]
                for mx in (1, 0)
            ]
            return [far], near
        kept, *sent = products(
            {(mz, mx, my): (my, (mx, n)) for n, mz in enumerate(group) for mx in range(LOW) for my in chip_range},
            [shape((LOW, size), BF16 if my else F32) for my in chip_range],
        )
        return sent, kept

    def first_hop(x_first, sent):
        return [swap(sent[0], 1, 0)] if x_first else [swap(array, 0, 2 * my) for my, array in enumerate(sent, 1)]

    def second_hop(group, x_first, received, kept):
        size = len(group)
        if x_first:
            groups = [[(0, my), (1, my)] for my in chip_range]
            parts = add(groups, [shape((size,), BF16 if my else F32) for my in chip_range], kept, *received)
            return [swap(array, 0, 2 * my) if my else array for my, array in enumerate(parts)]
        groups = [[(m, mx) for m in chip_range] for mx in range(LOW)]
        parts = add(groups, [shape((size,), BF16 if mx else F32) for mx in range(LOW)], kept, *received)
        return [swap(array, mx, 0) if mx else array for mx, array in enumerate(parts)]

    def sums_of(group, parts):
        groups = [[(m, n) for m in range(len(parts))] for n in range(len(group))]
        return add(groups, [shape((), BF16 if mz else F32) for mz in group], *parts)

    quarter = count // 4
    bounds = [range(n * quarter, (n + 1) * quarter) for n in range(4)]
    x_first = [True, False, True, False]
    firsts = [first_parts(*each) for each in zip(bounds, x_first)]
    received = [first_hop(first, sent) for first, (sent, _) in zip(x_first, firsts)]
    sums = [None] * 4
    for n in (2, 3, 0, 1):
        sums[n] = sums_of(bounds[n], second_hop(bounds[n], x_first[n], received[n], firsts[n][1]))
        if n == 3:
            received[:2], firsts[:2], sums[2:] = lax.optimization_barrier((received[:2], firsts[:2], sums[2:]))
    sums = along_line([total for group in sums for total in group])

    scale = 1.0 / (2.0 * teams * times * replicas)
    return pl.pallas_call(
        functools.partial(update_kernel, teams, scale),
        out_shape=jax.ShapeDtypeStruct(omega.shape, F32),
        in_specs=[SMEM, VMEM] + [VMEM] * count,
        out_specs=VMEM,
        compiler_params=small,
        name="update",
    )(place, omega, *sums)


def solution(mesh):
    teams, replicas = mesh.shape["blk"], mesh.shape["rep"]
    fine = Mesh(mesh.devices.reshape(teams // LOW, LOW, replicas // 2, 2), AXES)
    return jax.shard_map(
        functools.partial(per_device, teams, replicas),
        mesh=fine,
        in_specs=(P(REP, BLK), P(BLK, None, REP, None), P(BLK, None)),
        out_specs=P(BLK, None, REP, None),
        check_vma=False,
    )
```

```python
import functools

import jax
import jax.numpy as jnp
from jax import lax
from jax.experimental import pallas as pl
from jax.experimental.pallas import tpu as pltpu
from jax.sharding import Mesh, PartitionSpec as P

STEP_SIZE = 0.5
PENALTY = 0.1
LOW = 2
AXES = ("line", "low", "chip", "core")
BLK, REP = AXES[:2], AXES[2:]
COST = 12
F32 = jnp.float32
BF16 = jnp.bfloat16

VMEM = pl.BlockSpec(memory_space=pltpu.VMEM)
ANY = pl.BlockSpec(memory_space=pl.ANY)
HBM = pl.BlockSpec(memory_space=pltpu.HBM)
SMEM = pl.BlockSpec(memory_space=pltpu.SMEM)


def stored_offsets(place_ref, teams):
    drawn = [lax.rem(place_ref[2 + k] - place_ref[0] + teams, teams) for k in range(1, 5)]
    a = functools.reduce(jnp.minimum, drawn)
    b = functools.reduce(jnp.minimum, [jnp.where(d == a, teams, d) for d in drawn])
    offsets = [jnp.int32(0), a, b, teams - b, teams - a]
    slots = [jnp.int32(0)]
    for offset in offsets[1:]:
        slots.append(sum(jnp.where(d == offset, k + 1, 0) for k, d in enumerate(drawn)))
    return offsets, slots


def prepare_kernel(teams, place_ref, omega_ref, out_ref):
    _, slots = stored_offsets(place_ref, teams)
    for k in range(3):
        out_ref[k] = omega_ref[0, slots[k]].astype(BF16)


def deal_kernel(kept_ref, across_ref, out_ref, sems):
    shape = (out_ref.shape[0],) + out_ref.shape[2:]
    copies = [
        pltpu.make_async_copy(source.reshape(shape), out_ref.at[:, n], sems.at[n])
        for n, source in enumerate([kept_ref, across_ref])
    ]
    for copy in copies:
        copy.start()
    for copy in copies:
        copy.wait()


NN = (((1,), (0,)), ((), ()))
NT = (((1,), (1,)), ((), ()))


def gather_kernel(teams, chips, tile_rows, place_ref, *rest):
    weight_refs, omega_ref, sems = rest[:-2], rest[-2], rest[-1]
    planes = LOW * chips
    depth = teams // LOW
    team, replica = place_ref[0], place_ref[1]
    core, chip = lax.rem(replica, 2), lax.div(replica, 2)
    high, low = lax.div(team, LOW), lax.rem(team, LOW)
    copies = []
    for half in range(2):
        for mx in range(LOW):
            for my in range(chips):
                plane = mx * chips + my
                row = (2 * (chip ^ my) + (core ^ half)) * tile_rows
                for mz in range(depth):
                    i = (high ^ mz) * LOW + (low ^ mx)
                    target = omega_ref.at[i, :, pl.ds(pl.multiple_of(row, tile_rows), tile_rows)]
                    copies.append(
                        pltpu.make_async_copy(
                            weight_refs[half * planes + plane].at[mz],
                            target,
                            sems.at[(half * planes + plane) * depth + mz],
                        )
                    )
    for copy in copies:
        copy.start()
    for copy in copies:
        copy.wait()


def block(data_ref, low, c):
    return data_ref[lax.div(c, LOW), lax.rem(c, LOW) ^ low]


def mix_kernel(teams, replicas, tile_rows, place_ref, data_ref, omega_ref, right_ref, left_ref, flip_ref):
    chips = replicas // 2
    team, replica = place_ref[0], place_ref[1]
    core, chip = lax.rem(replica, 2), lax.div(replica, 2)
    low = lax.rem(team, LOW)
    offsets, _ = stored_offsets(place_ref, teams)
    times = right_ref.shape[1] // 2

    def mix(i, carry):
        total = None
        for k, offset in enumerate(offsets):
            c = lax.rem(i + offset, teams)
            right, dims = (omega_ref[i, k], NT) if k < 3 else (omega_ref[c, 5 - k], NN)
            term = lax.dot_general(block(data_ref, low, c), right, dims, preferred_element_type=F32)
            total = term if total is None else total + term
        mixed = total.astype(BF16)
        data = block(data_ref, low, i)
        right_ref[i, :times] = data
        right_ref[i, times:] = mixed
        for n, array in enumerate([mixed, data]):
            flip_ref[n] = array.T
            for m in range(chips):
                row = (2 * (chip ^ m) + core) * tile_rows
                left_ref[i, m * tile_rows : (m + 1) * tile_rows, n * times : (n + 1) * times] = flip_ref[
                    n, pl.ds(pl.multiple_of(row, tile_rows), tile_rows)
                ]
        return carry

    lax.fori_loop(0, teams, mix, 0, unroll=teams <= 8)


def product_kernel(teams, chips, wanted, place_ref, _, *rest):
    rights, lefts, outs = rest[0:4:2], rest[1:4:2], rest[4:]
    team = place_ref[0]
    high, low = lax.div(team, LOW), lax.rem(team, LOW)
    offsets, _ = stored_offsets(place_ref, teams)
    tile_rows = lefts[0].shape[1] // chips
    for mz, mx in sorted({key[:2] for key in wanted}):
        i = (high ^ mz) * LOW + (low ^ mx)
        for k, offset in enumerate(offsets):
            c = lax.rem(i + offset, teams)
            left = jnp.concatenate([ref[i] for ref in lefts], axis=1)
            right = jnp.concatenate([ref[c] for ref in rights], axis=0)
            product = lax.dot_general(left, right, NN, preferred_element_type=F32)
            for m in range(chips):
                if (mz, mx, m) in wanted:
                    out, place = wanted[mz, mx, m]
                    outs[out][place + (k,)] = product[m * tile_rows : (m + 1) * tile_rows].astype(outs[out].dtype)


def add_kernel(groups, *refs):
    outs = refs[len(refs) - len(groups) :]
    for out, terms in zip(outs, groups):
        total = None
        for source, index in terms:
            term = (refs[source][...] if index is None else refs[source][index]).astype(F32)
            total = term if total is None else total + term
        out[...] = total.astype(out.dtype)


def update_kernel(teams, scale, place_ref, omega_ref, *rest):
    parts, out_ref = rest[:-1], rest[-1]
    _, slots = stored_offsets(place_ref, teams)
    rows, width = out_ref.shape[2:]
    first = place_ref[1] * rows
    row_ids = first + lax.broadcasted_iota(jnp.int32, (rows, width), 0)
    diagonal = row_ids == lax.broadcasted_iota(jnp.int32, (rows, width), 1)
    for k in range(5):
        total = parts[0][k].astype(F32)
        for part in parts[1:]:
            total = total + part[k].astype(F32)
        current = omega_ref[0, slots[k]]
        gradient = total * scale
        if k == 0:
            gradient = gradient - jnp.where(diagonal, 1.0 / current, 0.0)
        value = current - STEP_SIZE * gradient
        bound = STEP_SIZE * PENALTY
        shrunk = jnp.where(value > bound, value - bound, jnp.where(value < -bound, value + bound, 0.0))
        if k == 0:
            shrunk = jnp.where(diagonal, value, shrunk)
        out_ref[0, slots[k]] = shrunk


def per_device(teams, replicas, signals, omega, pattern):
    chips = replicas // 2
    slots, tile_rows, width = omega.shape[1:]
    times = signals.shape[0] // teams
    place = jnp.concatenate([jnp.stack([lax.axis_index(BLK), lax.axis_index(REP)]).astype(jnp.int32), pattern[0]])

    def swap(array, blk_mask, rep_mask):
        route = [
            (b * replicas + r, (b ^ blk_mask) * replicas + (r ^ rep_mask))
            for b in range(teams)
            for r in range(replicas)
        ]
        return lax.ppermute(array, AXES, route)

    planes = LOW * chips
    count = teams // LOW
    planes = LOW * chips
    count = teams // LOW
    small = pltpu.CompilerParams(vmem_limit_bytes=(4 if teams <= 8 else 16) * 2**20)
    tiny = pltpu.CompilerParams(vmem_limit_bytes=2 * 2**20)

    def across_plane(arrays):
        return [
            swap(arrays[mx * chips + my], mx, 2 * my) if mx + my else arrays[0]
            for mx in range(LOW)
            for my in range(chips)
        ]

    def along_line(arrays):
        return [swap(array, m * LOW, 0) if m else array for m, array in enumerate(arrays)]

    low = lax.axis_index("low")
    across = swap(lax.dynamic_slice_in_dim(signals, (low ^ 1) * count * times, count * times, 0), 1, 0)
    upper = pl.pallas_call(
        functools.partial(prepare_kernel, teams),
        out_shape=jax.ShapeDtypeStruct((3, tile_rows, width), BF16),
        in_specs=[SMEM, VMEM],
        out_specs=VMEM,
        compiler_params=tiny,
        name="prepare",
    )(place, omega)
    line = jnp.stack(along_line([upper] * count))
    line, across, signals = lax.optimization_barrier((line, across, signals))
    kept = lax.dynamic_slice_in_dim(signals, low * count * times, count * times, 0)
    weights = across_plane([line] * planes)
    dealt = pl.pallas_call(
        deal_kernel,
        out_shape=jax.ShapeDtypeStruct((count, LOW, times, width), BF16),
        in_specs=[VMEM, VMEM],
        out_specs=HBM,
        scratch_shapes=[pltpu.SemaphoreType.DMA((2,))],
        compiler_params=tiny,
        name="deal",
    )(kept, across)
    own = lax.all_to_all(dealt, "line", 0, 0)
    weights += [swap(array, 0, 1) for array in weights]
    tiles = pl.pallas_call(
        functools.partial(gather_kernel, teams, chips, tile_rows),
        out_shape=jax.ShapeDtypeStruct((teams, 3, width, width), BF16),
        in_specs=[SMEM] + [ANY] * (2 * planes),
        out_specs=VMEM,
        scratch_shapes=[pltpu.SemaphoreType.DMA((2 * planes * count,))],
        compiler_params=tiny,
        name="gather",
    )(place, *weights)

    own, tiles = lax.optimization_barrier((own, tiles))

    def mix(data):
        return pl.pallas_call(
            functools.partial(mix_kernel, teams, replicas, tile_rows),
            out_shape=[
                jax.ShapeDtypeStruct((teams, 2 * times, width), BF16),
                jax.ShapeDtypeStruct((teams, chips * tile_rows, 2 * times), BF16),
            ],
            in_specs=[SMEM, VMEM, VMEM],
            out_specs=[VMEM, VMEM],
            scratch_shapes=[pltpu.VMEM((2, width, times), BF16)],
            compiler_params=small,
            name="mix",
        )(place, data, tiles)

    other = swap(own, 0, 1)
    cores = [*mix(own), *mix(other)]

    tile = (slots, tile_rows, width)

    def shape(lead, dtype):
        return jax.ShapeDtypeStruct(tuple(lead) + tile, dtype)

    def products(wanted, shapes):
        return pl.pallas_call(
            functools.partial(product_kernel, teams, chips, wanted),
            out_shape=shapes,
            in_specs=[SMEM, ANY] + [VMEM] * 4,
            out_specs=[VMEM] * len(shapes),
            compiler_params=small,
            name="products",
        )(place, own, *cores)

    def add(groups, shapes, *arrays, cost=None):
        return pl.pallas_call(
            functools.partial(add_kernel, groups),
            out_shape=shapes,
            in_specs=[VMEM] * len(arrays),
            out_specs=[VMEM] * len(shapes),
            compiler_params=small,
            cost_estimate=cost,
            name="add",
        )(*arrays)

    chip_range = range(chips)

    def first_parts(group, x_first):
        size = len(group)
        if x_first:
            far, near = [
                products(
                    {(mz, mx, my): (0, (my, n)) for n, mz in enumerate(group) for my in chip_range},
                    [shape((chips, size), BF16 if mx else F32)],
                )[0]
                for mx in (1, 0)
            ]
            return [far], near
        kept, *sent = products(
            {(mz, mx, my): (my, (mx, n)) for n, mz in enumerate(group) for mx in range(LOW) for my in chip_range},
            [shape((LOW, size), BF16 if my else F32) for my in chip_range],
        )
        return sent, kept

    def first_hop(x_first, sent):
        return [swap(sent[0], 1, 0)] if x_first else [swap(array, 0, 2 * my) for my, array in enumerate(sent, 1)]

    def plane_add(group, x_first, received, kept):
        size = len(group)
        if x_first:
            groups = [[(0, my), (1, my)] for my in chip_range]
            return add(groups, [shape((size,), BF16 if my else F32) for my in chip_range], kept, *received)
        groups = [[(m, mx) for m in chip_range] for mx in range(LOW)]
        return add(groups, [shape((size,), BF16 if mx else F32) for mx in range(LOW)], kept, *received)

    def second_hop(x_first, parts):
        return [swap(array, 0 if x_first else n, 2 * n if x_first else 0) if n else array for n, array in enumerate(parts)]

    def sums_of(group, parts):
        groups = [[(m, n) for m in range(len(parts))] for n in range(len(group))]
        return add(groups, [shape((), BF16 if mz else F32) for mz in group], *parts)

    quarter = count // 4
    bounds = [range(n * quarter, (n + 1) * quarter) for n in range(4)]
    x_first = [True, False, True, False]
    firsts = [first_parts(*each) for each in zip(bounds, x_first)]
    far = [plane_add(bounds[n], x_first[n], first_hop(x_first[n], firsts[n][0]), firsts[n][1]) for n in (2, 3)]
    far, near = lax.optimization_barrier((far, firsts[:2]))
    far_sums = [sums_of(bounds[n], second_hop(x_first[n], far[n - 2])) for n in (2, 3)]
    received = [first_hop(x_first[n], near[n][0]) for n in range(2)]
    near_sums = [
        sums_of(bounds[n], second_hop(x_first[n], plane_add(bounds[n], x_first[n], received[n], near[n][1])))
        for n in range(2)
    ]
    sums = along_line([total for group in near_sums + far_sums for total in group])
    half = 2 * quarter
    (far_total,) = add(
        [[(n, None) for n in range(half)]],
        [shape((), F32)],
        *sums[half:],
        cost=pl.CostEstimate(flops=COST * 10**9, bytes_accessed=COST * 3 * 10**6, transcendentals=0),
    )
    sums = sums[:half] + [far_total]

    scale = 1.0 / (2.0 * teams * times * replicas)
    return pl.pallas_call(
        functools.partial(update_kernel, teams, scale),
        out_shape=jax.ShapeDtypeStruct(omega.shape, F32),
        in_specs=[SMEM, VMEM] + [VMEM] * len(sums),
        out_specs=VMEM,
        compiler_params=small,
        name="update",
    )(place, omega, *sums)


def solution(mesh):
    teams, replicas = mesh.shape["blk"], mesh.shape["rep"]
    fine = Mesh(mesh.devices.reshape(teams // LOW, LOW, replicas // 2, 2), AXES)
    return jax.shard_map(
        functools.partial(per_device, teams, replicas),
        mesh=fine,
        in_specs=(P(REP, BLK), P(BLK, None, REP, None), P(BLK, None)),
        out_specs=P(BLK, None, REP, None),
        check_vma=False,
    )
```

```python
import functools

import jax
import jax.numpy as jnp
from jax import lax
from jax.experimental import pallas as pl
from jax.experimental.pallas import tpu as pltpu
from jax.sharding import Mesh, PartitionSpec as P

STEP_SIZE = 0.5
PENALTY = 0.1
LOW = 2
AXES = ("line", "low", "chip", "core")
BLK, REP = AXES[:2], AXES[2:]
COST = 12
F32 = jnp.float32
BF16 = jnp.bfloat16

VMEM = pl.BlockSpec(memory_space=pltpu.VMEM)
ANY = pl.BlockSpec(memory_space=pl.ANY)
HBM = pl.BlockSpec(memory_space=pltpu.HBM)
SMEM = pl.BlockSpec(memory_space=pltpu.SMEM)


def stored_offsets(place_ref, teams):
    drawn = [lax.rem(place_ref[2 + k] - place_ref[0] + teams, teams) for k in range(1, 5)]
    a = functools.reduce(jnp.minimum, drawn)
    b = functools.reduce(jnp.minimum, [jnp.where(d == a, teams, d) for d in drawn])
    offsets = [jnp.int32(0), a, b, teams - b, teams - a]
    slots = [jnp.int32(0)]
    for offset in offsets[1:]:
        slots.append(sum(jnp.where(d == offset, k + 1, 0) for k, d in enumerate(drawn)))
    return offsets, slots


def prepare_kernel(teams, place_ref, omega_ref, out_ref):
    _, slots = stored_offsets(place_ref, teams)
    for k in range(3):
        out_ref[k] = omega_ref[0, slots[k]].astype(BF16)


def deal_kernel(kept_ref, across_ref, out_ref, sems):
    shape = (out_ref.shape[0],) + out_ref.shape[2:]
    copies = [
        pltpu.make_async_copy(source.reshape(shape), out_ref.at[:, n], sems.at[n])
        for n, source in enumerate([kept_ref, across_ref])
    ]
    for copy in copies:
        copy.start()
    for copy in copies:
        copy.wait()


NN = (((1,), (0,)), ((), ()))
NT = (((1,), (1,)), ((), ()))


def gather_kernel(teams, chips, tile_rows, place_ref, *rest):
    weight_refs, omega_ref, sems = rest[:-2], rest[-2], rest[-1]
    planes = LOW * chips
    depth = teams // LOW
    team, replica = place_ref[0], place_ref[1]
    core, chip = lax.rem(replica, 2), lax.div(replica, 2)
    high, low = lax.div(team, LOW), lax.rem(team, LOW)
    copies = []
    for half in range(2):
        for mx in range(LOW):
            for my in range(chips):
                plane = mx * chips + my
                row = (2 * (chip ^ my) + (core ^ half)) * tile_rows
                for mz in range(depth):
                    i = (high ^ mz) * LOW + (low ^ mx)
                    target = omega_ref.at[i, :, pl.ds(pl.multiple_of(row, tile_rows), tile_rows)]
                    copies.append(
                        pltpu.make_async_copy(
                            weight_refs[half * planes + plane].at[mz],
                            target,
                            sems.at[(half * planes + plane) * depth + mz],
                        )
                    )
    for copy in copies:
        copy.start()
    for copy in copies:
        copy.wait()


def block(data_ref, low, c):
    return data_ref[lax.div(c, LOW), lax.rem(c, LOW) ^ low]


def mix_kernel(teams, replicas, tile_rows, place_ref, data_ref, omega_ref, kept_ref, mixed_ref, left_ref, flip_ref):
    chips = replicas // 2
    team, replica = place_ref[0], place_ref[1]
    core, chip = lax.rem(replica, 2), lax.div(replica, 2)
    low = lax.rem(team, LOW)
    offsets, _ = stored_offsets(place_ref, teams)
    times = mixed_ref.shape[1]

    def mix(i, carry):
        total = None
        for k, offset in enumerate(offsets):
            c = lax.rem(i + offset, teams)
            right, dims = (omega_ref[i, k], NT) if k < 3 else (omega_ref[c, 5 - k], NN)
            term = lax.dot_general(block(data_ref, low, c), right, dims, preferred_element_type=F32)
            total = term if total is None else total + term
        mixed = total.astype(BF16)
        data = block(data_ref, low, i)
        kept_ref[i] = data
        mixed_ref[i] = mixed
        for n, array in enumerate([mixed, data]):
            flip_ref[n] = array.T
            for m in range(chips):
                row = (2 * (chip ^ m) + core) * tile_rows
                left_ref[i, m * tile_rows : (m + 1) * tile_rows, n * times : (n + 1) * times] = flip_ref[
                    n, pl.ds(pl.multiple_of(row, tile_rows), tile_rows)
                ]
        return carry

    lax.fori_loop(0, teams, mix, 0, unroll=teams <= 8)


def product_kernel(teams, chips, wanted, place_ref, *rest):
    rights, lefts, outs = rest[0:2] + rest[3:5], rest[2:6:3], rest[6:]
    team = place_ref[0]
    high, low = lax.div(team, LOW), lax.rem(team, LOW)
    offsets, _ = stored_offsets(place_ref, teams)
    tile_rows = lefts[0].shape[1] // chips
    for mz, mx in sorted({key[:2] for key in wanted}):
        i = (high ^ mz) * LOW + (low ^ mx)
        for k, offset in enumerate(offsets):
            c = lax.rem(i + offset, teams)
            left = jnp.concatenate([ref[i] for ref in lefts], axis=1)
            right = jnp.concatenate([ref[c] for ref in rights], axis=0)
            product = lax.dot_general(left, right, NN, preferred_element_type=F32)
            for m in range(chips):
                if (mz, mx, m) in wanted:
                    out, place = wanted[mz, mx, m]
                    outs[out][place + (k,)] = product[m * tile_rows : (m + 1) * tile_rows].astype(outs[out].dtype)


def add_kernel(groups, *refs):
    outs = refs[len(refs) - len(groups) :]
    for out, terms in zip(outs, groups):
        total = None
        for source, index in terms:
            term = (refs[source][...] if index is None else refs[source][index]).astype(F32)
            total = term if total is None else total + term
        out[...] = total.astype(out.dtype)


def update_kernel(teams, scale, place_ref, omega_ref, *rest):
    parts, out_ref = rest[:-1], rest[-1]
    _, slots = stored_offsets(place_ref, teams)
    rows, width = out_ref.shape[2:]
    first = place_ref[1] * rows
    row_ids = first + lax.broadcasted_iota(jnp.int32, (rows, width), 0)
    diagonal = row_ids == lax.broadcasted_iota(jnp.int32, (rows, width), 1)
    for k in range(5):
        total = parts[0][k].astype(F32)
        for part in parts[1:]:
            total = total + part[k].astype(F32)
        current = omega_ref[0, slots[k]]
        gradient = total * scale
        if k == 0:
            gradient = gradient - jnp.where(diagonal, 1.0 / current, 0.0)
        value = current - STEP_SIZE * gradient
        bound = STEP_SIZE * PENALTY
        shrunk = jnp.where(value > bound, value - bound, jnp.where(value < -bound, value + bound, 0.0))
        if k == 0:
            shrunk = jnp.where(diagonal, value, shrunk)
        out_ref[0, slots[k]] = shrunk


def per_device(teams, replicas, signals, omega, pattern):
    chips = replicas // 2
    slots, tile_rows, width = omega.shape[1:]
    times = signals.shape[0] // teams
    place = jnp.concatenate([jnp.stack([lax.axis_index(BLK), lax.axis_index(REP)]).astype(jnp.int32), pattern[0]])

    def swap(array, blk_mask, rep_mask):
        route = [
            (b * replicas + r, (b ^ blk_mask) * replicas + (r ^ rep_mask))
            for b in range(teams)
            for r in range(replicas)
        ]
        return lax.ppermute(array, AXES, route)

    planes = LOW * chips
    count = teams // LOW
    planes = LOW * chips
    count = teams // LOW
    small = pltpu.CompilerParams(vmem_limit_bytes=(4 if teams <= 8 else 16) * 2**20)
    tiny = pltpu.CompilerParams(vmem_limit_bytes=2 * 2**20)

    def across_plane(arrays):
        return [
            swap(arrays[mx * chips + my], mx, 2 * my) if mx + my else arrays[0]
            for mx in range(LOW)
            for my in range(chips)
        ]

    def along_line(arrays):
        return [swap(array, m * LOW, 0) if m else array for m, array in enumerate(arrays)]

    low = lax.axis_index("low")
    across = swap(lax.dynamic_slice_in_dim(signals, (low ^ 1) * count * times, count * times, 0), 1, 0)
    upper = pl.pallas_call(
        functools.partial(prepare_kernel, teams),
        out_shape=jax.ShapeDtypeStruct((3, tile_rows, width), BF16),
        in_specs=[SMEM, VMEM],
        out_specs=VMEM,
        compiler_params=tiny,
        name="prepare",
    )(place, omega)
    line = jnp.stack(along_line([upper] * count))
    line, across, signals = lax.optimization_barrier((line, across, signals))
    kept = lax.dynamic_slice_in_dim(signals, low * count * times, count * times, 0)
    weights = across_plane([line] * planes)
    dealt = pl.pallas_call(
        deal_kernel,
        out_shape=jax.ShapeDtypeStruct((count, LOW, times, width), BF16),
        in_specs=[VMEM, VMEM],
        out_specs=HBM,
        scratch_shapes=[pltpu.SemaphoreType.DMA((2,))],
        compiler_params=tiny,
        name="deal",
    )(kept, across)
    own = lax.all_to_all(dealt, "line", 0, 0)
    weights += [swap(array, 0, 1) for array in weights]
    tiles = pl.pallas_call(
        functools.partial(gather_kernel, teams, chips, tile_rows),
        out_shape=jax.ShapeDtypeStruct((teams, 3, width, width), BF16),
        in_specs=[SMEM] + [ANY] * (2 * planes),
        out_specs=VMEM,
        scratch_shapes=[pltpu.SemaphoreType.DMA((2 * planes * count,))],
        compiler_params=tiny,
        name="gather",
    )(place, *weights)

    own, tiles = lax.optimization_barrier((own, tiles))

    def mix(data):
        return pl.pallas_call(
            functools.partial(mix_kernel, teams, replicas, tile_rows),
            out_shape=[
                jax.ShapeDtypeStruct((teams, times, width), BF16),
                jax.ShapeDtypeStruct((teams, times, width), BF16),
                jax.ShapeDtypeStruct((teams, chips * tile_rows, 2 * times), BF16),
            ],
            in_specs=[SMEM, VMEM, VMEM],
            out_specs=[VMEM] * 3,
            scratch_shapes=[pltpu.VMEM((2, width, times), BF16)],
            compiler_params=tiny,
            name="mix",
        )(place, data, tiles)

    other = swap(own, 0, 1)
    cores = [*mix(own), *mix(other)]

    tile = (slots, tile_rows, width)

    def shape(lead, dtype):
        return jax.ShapeDtypeStruct(tuple(lead) + tile, dtype)

    def products(wanted, shapes):
        return pl.pallas_call(
            functools.partial(product_kernel, teams, chips, wanted),
            out_shape=shapes,
            in_specs=[SMEM] + [VMEM] * 6,
            out_specs=[VMEM] * len(shapes),
            compiler_params=small,
            name="products",
        )(place, *cores)

    def add(groups, shapes, *arrays, cost=None):
        return pl.pallas_call(
            functools.partial(add_kernel, groups),
            out_shape=shapes,
            in_specs=[VMEM] * len(arrays),
            out_specs=[VMEM] * len(shapes),
            compiler_params=small,
            cost_estimate=cost,
            name="add",
        )(*arrays)

    chip_range = range(chips)

    def first_parts(group, x_first):
        size = len(group)
        if x_first:
            far, near = [
                products(
                    {(mz, mx, my): (0, (my, n)) for n, mz in enumerate(group) for my in chip_range},
                    [shape((chips, size), BF16 if mx else F32)],
                )[0]
                for mx in (1, 0)
            ]
            return [far], near
        kept, *sent = products(
            {(mz, mx, my): (my, (mx, n)) for n, mz in enumerate(group) for mx in range(LOW) for my in chip_range},
            [shape((LOW, size), BF16 if my else F32) for my in chip_range],
        )
        return sent, kept

    def first_hop(x_first, sent):
        return [swap(sent[0], 1, 0)] if x_first else [swap(array, 0, 2 * my) for my, array in enumerate(sent, 1)]

    def plane_add(group, x_first, received, kept):
        size = len(group)
        if x_first:
            groups = [[(0, my), (1, my)] for my in chip_range]
            return add(groups, [shape((size,), BF16 if my else F32) for my in chip_range], kept, *received)
        groups = [[(m, mx) for m in chip_range] for mx in range(LOW)]
        return add(groups, [shape((size,), BF16 if mx else F32) for mx in range(LOW)], kept, *received)

    def second_hop(x_first, parts):
        return [swap(array, 0 if x_first else n, 2 * n if x_first else 0) if n else array for n, array in enumerate(parts)]

    def sums_of(group, parts):
        groups = [[(m, n) for m in range(len(parts))] for n in range(len(group))]
        return add(groups, [shape((), BF16 if mz else F32) for mz in group], *parts)

    quarter = count // 4
    bounds = [range(n * quarter, (n + 1) * quarter) for n in range(4)]
    x_first = [True, False, True, False]
    firsts = [first_parts(*each) for each in zip(bounds, x_first)]
    far = [plane_add(bounds[n], x_first[n], first_hop(x_first[n], firsts[n][0]), firsts[n][1]) for n in (2, 3)]
    far, near = lax.optimization_barrier((far, firsts[:2]))
    far_sums = [sums_of(bounds[n], second_hop(x_first[n], far[n - 2])) for n in (2, 3)]
    received = [first_hop(x_first[n], near[n][0]) for n in range(2)]
    near_sums = [
        sums_of(bounds[n], second_hop(x_first[n], plane_add(bounds[n], x_first[n], received[n], near[n][1])))
        for n in range(2)
    ]
    sums = along_line([total for group in near_sums + far_sums for total in group])
    half = 2 * quarter
    (far_total,) = add(
        [[(n, None) for n in range(half)]],
        [shape((), F32)],
        *sums[half:],
        cost=pl.CostEstimate(flops=COST * 10**9, bytes_accessed=COST * 3 * 10**6, transcendentals=0),
    )
    sums = sums[:half] + [far_total]

    scale = 1.0 / (2.0 * teams * times * replicas)
    return pl.pallas_call(
        functools.partial(update_kernel, teams, scale),
        out_shape=jax.ShapeDtypeStruct(omega.shape, F32),
        in_specs=[SMEM, VMEM] + [VMEM] * len(sums),
        out_specs=VMEM,
        compiler_params=small,
        name="update",
    )(place, omega, *sums)


def solution(mesh):
    teams, replicas = mesh.shape["blk"], mesh.shape["rep"]
    fine = Mesh(mesh.devices.reshape(teams // LOW, LOW, replicas // 2, 2), AXES)
    return jax.shard_map(
        functools.partial(per_device, teams, replicas),
        mesh=fine,
        in_specs=(P(REP, BLK), P(BLK, None, REP, None), P(BLK, None)),
        out_specs=P(BLK, None, REP, None),
        check_vma=False,
    )
```

```python
import functools

import jax
import jax.numpy as jnp
from jax import lax
from jax.experimental import pallas as pl
from jax.experimental.pallas import tpu as pltpu
from jax.sharding import Mesh, PartitionSpec as P

STEP_SIZE = 0.5
PENALTY = 0.1
LOW = 2
AXES = ("line", "low", "chip", "core")
BLK, REP = AXES[:2], AXES[2:]
COST = 12
F32 = jnp.float32
BF16 = jnp.bfloat16

VMEM = pl.BlockSpec(memory_space=pltpu.VMEM)
ANY = pl.BlockSpec(memory_space=pl.ANY)
HBM = pl.BlockSpec(memory_space=pltpu.HBM)
SMEM = pl.BlockSpec(memory_space=pltpu.SMEM)


def stored_offsets(place_ref, teams):
    drawn = [lax.rem(place_ref[2 + k] - place_ref[0] + teams, teams) for k in range(1, 5)]
    a = functools.reduce(jnp.minimum, drawn)
    b = functools.reduce(jnp.minimum, [jnp.where(d == a, teams, d) for d in drawn])
    offsets = [jnp.int32(0), a, b, teams - b, teams - a]
    slots = [jnp.int32(0)]
    for offset in offsets[1:]:
        slots.append(sum(jnp.where(d == offset, k + 1, 0) for k, d in enumerate(drawn)))
    return offsets, slots


def prepare_kernel(teams, place_ref, omega_ref, out_ref):
    _, slots = stored_offsets(place_ref, teams)
    for k in range(3):
        out_ref[k] = omega_ref[0, slots[k]].astype(BF16)


def deal_kernel(kept_ref, across_ref, out_ref, sems):
    shape = (out_ref.shape[0],) + out_ref.shape[2:]
    copies = [
        pltpu.make_async_copy(source.reshape(shape), out_ref.at[:, n], sems.at[n])
        for n, source in enumerate([kept_ref, across_ref])
    ]
    for copy in copies:
        copy.start()
    for copy in copies:
        copy.wait()


NN = (((1,), (0,)), ((), ()))
NT = (((1,), (1,)), ((), ()))


def gather_kernel(teams, chips, tile_rows, place_ref, *rest):
    weight_refs, omega_refs, sems = rest[:-4], rest[-4:-1], rest[-1]
    planes = LOW * chips
    depth = teams // LOW
    team, replica = place_ref[0], place_ref[1]
    core, chip = lax.rem(replica, 2), lax.div(replica, 2)
    high, low = lax.div(team, LOW), lax.rem(team, LOW)
    copies = []
    for half in range(2):
        for mx in range(LOW):
            for my in range(chips):
                plane = mx * chips + my
                row = (2 * (chip ^ my) + (core ^ half)) * tile_rows
                for mz in range(depth):
                    i = (high ^ mz) * LOW + (low ^ mx)
                    rows = pl.ds(pl.multiple_of(row, tile_rows), tile_rows)
                    for k, omega_ref in enumerate(omega_refs):
                        copies.append(
                            pltpu.make_async_copy(
                                weight_refs[half * planes + plane].at[mz, k],
                                omega_ref.at[i, rows],
                                sems.at[k, (half * planes + plane) * depth + mz],
                            )
                        )
    for copy in copies:
        copy.start()
    for copy in copies:
        copy.wait()


def block(data_ref, low, c):
    return data_ref[lax.div(c, LOW), lax.rem(c, LOW) ^ low]


def mix_kernel(teams, replicas, tile_rows, place_ref, data_ref, omega_0, omega_1, omega_2, kept_ref, mixed_ref, left_ref, flip_ref):
    chips = replicas // 2
    team, replica = place_ref[0], place_ref[1]
    core, chip = lax.rem(replica, 2), lax.div(replica, 2)
    low = lax.rem(team, LOW)
    offsets, _ = stored_offsets(place_ref, teams)
    times = mixed_ref.shape[1]
    omega_refs = omega_0, omega_1, omega_2

    def mix(i, carry):
        total = None
        for k, offset in enumerate(offsets):
            c = lax.rem(i + offset, teams)
            right, dims = (omega_refs[k][i], NT) if k < 3 else (omega_refs[5 - k][c], NN)
            term = lax.dot_general(block(data_ref, low, c), right, dims, preferred_element_type=F32)
            total = term if total is None else total + term
        mixed = total.astype(BF16)
        data = block(data_ref, low, i)
        kept_ref[i] = data
        mixed_ref[i] = mixed
        for n, array in enumerate([mixed, data]):
            flip_ref[n] = array.T
            for m in range(chips):
                row = (2 * (chip ^ m) + core) * tile_rows
                left_ref[i, m * tile_rows : (m + 1) * tile_rows, n * times : (n + 1) * times] = flip_ref[
                    n, pl.ds(pl.multiple_of(row, tile_rows), tile_rows)
                ]
        return carry

    lax.fori_loop(0, teams, mix, 0, unroll=teams <= 8)


def product_kernel(teams, chips, wanted, place_ref, *rest):
    rights, lefts, outs = rest[0:2] + rest[3:5], rest[2:6:3], rest[6:]
    team = place_ref[0]
    high, low = lax.div(team, LOW), lax.rem(team, LOW)
    offsets, _ = stored_offsets(place_ref, teams)
    tile_rows = lefts[0].shape[1] // chips
    for mz, mx in sorted({key[:2] for key in wanted}):
        i = (high ^ mz) * LOW + (low ^ mx)
        for k, offset in enumerate(offsets):
            c = lax.rem(i + offset, teams)
            left = jnp.concatenate([ref[i] for ref in lefts], axis=1)
            right = jnp.concatenate([ref[c] for ref in rights], axis=0)
            product = lax.dot_general(left, right, NN, preferred_element_type=F32)
            for m in range(chips):
                if (mz, mx, m) in wanted:
                    out, place = wanted[mz, mx, m]
                    outs[out][place + (k,)] = product[m * tile_rows : (m + 1) * tile_rows].astype(outs[out].dtype)


def add_kernel(groups, *refs):
    outs = refs[len(refs) - len(groups) :]
    for out, terms in zip(outs, groups):
        total = None
        for source, index in terms:
            term = (refs[source][...] if index is None else refs[source][index]).astype(F32)
            total = term if total is None else total + term
        out[...] = total.astype(out.dtype)


def update_kernel(teams, scale, place_ref, omega_ref, *rest):
    parts, out_ref = rest[:-1], rest[-1]
    _, slots = stored_offsets(place_ref, teams)
    rows, width = out_ref.shape[2:]
    first = place_ref[1] * rows
    row_ids = first + lax.broadcasted_iota(jnp.int32, (rows, width), 0)
    diagonal = row_ids == lax.broadcasted_iota(jnp.int32, (rows, width), 1)
    for k in range(5):
        total = parts[0][k].astype(F32)
        for part in parts[1:]:
            total = total + part[k].astype(F32)
        current = omega_ref[0, slots[k]]
        gradient = total * scale
        if k == 0:
            gradient = gradient - jnp.where(diagonal, 1.0 / current, 0.0)
        value = current - STEP_SIZE * gradient
        bound = STEP_SIZE * PENALTY
        shrunk = jnp.where(value > bound, value - bound, jnp.where(value < -bound, value + bound, 0.0))
        if k == 0:
            shrunk = jnp.where(diagonal, value, shrunk)
        out_ref[0, slots[k]] = shrunk


def per_device(teams, replicas, signals, omega, pattern):
    chips = replicas // 2
    slots, tile_rows, width = omega.shape[1:]
    times = signals.shape[0] // teams
    place = jnp.concatenate([jnp.stack([lax.axis_index(BLK), lax.axis_index(REP)]).astype(jnp.int32), pattern[0]])

    def swap(array, blk_mask, rep_mask):
        route = [
            (b * replicas + r, (b ^ blk_mask) * replicas + (r ^ rep_mask))
            for b in range(teams)
            for r in range(replicas)
        ]
        return lax.ppermute(array, AXES, route)

    planes = LOW * chips
    count = teams // LOW
    planes = LOW * chips
    count = teams // LOW
    small = pltpu.CompilerParams(vmem_limit_bytes=(6 if teams <= 8 else 16) * 2**20)
    tiny = pltpu.CompilerParams(vmem_limit_bytes=2 * 2**20)

    def across_plane(arrays):
        return [
            swap(arrays[mx * chips + my], mx, 2 * my) if mx + my else arrays[0]
            for mx in range(LOW)
            for my in range(chips)
        ]

    def along_line(arrays):
        return [swap(array, m * LOW, 0) if m else array for m, array in enumerate(arrays)]

    low = lax.axis_index("low")
    across = swap(lax.dynamic_slice_in_dim(signals, (low ^ 1) * count * times, count * times, 0), 1, 0)
    upper = pl.pallas_call(
        functools.partial(prepare_kernel, teams),
        out_shape=jax.ShapeDtypeStruct((3, tile_rows, width), BF16),
        in_specs=[SMEM, VMEM],
        out_specs=VMEM,
        compiler_params=tiny,
        name="prepare",
    )(place, omega)
    line = jnp.stack(along_line([upper] * count))
    line, across, signals = lax.optimization_barrier((line, across, signals))
    kept = lax.dynamic_slice_in_dim(signals, low * count * times, count * times, 0)
    weights = across_plane([line] * planes)
    dealt = pl.pallas_call(
        deal_kernel,
        out_shape=jax.ShapeDtypeStruct((count, LOW, times, width), BF16),
        in_specs=[VMEM, VMEM],
        out_specs=HBM,
        scratch_shapes=[pltpu.SemaphoreType.DMA((2,))],
        compiler_params=tiny,
        name="deal",
    )(kept, across)
    own = lax.all_to_all(dealt, "line", 0, 0)
    weights += [swap(array, 0, 1) for array in weights]
    tiles = pl.pallas_call(
        functools.partial(gather_kernel, teams, chips, tile_rows),
        out_shape=[jax.ShapeDtypeStruct((teams, width, width), BF16)] * 3,
        in_specs=[SMEM] + [ANY] * (2 * planes),
        out_specs=[VMEM] * 3,
        scratch_shapes=[pltpu.SemaphoreType.DMA((3, 2 * planes * count))],
        compiler_params=small,
        name="gather",
    )(place, *weights)

    own, tiles = lax.optimization_barrier((own, tiles))

    def mix(data):
        return pl.pallas_call(
            functools.partial(mix_kernel, teams, replicas, tile_rows),
            out_shape=[
                jax.ShapeDtypeStruct((teams, times, width), BF16),
                jax.ShapeDtypeStruct((teams, times, width), BF16),
                jax.ShapeDtypeStruct((teams, chips * tile_rows, 2 * times), BF16),
            ],
            in_specs=[SMEM] + [VMEM] * 4,
            out_specs=[VMEM] * 3,
            scratch_shapes=[pltpu.VMEM((2, width, times), BF16)],
            compiler_params=small,
            name="mix",
        )(place, data, *tiles)

    other = swap(own, 0, 1)
    cores = [*mix(own), *mix(other)]

    tile = (slots, tile_rows, width)

    def shape(lead, dtype):
        return jax.ShapeDtypeStruct(tuple(lead) + tile, dtype)

    def products(wanted, shapes):
        return pl.pallas_call(
            functools.partial(product_kernel, teams, chips, wanted),
            out_shape=shapes,
            in_specs=[SMEM] + [VMEM] * 6,
            out_specs=[VMEM] * len(shapes),
            compiler_params=small,
            name="products",
        )(place, *cores)

    def add(groups, shapes, *arrays, cost=None):
        return pl.pallas_call(
            functools.partial(add_kernel, groups),
            out_shape=shapes,
            in_specs=[VMEM] * len(arrays),
            out_specs=[VMEM] * len(shapes),
            compiler_params=small,
            cost_estimate=cost,
            name="add",
        )(*arrays)

    chip_range = range(chips)

    def first_parts(group, x_first):
        size = len(group)
        if x_first:
            far, near = [
                products(
                    {(mz, mx, my): (0, (my, n)) for n, mz in enumerate(group) for my in chip_range},
                    [shape((chips, size), BF16 if mx else F32)],
                )[0]
                for mx in (1, 0)
            ]
            return [far], near
        kept, *sent = products(
            {(mz, mx, my): (my, (mx, n)) for n, mz in enumerate(group) for mx in range(LOW) for my in chip_range},
            [shape((LOW, size), BF16 if my else F32) for my in chip_range],
        )
        return sent, kept

    def first_hop(x_first, sent):
        return [swap(sent[0], 1, 0)] if x_first else [swap(array, 0, 2 * my) for my, array in enumerate(sent, 1)]

    def plane_add(group, x_first, received, kept):
        size = len(group)
        if x_first:
            groups = [[(0, my), (1, my)] for my in chip_range]
            return add(groups, [shape((size,), BF16 if my else F32) for my in chip_range], kept, *received)
        groups = [[(m, mx) for m in chip_range] for mx in range(LOW)]
        return add(groups, [shape((size,), BF16 if mx else F32) for mx in range(LOW)], kept, *received)

    def second_hop(x_first, parts):
        return [swap(array, 0 if x_first else n, 2 * n if x_first else 0) if n else array for n, array in enumerate(parts)]

    def sums_of(group, parts):
        groups = [[(m, n) for m in range(len(parts))] for n in range(len(group))]
        return add(groups, [shape((), BF16 if mz else F32) for mz in group], *parts)

    quarter = count // 4
    bounds = [range(n * quarter, (n + 1) * quarter) for n in range(4)]
    x_first = [True, False, True, False]
    firsts = [first_parts(*each) for each in zip(bounds, x_first)]
    far = [plane_add(bounds[n], x_first[n], first_hop(x_first[n], firsts[n][0]), firsts[n][1]) for n in (2, 3)]
    far, near = lax.optimization_barrier((far, firsts[:2]))
    far_sums = [sums_of(bounds[n], second_hop(x_first[n], far[n - 2])) for n in (2, 3)]
    received = [first_hop(x_first[n], near[n][0]) for n in range(2)]
    near_sums = [
        sums_of(bounds[n], second_hop(x_first[n], plane_add(bounds[n], x_first[n], received[n], near[n][1])))
        for n in range(2)
    ]
    sums = along_line([total for group in near_sums + far_sums for total in group])
    half = 2 * quarter
    (far_total,) = add(
        [[(n, None) for n in range(half)]],
        [shape((), F32)],
        *sums[half:],
        cost=pl.CostEstimate(flops=COST * 10**9, bytes_accessed=COST * 3 * 10**6, transcendentals=0),
    )
    sums = sums[:half] + [far_total]

    scale = 1.0 / (2.0 * teams * times * replicas)
    return pl.pallas_call(
        functools.partial(update_kernel, teams, scale),
        out_shape=jax.ShapeDtypeStruct(omega.shape, F32),
        in_specs=[SMEM, VMEM] + [VMEM] * len(sums),
        out_specs=VMEM,
        compiler_params=small,
        name="update",
    )(place, omega, *sums)


def solution(mesh):
    teams, replicas = mesh.shape["blk"], mesh.shape["rep"]
    fine = Mesh(mesh.devices.reshape(teams // LOW, LOW, replicas // 2, 2), AXES)
    return jax.shard_map(
        functools.partial(per_device, teams, replicas),
        mesh=fine,
        in_specs=(P(REP, BLK), P(BLK, None, REP, None), P(BLK, None)),
        out_specs=P(BLK, None, REP, None),
        check_vma=False,
    )
```
